32 devices in a mesh: rep: 2 (over x), shard: 16 (over z, y, core).
Axes of the slice: x: 2, y: 2, z: 4, core: 2. Of those that a mesh axis runs over, the one named last changes fastest.
Arguments:
- tokens: bfloat16 [5632, 1024], P(('rep', 'shard')), may hold values from -6 to 6
- cotangent: bfloat16 [5632, 1024], P(('rep', 'shard')), may hold values from -6 to 6
- lengths: int32 [64], replicated, may hold values from 1 to 176, as said below
- owners: int32 [64], replicated, may hold values from 0 to 31, as said below
- first_gain: bfloat16 [1024], P('shard'), may hold values from 0.099609375 to 1.8984375
- first_bias: bfloat16 [1024], P('shard'), may hold values from -2 to 2
- joint_weight: bfloat16 [1024, 3072], P('shard'), may hold values from -0.1875 to 0.1875
- joint_bias: bfloat16 [3072], P('shard'), may hold values from -3 to 3
- output_weight: bfloat16 [1024, 1024], P('shard'), may hold values from -0.875 to 0.875
- output_bias: bfloat16 [1024], P('shard'), may hold values from -2 to 2
- second_gain: bfloat16 [1024], P('shard'), may hold values from 0.099609375 to 1.8984375
- second_bias: bfloat16 [1024], P('shard'), may hold values from -2 to 2
- up_weight: bfloat16 [1024, 4096], P('shard'), may hold values from -0.1875 to 0.1875
- up_bias: bfloat16 [4096], P('shard'), may hold values from -3 to 3
- down_weight: bfloat16 [4096, 1024], P('shard'), may hold values from -0.09375 to 0.09375
- down_bias: bfloat16 [1024], P('shard'), may hold values from -2 to 2
Outputs:
- result: bfloat16 [5632, 1024], P(('rep', 'shard'))
- grad_tokens: float32 [5632, 1024], P(('rep', 'shard'))
- first_gain_grad: float32 [1024], P('shard')
- first_bias_grad: float32 [1024], P('shard')
- joint_weight_grad: float32 [1024, 3072], P('shard')
- joint_bias_grad: float32 [3072], P('shard')
- output_weight_grad: float32 [1024, 1024], P('shard')
- output_bias_grad: float32 [1024], P('shard')
- second_gain_grad: float32 [1024], P('shard')
- second_bias_grad: float32 [1024], P('shard')
- up_weight_grad: float32 [1024, 4096], P('shard')
- up_bias_grad: float32 [4096], P('shard')
- down_weight_grad: float32 [4096, 1024], P('shard')
- down_bias_grad: float32 [1024], P('shard')
The draws below stay inside these ranges and needn't reach their ends.
Inputs may be any that keep to these rules, and one draw needn't show every extreme that they name: `lengths`: the sequences of one device, in increasing number, lie end to end from its first row of tokens and cotangent and total at most 176 tokens; in every draw one device holds a single sequence of exactly 176 tokens. `owners`: A device is numbered rep index * size of shard + shard index; every device holds one sequence or more.
All inputs are finite; a program needn't handle non-finite values.
Results may differ from the reference program's by a relative error of at most 0.0083.
Values may be sent and summed in bfloat16 or wider, within the bound.
No kernel may reach another device: no remote copies, remote signals or barrier semaphores. Data moves between devices by JAX's collectives and lax.ppermute only.
A program may use at most 192 MiB of HBM per device.

```python
import jax
import jax.numpy as jnp
from jax import lax

D = 1024
HEADS = 16
HEAD = 64
ROT = 16
FF = 4096
CAP = 176
SEQS = 64
TOKENS = 5632
DEVICES = 32


def deal(key):
    subkeys = jax.random.split(key, 4)
    leading = jax.random.permutation(subkeys[0], DEVICES).astype(jnp.int32)
    fullest = leading[0]
    extras = jax.random.randint(subkeys[1], (SEQS - DEVICES,), 0, DEVICES - 1, dtype=jnp.int32)
    extras = extras + (extras >= fullest).astype(jnp.int32)
    owners = jnp.concatenate([leading, extras])
    weights = jax.random.randint(subkeys[2], (SEQS,), 1, 9, dtype=jnp.int32)
    budget = jax.random.randint(subkeys[3], (DEVICES,), CAP // 2, CAP + 1, dtype=jnp.int32)
    devices_all = jnp.arange(DEVICES, dtype=jnp.int32)
    budget = jnp.where(devices_all == fullest, CAP, budget)
    member = (owners[:, None] == devices_all[None, :]).astype(jnp.int32)
    counts = jnp.sum(member, axis=0)
    weight_sum = jnp.sum(member * weights[:, None], axis=0)
    budget = jnp.maximum(budget, counts)
    spare_room = jnp.sum(member * (budget - counts)[None, :], axis=1)
    total_weight = jnp.sum(member * weight_sum[None, :], axis=1)
    lengths = 1 + spare_room * weights // total_weight
    return (owners, lengths.astype(jnp.int32))


def draw_lengths(key, part):
    owners, lengths = deal(key)
    return lengths


def draw_owners(key, part):
    owners, lengths = deal(key)
    return owners


def spiked(values, stream_key, source, target, parts, factor):
    def block_of(axis_at):
        return (jnp.arange(values.shape[axis_at]) // (values.shape[axis_at] // parts)).reshape((-1,) + (1,) * (values.ndim - 1 - axis_at))

    first = jax.random.permutation(stream_key, parts)[block_of(target)]
    second = (block_of(target) + parts // 2) % parts
    return jnp.where((block_of(source) == first) | (block_of(source) == second), factor * values, values)


def steps_of(stream_key, dims, cuts, smallest, top_value):
    level, own = 1.0, jax.random.fold_in(stream_key, 6)
    for dim, parts in cuts:
        heights = jnp.exp(jax.random.uniform(jax.random.fold_in(own, dim), (parts,), jnp.float32, smallest / len(cuts), top_value / len(cuts)))
        level = level * jnp.repeat(heights, dims[dim] // parts).reshape([-1 if axis == dim else 1 for axis in range(len(dims))])
    return level


def centred(key, shape, scale, bound, cuts=(), kind=jnp.bfloat16):
    values = jax.random.normal(key, shape, jnp.float32) * scale
    if len(cuts) > 0:
        values = steps_of(key, shape, cuts, -0.22, 0.18) * values
    return jnp.clip(values, min=-bound, max=bound).astype(kind)


def bell_draw_with(key, extent, spread, bound, pieces, heavy, kind=jnp.bfloat16):
    values = spread * jax.random.normal(key, extent, jnp.float32)
    if pieces:
        values = values * steps_of(key, extent, pieces, -0.22, 0.18)
    return jnp.clip(spiked(values, jax.random.fold_in(key, 3), *heavy), -bound, bound).astype(kind)


def setup_inputs(seed: int = 0) -> dict:
    key_of = jax.random.split(jax.random.key(seed), 17)
    return {
        "tokens": centred(key_of[0], (TOKENS, D), 1.0, 6.0, ((0, 32),)),
        "cotangent": bell_draw_with(key_of[1], (TOKENS, D), 1.0, 6.0, ((0, 32),), (0, 1, 32, 2.75)),
        "lengths": draw_lengths(jax.random.fold_in(key_of[16], 71), 0),
        "owners": draw_owners(jax.random.fold_in(key_of[16], 71), 0),
        "first_gain": jnp.clip(1.0 + 0.18 * jax.random.normal(key_of[4], (D,), jnp.float32), 0.099609375, 1.8984375).astype(jnp.bfloat16),
        "first_bias": centred(key_of[5], (D,), 0.3, 2.0, ((0, 16),)),
        "joint_weight": centred(key_of[6], (D, 3 * D), D ** -0.5, 0.1875, ((0, 16),)),
        "joint_bias": centred(key_of[7], (3 * D,), 0.5, 3.0, ((0, 16),)),
        "output_weight": centred(key_of[8], (D, D), (D * 8 // CAP) ** -0.5, 0.875, ((0, 16),)),
        "output_bias": centred(key_of[9], (D,), 0.3, 2.0, ((0, 16),)),
        "second_gain": jnp.clip(1.0 + 0.18 * jax.random.normal(key_of[10], (D,), jnp.float32), 0.099609375, 1.8984375).astype(jnp.bfloat16),
        "second_bias": centred(key_of[11], (D,), 0.3, 2.0, ((0, 16),)),
        "up_weight": centred(key_of[12], (D, FF), D ** -0.5, 0.1875, ((0, 16),)),
        "up_bias": centred(key_of[13], (FF,), 0.5, 3.0, ((0, 16),)),
        "down_weight": centred(key_of[14], (FF, D), FF ** -0.5, 0.09375, ((0, 16),)),
        "down_bias": centred(key_of[15], (D,), 0.3, 2.0, ((0, 16),)),
    }


@jax.custom_vjp
def low(v):
    return lax.optimization_barrier(v.astype(jnp.bfloat16)).astype(jnp.float32)

@jax.custom_vjp
def low_back(v):
    return v

def low_keep(v):
    return (low(v), None)

def low_pass(kept, grad):
    return (grad,)

def back_keep(v):
    return (v, None)

def back_low(kept, grad):
    return (low(grad),)
low.defvjp(low_keep, low_pass)
low_back.defvjp(back_keep, back_low)
EPSILON = 1e-05
HIGHEST = lax.Precision.HIGHEST

def layout(lengths, owners, device):
    owned = owners == device
    own_lengths = jnp.where(owned, lengths, 0).astype(jnp.int32)
    end_points = jnp.cumsum(own_lengths, dtype=jnp.int32)
    filled = jnp.sum(own_lengths, dtype=jnp.int32)
    places = jnp.arange(CAP, dtype=jnp.int32)
    passed = end_points[None, :] <= places[:, None]
    before_count = lax.optimization_barrier(jnp.sum(passed.astype(jnp.int32), axis=1, dtype=jnp.int32))
    seq_start = lax.optimization_barrier(jnp.max(jnp.where(passed, end_points[None, :], 0), axis=1)).astype(jnp.int32)
    filled_row = places < filled
    seq_total = lengths.shape[0]
    segment = jnp.where(filled_row, before_count, seq_total + places).astype(jnp.int32)
    position = jnp.where(filled_row, places - seq_start, 0).astype(jnp.int32)
    return (segment, position)

def rotate(vectors, position, direction):
    half_rot = ROT // 2
    frequency = 10000.0 ** (-jnp.arange(half_rot, dtype=jnp.float32) / half_rot)
    angles = position.astype(jnp.float32)[:, None] * frequency[None, :]
    cosine = jnp.cos(angles)[:, None, :]
    sine_part = direction * jnp.sin(angles)[:, None, :]
    lead_part = vectors[..., :half_rot]
    trail_part = vectors[..., half_rot:ROT]
    turned_lead = lead_part * cosine - trail_part * sine_part
    turned_trail = trail_part * cosine + lead_part * sine_part
    return jnp.concatenate([turned_lead, turned_trail, vectors[..., ROT:]], axis=-1)

def normalize(values, gain, shift):
    centre = values - lax.optimization_barrier(jnp.mean(values, axis=-1, keepdims=True))
    scaled = centre * lax.rsqrt(lax.optimization_barrier(jnp.mean(centre * centre, axis=-1, keepdims=True)) + EPSILON)
    return scaled * gain + shift

def one_block(params, values, device, lengths, owners):
    first_gain, first_bias, joint_weight, joint_bias, output_weight, output_bias, second_gain, second_bias, up_weight, up_bias, down_weight, down_bias = params
    score_scale = HEAD ** (-0.5)
    segment, position = layout(lengths, owners, device)
    places = jnp.arange(CAP, dtype=jnp.int32)
    allowed = (segment[:, None] == segment[None, :]) & (places[None, :] <= places[:, None])
    first_in = low(normalize(values, first_gain, first_bias))
    projected = low_back(jnp.dot(first_in, joint_weight, precision=HIGHEST) + joint_bias)
    heads_view = projected.reshape(CAP, 3, HEADS, HEAD)
    query_in = low(rotate(heads_view[:, 0], position, 1.0))
    keys_in = low(rotate(heads_view[:, 1], position, 1.0))
    value_in = low(heads_view[:, 2])
    scores = low_back(jnp.einsum('qhd,khd->hqk', query_in, keys_in, precision=HIGHEST) * score_scale)
    probs = low(jax.nn.softmax(jnp.where(allowed[None], scores, -1e+30), axis=-1))
    mixed = jnp.einsum('hqk,khd->qhd', probs, value_in, precision=HIGHEST).reshape(CAP, D)
    mixed = low(low_back(mixed))
    attention = jnp.dot(mixed, output_weight, precision=HIGHEST) + output_bias
    second_in = low(normalize(values, second_gain, second_bias))
    before = low_back(jnp.dot(second_in, up_weight, precision=HIGHEST) + up_bias)
    active = low(jax.nn.gelu(before, approximate=False))
    feed_out = jnp.dot(active, down_weight, precision=HIGHEST) + down_bias
    return values + attention + feed_out

def reference(tokens, cotangent, lengths, owners, first_gain, first_bias, joint_weight, joint_bias, output_weight, output_bias, second_gain, second_bias, up_weight, up_bias, down_weight, down_bias):
    params = tuple((item.astype(jnp.float32) for item in (first_gain, first_bias, joint_weight, joint_bias, output_weight, output_bias, second_gain, second_bias, up_weight, up_bias, down_weight, down_bias)))
    blocks = tokens.astype(jnp.float32).reshape(DEVICES, CAP, D)
    indices = jnp.arange(DEVICES, dtype=jnp.int32)
    step_fn = jax.checkpoint(one_block)

    def forward(blocks, params):

        def scan_body(carried, inputs):
            return (carried, step_fn(params, inputs[0], inputs[1], lengths, owners))
        unused, outputs = lax.scan(scan_body, None, (blocks, indices))
        return outputs
    outputs, pullback = jax.vjp(forward, blocks, params)
    grad_blocks, grad_params = pullback(cotangent.astype(jnp.float32).reshape(DEVICES, CAP, D))
    result = outputs.reshape(DEVICES * CAP, D).astype(jnp.bfloat16)
    grad_tokens = grad_blocks.reshape(DEVICES * CAP, D)
    return (result, grad_tokens, grad_params[0], grad_params[1], grad_params[2], grad_params[3], grad_params[4], grad_params[5], grad_params[6], grad_params[7], grad_params[8], grad_params[9], grad_params[10], grad_params[11])
```

```python
from functools import partial

import jax
import jax.numpy as jnp
from jax import lax
from jax.sharding import Mesh, PartitionSpec as P

D = 1024
HEADS = 16
HEAD = 64
ROT = 16


EPSILON = 1e-05


def layout(lengths, owners, device, row_count):
    owned = owners == device
    own_lengths = jnp.where(owned, lengths, 0)
    end_points = jnp.cumsum(own_lengths, dtype=jnp.int32)
    filled = jnp.sum(own_lengths, dtype=jnp.int32)
    places = jnp.arange(row_count, dtype=jnp.int32)
    passed = end_points[None, :] <= places[:, None]
    before_count = jnp.sum(passed.astype(jnp.int32), axis=1, dtype=jnp.int32)
    seq_start = jnp.max(jnp.where(passed, end_points[None, :], 0), axis=1)
    filled_row = places < filled
    seq_total = lengths.shape[0]
    segment = jnp.where(filled_row, before_count, seq_total + places)
    position = jnp.where(filled_row, places - seq_start, 0)
    return (segment, position)


def rotate(vectors, position, direction):
    half_rot = ROT // 2
    frequency = 10000.0 ** (-jnp.arange(half_rot, dtype=jnp.float32) / half_rot)
    angles = position.astype(jnp.float32)[:, None] * frequency[None, :]
    cosine = jnp.cos(angles)[:, None, :]
    sine_part = direction * jnp.sin(angles)[:, None, :]
    lead_part = vectors[..., :half_rot]
    trail_part = vectors[..., half_rot:ROT]
    turned_lead = lead_part * cosine - trail_part * sine_part
    turned_trail = trail_part * cosine + lead_part * sine_part
    return jnp.concatenate([turned_lead, turned_trail, vectors[..., ROT:]], axis=-1)


def normalize(values, gain, shift):
    centre = values - jnp.mean(values, axis=-1, keepdims=True)
    normed = centre * lax.rsqrt(jnp.mean(centre * centre, axis=-1, keepdims=True) + EPSILON)
    return (normed, normed * gain + shift)


def norm_back(grad_hidden, normed, gain, values):
    gain_grad = jnp.sum(grad_hidden * normed, axis=0)
    shift_grad = jnp.sum(grad_hidden, axis=0)
    grad_normed = grad_hidden * gain
    centre = values - jnp.mean(values, axis=-1, keepdims=True)
    factor = lax.rsqrt(jnp.mean(centre * centre, axis=-1, keepdims=True) + EPSILON)
    grad_values = factor * (
        grad_normed
        - jnp.mean(grad_normed, axis=-1, keepdims=True)
        - normed * jnp.mean(grad_normed * normed, axis=-1, keepdims=True)
    )
    return (gain_grad, shift_grad, grad_values)


def contract_rows(left, right):
    return lax.dot_general(
        left, right, (((0,), (0,)), ((), ())), preferred_element_type=jnp.float32
    )


def across(left, right):
    return lax.dot_general(
        left, right, (((1,), (1,)), ((), ())), preferred_element_type=jnp.float32
    )


def local(
    tokens,
    cotangent,
    lengths,
    owners,
    first_gain,
    first_bias,
    joint_weight,
    joint_bias,
    output_weight,
    output_bias,
    second_gain,
    second_bias,
    up_weight,
    up_bias,
    down_weight,
    down_bias,
):
    row_count = tokens.shape[0]
    score_scale = HEAD ** (-0.5)
    device = lax.axis_index(("rep", "shard"))
    segment, position = layout(lengths, owners, device, row_count)
    places = jnp.arange(row_count, dtype=jnp.int32)
    allowed = (segment[:, None] == segment[None, :]) & (places[None, :] <= places[:, None])
    gain_one, shift_one, joint_full, joint_offset, output_full, output_offset = (
        lax.all_gather(first_gain, "shard", axis=0, tiled=True),
        lax.all_gather(first_bias, "shard", axis=0, tiled=True),
        lax.all_gather(joint_weight, "shard", axis=0, tiled=True),
        lax.all_gather(joint_bias, "shard", axis=0, tiled=True),
        lax.all_gather(output_weight, "shard", axis=0, tiled=True),
        lax.all_gather(output_bias, "shard", axis=0, tiled=True),
    )
    gain_two, shift_two, up_full, up_offset, down_full, down_offset = (
        lax.all_gather(second_gain, "shard", axis=0, tiled=True),
        lax.all_gather(second_bias, "shard", axis=0, tiled=True),
        lax.all_gather(up_weight, "shard", axis=0, tiled=True),
        lax.all_gather(up_bias, "shard", axis=0, tiled=True),
        lax.all_gather(down_weight, "shard", axis=0, tiled=True),
        lax.all_gather(down_bias, "shard", axis=0, tiled=True),
    )
    values = tokens.astype(jnp.float32)
    normed_one, hidden_one = normalize(
        values, gain_one.astype(jnp.float32), shift_one.astype(jnp.float32)
    )
    input_one = hidden_one.astype(jnp.bfloat16)
    projected = jnp.dot(
        input_one, joint_full, preferred_element_type=jnp.float32
    ) + joint_offset.astype(jnp.float32)
    heads_view = projected.reshape(row_count, 3, HEADS, HEAD)
    query_low = rotate(heads_view[:, 0], position, 1.0).astype(jnp.bfloat16)
    keys_low = rotate(heads_view[:, 1], position, 1.0).astype(jnp.bfloat16)
    value_low = heads_view[:, 2].astype(jnp.bfloat16)
    masked = jnp.where(
        allowed[None],
        jnp.einsum("qhd,khd->hqk", query_low, keys_low, preferred_element_type=jnp.float32)
        * score_scale,
        -1e30,
    )
    row_peak = jnp.max(masked, axis=-1, keepdims=True)
    logsum = row_peak + jnp.log(jnp.sum(jnp.exp(masked - row_peak), axis=-1, keepdims=True))
    probs_low = jnp.exp(masked - logsum).astype(jnp.bfloat16)
    mixed_low = (
        jnp.einsum("hqk,khd->qhd", probs_low, value_low, preferred_element_type=jnp.float32)
        .reshape(row_count, D)
        .astype(jnp.bfloat16)
    )
    attention = jnp.dot(
        mixed_low, output_full, preferred_element_type=jnp.float32
    ) + output_offset.astype(jnp.float32)
    normed_two, hidden_two = normalize(
        values, gain_two.astype(jnp.float32), shift_two.astype(jnp.float32)
    )
    input_two = hidden_two.astype(jnp.bfloat16)
    before = jnp.dot(input_two, up_full, preferred_element_type=jnp.float32) + up_offset.astype(
        jnp.float32
    )
    active_low = jax.nn.gelu(before, approximate=False).astype(jnp.bfloat16)
    feed_out = jnp.dot(
        active_low, down_full, preferred_element_type=jnp.float32
    ) + down_offset.astype(jnp.float32)
    result = (values + attention + feed_out).astype(jnp.bfloat16)
    back_one = (
        lax.all_gather(first_gain, "shard", axis=0, tiled=True),
        lax.all_gather(joint_weight, "shard", axis=0, tiled=True),
        lax.all_gather(output_weight, "shard", axis=0, tiled=True),
    )
    back_two = (
        lax.all_gather(second_gain, "shard", axis=0, tiled=True),
        lax.all_gather(up_weight, "shard", axis=0, tiled=True),
        lax.all_gather(down_weight, "shard", axis=0, tiled=True),
    )
    gain_back_one, joint_back, output_back = back_one
    gain_back_two, up_back, down_back = back_two
    grad_out = cotangent.astype(jnp.float32)
    down_weight_grad = contract_rows(active_low, cotangent)
    down_bias_grad = jnp.sum(grad_out, axis=0)
    grad_active = across(cotangent, down_back)
    gelu_exact = partial(jax.nn.gelu, approximate=False)
    grad_before = jax.vjp(gelu_exact, before)[1](grad_active)[0].astype(jnp.bfloat16)
    up_weight_grad = contract_rows(input_two, grad_before)
    up_bias_grad = jnp.sum(grad_before.astype(jnp.float32), axis=0)
    gain_two_grad, shift_two_grad, grad_from_two = norm_back(
        across(grad_before, up_back), normed_two, gain_back_two.astype(jnp.float32), values
    )
    output_weight_grad = contract_rows(mixed_low, cotangent)
    grad_mixed = across(cotangent, output_back).astype(jnp.bfloat16).reshape(row_count, HEADS, HEAD)
    masked_again = jnp.where(
        allowed[None],
        jnp.einsum("qhd,khd->hqk", query_low, keys_low, preferred_element_type=jnp.float32)
        * score_scale,
        -1e30,
    )
    prob_back = jnp.exp(masked_again - logsum)
    prob_back_low = prob_back.astype(jnp.bfloat16)
    grad_probs = jnp.einsum(
        "qhd,khd->hqk", grad_mixed, value_low, preferred_element_type=jnp.float32
    )
    grad_value = jnp.einsum(
        "hqk,qhd->khd", prob_back_low, grad_mixed, preferred_element_type=jnp.float32
    )
    spread = jnp.sum(grad_probs * prob_back, axis=-1, keepdims=True)
    grad_scores = (prob_back * (grad_probs - spread)).astype(jnp.bfloat16)
    grad_query = rotate(
        jnp.einsum("hqk,khd->qhd", grad_scores, keys_low, preferred_element_type=jnp.float32)
        * score_scale,
        position,
        -1.0,
    )
    grad_keys = rotate(
        jnp.einsum("hqk,qhd->khd", grad_scores, query_low, preferred_element_type=jnp.float32)
        * score_scale,
        position,
        -1.0,
    )
    grad_joint = (
        jnp.stack([grad_query, grad_keys, grad_value], axis=1)
        .reshape(row_count, 3 * D)
        .astype(jnp.bfloat16)
    )
    joint_weight_grad = contract_rows(input_one, grad_joint)
    joint_bias_grad = jnp.sum(grad_joint.astype(jnp.float32), axis=0)
    gain_one_grad, shift_one_grad, grad_from_one = norm_back(
        across(grad_joint, joint_back), normed_one, gain_back_one.astype(jnp.float32), values
    )
    grad_tokens = grad_out + grad_from_one + grad_from_two
    group_shares = (
        lax.psum_scatter(gain_one_grad, "shard", scatter_dimension=0, tiled=True),
        lax.psum_scatter(shift_one_grad, "shard", scatter_dimension=0, tiled=True),
        lax.psum_scatter(joint_weight_grad, "shard", scatter_dimension=0, tiled=True),
        lax.psum_scatter(joint_bias_grad, "shard", scatter_dimension=0, tiled=True),
        lax.psum_scatter(output_weight_grad, "shard", scatter_dimension=0, tiled=True),
        lax.psum_scatter(down_bias_grad, "shard", scatter_dimension=0, tiled=True),
        lax.psum_scatter(gain_two_grad, "shard", scatter_dimension=0, tiled=True),
        lax.psum_scatter(shift_two_grad, "shard", scatter_dimension=0, tiled=True),
        lax.psum_scatter(up_weight_grad, "shard", scatter_dimension=0, tiled=True),
        lax.psum_scatter(up_bias_grad, "shard", scatter_dimension=0, tiled=True),
        lax.psum_scatter(down_weight_grad, "shard", scatter_dimension=0, tiled=True),
        lax.psum_scatter(down_bias_grad, "shard", scatter_dimension=0, tiled=True),
    )
    (
        share_gain_one,
        share_shift_one,
        share_joint_weight,
        share_joint_bias,
        share_output_weight,
        share_output_bias,
        share_gain_two,
        share_shift_two,
        share_up_weight,
        share_up_bias,
        share_down_weight,
        share_down_bias,
    ) = group_shares
    owned = lax.psum(
        (
            share_gain_one,
            share_shift_one,
            share_joint_weight,
            share_joint_bias,
            share_output_weight,
            share_output_bias,
            share_gain_two,
            share_shift_two,
            share_up_weight,
            share_up_bias,
            share_down_weight,
            share_down_bias,
        ),
        "rep",
    )
    return (
        result,
        grad_tokens,
        owned[0],
        owned[1],
        owned[2],
        owned[3],
        owned[4],
        owned[5],
        owned[6],
        owned[7],
        owned[8],
        owned[9],
        owned[10],
        owned[11],
    )


PAIR = [(0, 1), (1, 0)]
BLOCKS = 8


def swap(values, *axes):
    if len(axes) == 1:
        return lax.ppermute(values, axes[0], PAIR)
    return lax.ppermute(values, axes, [(i, 3 - i) for i in range(4)])


def join(own, other, at, axis=0):
    first = at == 0
    return jnp.concatenate(
        [jnp.where(first, own, other), jnp.where(first, other, own)], axis=axis
    )


def stack(own, other, at, axis=0):
    first = at == 0
    return jnp.stack([jnp.where(first, own, other), jnp.where(first, other, own)], axis=axis)


def take(values, at, axis=0):
    return lax.dynamic_index_in_dim(values, at, axis, keepdims=False)


def gather_rows(own):
    lane = jnp.concatenate([own, swap(own, "x"), swap(own, "p"), swap(own, "x", "p")], axis=0)
    return jnp.concatenate([lane, swap(lane, "c")], axis=0)


def scatter_rows(partial_sums):
    low = partial_sums.astype(jnp.bfloat16)
    half = low.shape[0] // 2
    rows = half // 4
    lane = low[:half].astype(jnp.float32) + swap(low[half:], "c").astype(jnp.float32)
    sent = lane[rows:].astype(jnp.bfloat16)
    return (
        lane[:rows]
        + swap(sent[:rows], "x").astype(jnp.float32)
        + swap(sent[rows : 2 * rows], "p").astype(jnp.float32)
        + swap(sent[2 * rows :], "x", "p").astype(jnp.float32)
    )


def low(values):
    return values.astype(jnp.bfloat16)


def wide(values):
    return values.astype(jnp.float32)


def grouped(
    tokens,
    cotangent,
    lengths,
    owners,
    first_gain,
    first_bias,
    joint_weight,
    joint_bias,
    output_weight,
    output_bias,
    second_gain,
    second_bias,
    up_weight,
    up_bias,
    down_weight,
    down_bias,
):
    x, o, p, q, c = (lax.axis_index(name) for name in ("x", "o", "p", "q", "c"))
    cap = tokens.shape[0]
    rows = BLOCKS * cap
    part = joint_weight.shape[0]
    unit = up_weight.shape[1] // 32
    score_scale = HEAD ** (-0.5)

    small = jnp.concatenate(
        [first_gain, first_bias, second_gain, second_bias, output_bias, down_bias, joint_bias, up_bias]
    )[None]
    for name, at in (("c", c), ("q", q), ("p", p), ("o", o)):
        small = join(small, swap(small, name), at)

    def vector(start, size):
        return wide(small[:, start : start + size]).reshape(-1)

    gain_one, shift_one, gain_two, shift_two, output_offset, down_offset = (
        vector(i * part, part) for i in range(6)
    )
    joint_own = joint_bias.shape[0]
    joint_offset = vector(6 * part, joint_own)
    up_offset = vector(6 * part + joint_own, up_bias.shape[0])

    all_tokens = gather_rows(tokens)

    joint_cut = take(joint_weight.reshape(part, 3, 2, 2, 2, 2, HEAD), x, 2)
    up_cut = take(up_weight.reshape(part, 2, 2, 2, 2, 2, unit), x, 5)
    joint_cut = joint_cut.transpose(2, 4, 0, 1, 3, 5).reshape(2, 2, part, 6 * HEAD)
    up_cut = up_cut.transpose(2, 4, 0, 1, 3, 5).reshape(2, 2, part, 4 * unit)

    def turn(cut):
        both = stack(take(cut, p), swap(take(cut, 1 - p), "p"), p)
        return stack(take(both, c, 1), swap(take(both, 1 - c, 1), "c"), c, 1)

    def spread(own):
        other = swap(own, "o")
        return stack(stack(own, swap(own, "q"), q), stack(other, swap(other, "q"), q), o)

    joint_full = spread(turn(joint_cut)).transpose(0, 2, 1, 3, 4, 5).reshape(D, 6 * HEAD)
    up_full = spread(turn(up_cut)).transpose(0, 2, 1, 3, 4, 5).reshape(D, 4 * unit)
    down_full = spread(take(down_weight.reshape(2, unit, D), x)).reshape(4 * unit, D)
    output_far = lax.ppermute(output_weight, ("x", "o"), [(0, 1), (3, 2)])
    output_head = jnp.where(x == o, output_weight, output_far)
    output_full = join(output_head, swap(output_head, "q"), q)
    all_cotangent = gather_rows(cotangent)

    joint_offset = take(take(take(joint_offset.reshape(3, 2, 2, 2, 2, HEAD), x, 1), p, 1), c, 2)
    joint_offset = joint_offset.reshape(6 * HEAD)
    up_offset = take(take(take(up_offset.reshape(2, 2, 2, 2, 2, unit), x, 4), c, 3), p, 1)
    up_offset = up_offset.reshape(4 * unit)

    blocks = [(cc, pp, xx) for cc in (0, 1) for pp in (0, 1) for xx in (0, 1)]
    devices = jnp.stack(
        [
            ((((x ^ xx) * 2 + o) * 2 + (p ^ pp)) * 2 + q) * 2 + (c ^ cc)
            for cc, pp, xx in blocks
        ]
    )
    segment, position = jax.vmap(lambda device: layout(lengths, owners, device, cap))(devices)
    places = jnp.arange(cap, dtype=jnp.int32)
    allowed = (segment[:, :, None] == segment[:, None, :]) & (
        places[None, None, :] <= places[None, :, None]
    )
    position = position.reshape(rows)

    values = wide(all_tokens)
    centre = values - jnp.mean(values, axis=-1, keepdims=True)
    normed = centre * lax.rsqrt(jnp.mean(centre * centre, axis=-1, keepdims=True) + EPSILON)
    input_one = low(normed * gain_one + shift_one)
    input_two = low(normed * gain_two + shift_two)

    projected = (
        jnp.dot(input_one, joint_full, preferred_element_type=jnp.float32) + joint_offset
    ).reshape(rows, 3, 2, HEAD)
    query_low = low(rotate(projected[:, 0], position, 1.0)).reshape(BLOCKS, cap, 2, HEAD)
    keys_low = low(rotate(projected[:, 1], position, 1.0)).reshape(BLOCKS, cap, 2, HEAD)
    value_low = low(projected[:, 2]).reshape(BLOCKS, cap, 2, HEAD)
    dot = partial(jnp.einsum, preferred_element_type=jnp.float32)
    masked = jnp.where(
        allowed[:, None], dot("bqhd,bkhd->bhqk", query_low, keys_low) * score_scale, -1e30
    )
    raised = jnp.exp(masked - jnp.max(masked, axis=-1, keepdims=True))
    probs = raised / jnp.sum(raised, axis=-1, keepdims=True)
    probs_low = low(probs)
    mixed_low = low(dot("bhqk,bkhd->bqhd", probs_low, value_low)).reshape(rows, 2 * HEAD)
    before = jnp.dot(input_two, up_full, preferred_element_type=jnp.float32) + up_offset
    gelu_exact = partial(jax.nn.gelu, approximate=False)
    active, gelu_back = jax.vjp(gelu_exact, before)
    active_low = low(active)
    lead = jnp.concatenate([mixed_low, active_low], axis=1)
    tail_weight = jnp.concatenate([output_full, down_full], axis=0)
    branches = scatter_rows(jnp.dot(lead, tail_weight, preferred_element_type=jnp.float32))
    own_values = wide(tokens)
    result = low(own_values + branches + output_offset + down_offset)

    lead_grad = contract_rows(lead, all_cotangent)
    output_grad = lead_grad[: 2 * HEAD].reshape(2, HEAD, D)
    down_grad = lead_grad[2 * HEAD :].reshape(2, 2, unit, D)
    grad_lead = across(all_cotangent, tail_weight)
    grad_mixed = low(grad_lead[:, : 2 * HEAD]).reshape(BLOCKS, cap, 2, HEAD)
    grad_before = low(gelu_back(grad_lead[:, 2 * HEAD :])[0])
    up_grad = contract_rows(input_two, grad_before)
    grad_probs = dot("bqhd,bkhd->bhqk", grad_mixed, value_low)
    grad_value = dot("bhqk,bqhd->bkhd", probs_low, grad_mixed)
    spread_sum = jnp.sum(grad_probs * probs, axis=-1, keepdims=True)
    grad_scores = low(probs * (grad_probs - spread_sum))
    grad_query = dot("bhqk,bkhd->bqhd", grad_scores, keys_low).reshape(rows, 2, HEAD)
    grad_keys = dot("bhqk,bqhd->bkhd", grad_scores, query_low).reshape(rows, 2, HEAD)
    grad_joint = low(
        jnp.stack(
            [
                rotate(grad_query * score_scale, position, -1.0),
                rotate(grad_keys * score_scale, position, -1.0),
                grad_value.reshape(rows, 2, HEAD),
            ],
            axis=1,
        ).reshape(rows, 6 * HEAD)
    )
    joint_grad = contract_rows(input_one, grad_joint)
    grad_first = across(grad_joint, joint_full)
    grad_second = across(grad_before, up_full)
    pulled = scatter_rows(grad_first * gain_one + grad_second * gain_two)

    def place(values, index, size, axis):
        hot = (jnp.arange(size) == index).reshape([size if i == axis else 1 for i in range(values.ndim + 1)])
        return jnp.where(hot, jnp.expand_dims(values, axis), 0.0)

    joint_sum = jnp.sum(wide(grad_joint), axis=0).reshape(3, 2, HEAD)
    joint_sum = place(place(place(joint_sum, c, 2, 2), p, 2, 1), x, 2, 1)
    up_sum = jnp.sum(wide(grad_before), axis=0).reshape(2, 2, unit)
    up_sum = place(place(place(up_sum, x, 2, 2), c, 2, 2), p, 2, 1)
    sums = jnp.concatenate(
        [
            jnp.sum(grad_first * normed, axis=0).reshape(-1, part),
            jnp.sum(grad_first, axis=0).reshape(-1, part),
            jnp.sum(grad_second * normed, axis=0).reshape(-1, part),
            jnp.sum(grad_second, axis=0).reshape(-1, part),
            jnp.sum(wide(cotangent), axis=0).reshape(-1, part),
            joint_sum.reshape(-1, joint_own),
            up_sum.reshape(-1, up_bias.shape[0]),
        ],
        axis=1,
    )
    for name in ("c", "q", "p", "o", "x"):
        sums = sums + swap(sums, name)
    own_sums = take(sums, ((o * 2 + p) * 2 + q) * 2 + c)

    def reduce(parts):
        ours = take(parts, q, 1) + wide(swap(low(take(parts, 1 - q, 1)), "q"))
        return take(ours, o) + wide(swap(low(take(ours, 1 - o)), "o"))

    def settle(values):
        low_values = low(values)
        return low_values, swap(low_values, "x")

    def hand(parts, columns):
        final = low(reduce(parts.reshape(2, 2, 2, 2, part, columns).transpose(0, 2, 1, 3, 4, 5)))
        both = stack(take(final, c, 1), swap(take(final, 1 - c, 1), "c"), c)
        both = stack(take(both, p, 1), swap(take(both, 1 - p, 1), "p"), p)
        return stack(both, swap(both, "x"), x)

    down_own = low(reduce(down_grad))
    down_own = wide(join(down_own, swap(down_own, "x"), x))
    output_own = take(output_grad, q) + wide(swap(low(take(output_grad, 1 - q)), "q"))
    output_own = low(output_own + wide(lax.ppermute(low(output_own), ("x", "o"), [(1, 0), (2, 3)])))
    output_own = wide(
        jnp.where(x == o, output_own, lax.ppermute(output_own, ("x", "o"), [(0, 2), (3, 1)]))
    )
    joint_own_grad = wide(
        hand(joint_grad, 6 * HEAD)
        .reshape(2, 2, 2, part, 3, 2, HEAD)
        .transpose(3, 4, 0, 1, 5, 2, 6)
        .reshape(part, 3 * D)
    )
    up_own_grad = wide(
        hand(up_grad, 4 * unit)
        .reshape(2, 2, 2, part, 2, 2, unit)
        .transpose(3, 4, 1, 5, 2, 0, 6)
        .reshape(part, 32 * unit)
    )

    own_centre = own_values - jnp.mean(own_values, axis=-1, keepdims=True)
    factor = lax.rsqrt(jnp.mean(own_centre * own_centre, axis=-1, keepdims=True) + EPSILON)
    own_normed = own_centre * factor
    grad_tokens = wide(cotangent) + factor * (
        pulled
        - jnp.mean(pulled, axis=-1, keepdims=True)
        - own_normed * jnp.mean(pulled * own_normed, axis=-1, keepdims=True)
    )
    pieces = [own_sums[i * part : (i + 1) * part] for i in range(5)]
    return (
        result,
        grad_tokens,
        pieces[0],
        pieces[1],
        joint_own_grad,
        own_sums[5 * part : 5 * part + joint_own],
        output_own,
        pieces[4],
        pieces[2],
        pieces[3],
        up_own_grad,
        own_sums[5 * part + joint_own :],
        down_own,
        pieces[4],
    )


def solution(mesh):
    if mesh.shape["rep"] == 2 and mesh.shape["shard"] * HEAD == D:
        work, body = Mesh(mesh.devices.reshape(2, 2, 2, 2, 2), ("x", "o", "p", "q", "c")), grouped
        group = ("o", "p", "q", "c")
        every = ("x", *group)
    else:
        work, body = mesh, local
        group, every = "shard", ("rep", "shard")
    row, vec, mat = P(every, None), P(group), P(group, None)
    return jax.shard_map(
        body,
        mesh=work,
        in_specs=(row, row, P(), P(), vec, vec, mat, vec, mat, vec, vec, vec, mat, vec, mat, vec),
        out_specs=(row, row, vec, vec, mat, vec, mat, vec, vec, vec, mat, vec, mat, vec),
        check_vma=False,
    )
```

```python
from functools import partial

import jax
import jax.numpy as jnp
from jax import lax
from jax.experimental import pallas as pl
from jax.experimental.pallas import tpu as pltpu
from jax.sharding import Mesh, PartitionSpec as P

D = 1024
HEADS = 16
HEAD = 64
ROT = 16


EPSILON = 1e-05


def layout(lengths, owners, device, row_count):
    owned = owners == device
    own_lengths = jnp.where(owned, lengths, 0)
    end_points = jnp.cumsum(own_lengths, dtype=jnp.int32)
    filled = jnp.sum(own_lengths, dtype=jnp.int32)
    places = jnp.arange(row_count, dtype=jnp.int32)
    passed = end_points[None, :] <= places[:, None]
    before_count = jnp.sum(passed.astype(jnp.int32), axis=1, dtype=jnp.int32)
    seq_start = jnp.max(jnp.where(passed, end_points[None, :], 0), axis=1)
    filled_row = places < filled
    seq_total = lengths.shape[0]
    segment = jnp.where(filled_row, before_count, seq_total + places)
    position = jnp.where(filled_row, places - seq_start, 0)
    return (segment, position)


def rotate(vectors, position, direction):
    half_rot = ROT // 2
    frequency = 10000.0 ** (-jnp.arange(half_rot, dtype=jnp.float32) / half_rot)
    angles = position.astype(jnp.float32)[:, None] * frequency[None, :]
    cosine = jnp.cos(angles)[:, None, :]
    sine_part = direction * jnp.sin(angles)[:, None, :]
    lead_part = vectors[..., :half_rot]
    trail_part = vectors[..., half_rot:ROT]
    turned_lead = lead_part * cosine - trail_part * sine_part
    turned_trail = trail_part * cosine + lead_part * sine_part
    return jnp.concatenate([turned_lead, turned_trail, vectors[..., ROT:]], axis=-1)


def normalize(values, gain, shift):
    centre = values - jnp.mean(values, axis=-1, keepdims=True)
    normed = centre * lax.rsqrt(jnp.mean(centre * centre, axis=-1, keepdims=True) + EPSILON)
    return (normed, normed * gain + shift)


def norm_back(grad_hidden, normed, gain, values):
    gain_grad = jnp.sum(grad_hidden * normed, axis=0)
    shift_grad = jnp.sum(grad_hidden, axis=0)
    grad_normed = grad_hidden * gain
    centre = values - jnp.mean(values, axis=-1, keepdims=True)
    factor = lax.rsqrt(jnp.mean(centre * centre, axis=-1, keepdims=True) + EPSILON)
    grad_values = factor * (
        grad_normed
        - jnp.mean(grad_normed, axis=-1, keepdims=True)
        - normed * jnp.mean(grad_normed * normed, axis=-1, keepdims=True)
    )
    return (gain_grad, shift_grad, grad_values)


def contract_rows(left, right):
    return lax.dot_general(
        left, right, (((0,), (0,)), ((), ())), preferred_element_type=jnp.float32
    )


def across(left, right):
    return lax.dot_general(
        left, right, (((1,), (1,)), ((), ())), preferred_element_type=jnp.float32
    )


def local(
    tokens,
    cotangent,
    lengths,
    owners,
    first_gain,
    first_bias,
    joint_weight,
    joint_bias,
    output_weight,
    output_bias,
    second_gain,
    second_bias,
    up_weight,
    up_bias,
    down_weight,
    down_bias,
):
    row_count = tokens.shape[0]
    score_scale = HEAD ** (-0.5)
    device = lax.axis_index(("rep", "shard"))
    segment, position = layout(lengths, owners, device, row_count)
    places = jnp.arange(row_count, dtype=jnp.int32)
    allowed = (segment[:, None] == segment[None, :]) & (places[None, :] <= places[:, None])
    gain_one, shift_one, joint_full, joint_offset, output_full, output_offset = (
        lax.all_gather(first_gain, "shard", axis=0, tiled=True),
        lax.all_gather(first_bias, "shard", axis=0, tiled=True),
        lax.all_gather(joint_weight, "shard", axis=0, tiled=True),
        lax.all_gather(joint_bias, "shard", axis=0, tiled=True),
        lax.all_gather(output_weight, "shard", axis=0, tiled=True),
        lax.all_gather(output_bias, "shard", axis=0, tiled=True),
    )
    gain_two, shift_two, up_full, up_offset, down_full, down_offset = (
        lax.all_gather(second_gain, "shard", axis=0, tiled=True),
        lax.all_gather(second_bias, "shard", axis=0, tiled=True),
        lax.all_gather(up_weight, "shard", axis=0, tiled=True),
        lax.all_gather(up_bias, "shard", axis=0, tiled=True),
        lax.all_gather(down_weight, "shard", axis=0, tiled=True),
        lax.all_gather(down_bias, "shard", axis=0, tiled=True),
    )
    values = tokens.astype(jnp.float32)
    normed_one, hidden_one = normalize(
        values, gain_one.astype(jnp.float32), shift_one.astype(jnp.float32)
    )
    input_one = hidden_one.astype(jnp.bfloat16)
    projected = jnp.dot(
        input_one, joint_full, preferred_element_type=jnp.float32
    ) + joint_offset.astype(jnp.float32)
    heads_view = projected.reshape(row_count, 3, HEADS, HEAD)
    query_low = rotate(heads_view[:, 0], position, 1.0).astype(jnp.bfloat16)
    keys_low = rotate(heads_view[:, 1], position, 1.0).astype(jnp.bfloat16)
    value_low = heads_view[:, 2].astype(jnp.bfloat16)
    masked = jnp.where(
        allowed[None],
        jnp.einsum("qhd,khd->hqk", query_low, keys_low, preferred_element_type=jnp.float32)
        * score_scale,
        -1e30,
    )
    row_peak = jnp.max(masked, axis=-1, keepdims=True)
    logsum = row_peak + jnp.log(jnp.sum(jnp.exp(masked - row_peak), axis=-1, keepdims=True))
    probs_low = jnp.exp(masked - logsum).astype(jnp.bfloat16)
    mixed_low = (
        jnp.einsum("hqk,khd->qhd", probs_low, value_low, preferred_element_type=jnp.float32)
        .reshape(row_count, D)
        .astype(jnp.bfloat16)
    )
    attention = jnp.dot(
        mixed_low, output_full, preferred_element_type=jnp.float32
    ) + output_offset.astype(jnp.float32)
    normed_two, hidden_two = normalize(
        values, gain_two.astype(jnp.float32), shift_two.astype(jnp.float32)
    )
    input_two = hidden_two.astype(jnp.bfloat16)
    before = jnp.dot(input_two, up_full, preferred_element_type=jnp.float32) + up_offset.astype(
        jnp.float32
    )
    active_low = jax.nn.gelu(before, approximate=False).astype(jnp.bfloat16)
    feed_out = jnp.dot(
        active_low, down_full, preferred_element_type=jnp.float32
    ) + down_offset.astype(jnp.float32)
    result = (values + attention + feed_out).astype(jnp.bfloat16)
    back_one = (
        lax.all_gather(first_gain, "shard", axis=0, tiled=True),
        lax.all_gather(joint_weight, "shard", axis=0, tiled=True),
        lax.all_gather(output_weight, "shard", axis=0, tiled=True),
    )
    back_two = (
        lax.all_gather(second_gain, "shard", axis=0, tiled=True),
        lax.all_gather(up_weight, "shard", axis=0, tiled=True),
        lax.all_gather(down_weight, "shard", axis=0, tiled=True),
    )
    gain_back_one, joint_back, output_back = back_one
    gain_back_two, up_back, down_back = back_two
    grad_out = cotangent.astype(jnp.float32)
    down_weight_grad = contract_rows(active_low, cotangent)
    down_bias_grad = jnp.sum(grad_out, axis=0)
    grad_active = across(cotangent, down_back)
    gelu_exact = partial(jax.nn.gelu, approximate=False)
    grad_before = jax.vjp(gelu_exact, before)[1](grad_active)[0].astype(jnp.bfloat16)
    up_weight_grad = contract_rows(input_two, grad_before)
    up_bias_grad = jnp.sum(grad_before.astype(jnp.float32), axis=0)
    gain_two_grad, shift_two_grad, grad_from_two = norm_back(
        across(grad_before, up_back), normed_two, gain_back_two.astype(jnp.float32), values
    )
    output_weight_grad = contract_rows(mixed_low, cotangent)
    grad_mixed = across(cotangent, output_back).astype(jnp.bfloat16).reshape(row_count, HEADS, HEAD)
    masked_again = jnp.where(
        allowed[None],
        jnp.einsum("qhd,khd->hqk", query_low, keys_low, preferred_element_type=jnp.float32)
        * score_scale,
        -1e30,
    )
    prob_back = jnp.exp(masked_again - logsum)
    prob_back_low = prob_back.astype(jnp.bfloat16)
    grad_probs = jnp.einsum(
        "qhd,khd->hqk", grad_mixed, value_low, preferred_element_type=jnp.float32
    )
    grad_value = jnp.einsum(
        "hqk,qhd->khd", prob_back_low, grad_mixed, preferred_element_type=jnp.float32
    )
    spread = jnp.sum(grad_probs * prob_back, axis=-1, keepdims=True)
    grad_scores = (prob_back * (grad_probs - spread)).astype(jnp.bfloat16)
    grad_query = rotate(
        jnp.einsum("hqk,khd->qhd", grad_scores, keys_low, preferred_element_type=jnp.float32)
        * score_scale,
        position,
        -1.0,
    )
    grad_keys = rotate(
        jnp.einsum("hqk,qhd->khd", grad_scores, query_low, preferred_element_type=jnp.float32)
        * score_scale,
        position,
        -1.0,
    )
    grad_joint = (
        jnp.stack([grad_query, grad_keys, grad_value], axis=1)
        .reshape(row_count, 3 * D)
        .astype(jnp.bfloat16)
    )
    joint_weight_grad = contract_rows(input_one, grad_joint)
    joint_bias_grad = jnp.sum(grad_joint.astype(jnp.float32), axis=0)
    gain_one_grad, shift_one_grad, grad_from_one = norm_back(
        across(grad_joint, joint_back), normed_one, gain_back_one.astype(jnp.float32), values
    )
    grad_tokens = grad_out + grad_from_one + grad_from_two
    group_shares = (
        lax.psum_scatter(gain_one_grad, "shard", scatter_dimension=0, tiled=True),
        lax.psum_scatter(shift_one_grad, "shard", scatter_dimension=0, tiled=True),
        lax.psum_scatter(joint_weight_grad, "shard", scatter_dimension=0, tiled=True),
        lax.psum_scatter(joint_bias_grad, "shard", scatter_dimension=0, tiled=True),
        lax.psum_scatter(output_weight_grad, "shard", scatter_dimension=0, tiled=True),
        lax.psum_scatter(down_bias_grad, "shard", scatter_dimension=0, tiled=True),
        lax.psum_scatter(gain_two_grad, "shard", scatter_dimension=0, tiled=True),
        lax.psum_scatter(shift_two_grad, "shard", scatter_dimension=0, tiled=True),
        lax.psum_scatter(up_weight_grad, "shard", scatter_dimension=0, tiled=True),
        lax.psum_scatter(up_bias_grad, "shard", scatter_dimension=0, tiled=True),
        lax.psum_scatter(down_weight_grad, "shard", scatter_dimension=0, tiled=True),
        lax.psum_scatter(down_bias_grad, "shard", scatter_dimension=0, tiled=True),
    )
    (
        share_gain_one,
        share_shift_one,
        share_joint_weight,
        share_joint_bias,
        share_output_weight,
        share_output_bias,
        share_gain_two,
        share_shift_two,
        share_up_weight,
        share_up_bias,
        share_down_weight,
        share_down_bias,
    ) = group_shares
    owned = lax.psum(
        (
            share_gain_one,
            share_shift_one,
            share_joint_weight,
            share_joint_bias,
            share_output_weight,
            share_output_bias,
            share_gain_two,
            share_shift_two,
            share_up_weight,
            share_up_bias,
            share_down_weight,
            share_down_bias,
        ),
        "rep",
    )
    return (
        result,
        grad_tokens,
        owned[0],
        owned[1],
        owned[2],
        owned[3],
        owned[4],
        owned[5],
        owned[6],
        owned[7],
        owned[8],
        owned[9],
        owned[10],
        owned[11],
    )


PAIR = [(0, 1), (1, 0)]
BLOCKS = 8
LANE = 128
GROUP = ("o", "p", "q", "c")
VMEM_BYTES = 56 * 1024 * 1024


def swap(values, *axes):
    if len(axes) == 1:
        return lax.ppermute(values, axes[0], PAIR)
    return lax.ppermute(values, axes, [(i, 3 - i) for i in range(4)])


def join(own, other, at, axis=0):
    first = at == 0
    return jnp.concatenate(
        [jnp.where(first, own, other), jnp.where(first, other, own)], axis=axis
    )


def take(values, at, axis=0):
    return lax.dynamic_index_in_dim(values, at, axis, keepdims=False)


def low(values):
    return values.astype(jnp.bfloat16)


def wide(values):
    return values.astype(jnp.float32)


def times(left, right):
    return jnp.dot(left, right, preferred_element_type=jnp.float32)


def places_of(ids_ref):
    return tuple(ids_ref[i] for i in range(5))


def call(kernel, outs, scratch, flops, *operands, memory):
    whole = pl.BlockSpec(memory_space=pltpu.VMEM)
    specs = {
        "s": pl.BlockSpec(memory_space=pltpu.SMEM),
        "v": whole,
        "h": pl.BlockSpec(memory_space=pl.ANY),
    }
    size = sum(leaf.size * leaf.dtype.itemsize for leaf in (*operands, *outs))
    return pl.pallas_call(
        kernel,
        out_shape=tuple(outs),
        in_specs=[specs[kind] for kind in memory],
        out_specs=tuple(whole for _ in outs),
        scratch_shapes=scratch,
        compiler_params=pltpu.CompilerParams(vmem_limit_bytes=VMEM_BYTES),
        cost_estimate=pl.CostEstimate(flops=flops, bytes_accessed=size, transcendentals=0),
    )(*operands)


def fetch(pairs, sems):
    copies = [
        pltpu.make_async_copy(source, target, sems.at[i])
        for i, (source, target) in enumerate(pairs)
    ]
    for copy in copies:
        copy.start()
    return copies


def finish(copies):
    for copy in copies:
        copy.wait()


def row_pairs(near, far, target, start, cap):
    return [
        (source.at[k, pl.ds(start, cap)], target.at[pl.ds((half * 4 + k) * cap, cap)])
        for half, source in enumerate((near, far))
        for k in range(4)
    ]


def sheet_pairs(pieces, target, places):
    x, o, p, q, c = places
    pairs = []
    for index, piece in enumerate(pieces):
        jo, jq = index // 2, index % 2
        rows = piece.shape[1]
        for k in range(4):
            jc, jp = k // 2, k % 2
            at = ((((o ^ jo) * 2 + (p ^ jp)) * 2 + (q ^ jq)) * 2 + (c ^ jc)) * rows
            pairs.append((piece.at[k], target.at[pl.ds(pl.multiple_of(at, rows), rows)]))
    return pairs


def tall_pairs(pieces, target, places):
    x, o, p, q, c = places
    pairs = []
    for index, piece in enumerate(pieces):
        jo, jq = index // 2, index % 2
        rows = piece.shape[0]
        at = ((o ^ jo) * 2 + (q ^ jq)) * rows
        pairs.append((piece, target.at[pl.ds(pl.multiple_of(at, rows), rows)]))
    return pairs


def norm_of(tokens):
    values = wide(tokens)
    centre = values - jnp.mean(values, axis=-1, keepdims=True)
    return centre * lax.rsqrt(jnp.mean(centre * centre, axis=-1, keepdims=True) + EPSILON)


def fold(values):
    rows, columns = values.shape
    return jnp.sum(values.reshape(rows // 8, 8, columns), axis=0)


def block_rows(block, cap):
    return pl.ds(pl.multiple_of(block * cap, 16), cap)


def cut_kernel(ids, joint, up, down, keep, send, half):
    x, o, p, q, c = places_of(ids)
    parts = joint.shape[1] // D

    def block(ref, index):
        return ref[:, pl.ds(pl.multiple_of(index * LANE, LANE), LANE)]

    for jp, target in ((0, keep), (1, send)):
        for jc in (0, 1):
            pp, cc = p ^ jp, c ^ jc
            for part in range(parts):
                target[jc, :, part * LANE : (part + 1) * LANE] = block(
                    joint, part * 8 + x * 4 + pp * 2 + cc
                )
            for k in range(4):
                oo, qq = k // 2, k % 2
                at = (parts + k) * LANE
                target[jc, :, at : at + LANE] = block(
                    up, (((oo * 2 + pp) * 2 + qq) * 2 + cc) * 2 + x
                )
    rows = half.shape[0]
    half[...] = down[pl.ds(pl.multiple_of(x * rows, rows), rows), :]


def attention_kernel(
    ids,
    near,
    far,
    sheet_0,
    sheet_1,
    sheet_2,
    sheet_3,
    output_weight,
    cosine,
    sine,
    position,
    gain,
    shift,
    offset,
    mixed_ref,
    grad_ref,
    home,
    away,
    output_grad,
    grad_sum,
    tokens,
    cotangent,
    joint,
    inputs,
    total,
    sems,
):
    places = places_of(ids)
    cap = near.shape[1] // 2
    copies = fetch(
        sheet_pairs((sheet_0, sheet_1, sheet_2, sheet_3), joint, places)
        + row_pairs(near, far, tokens, 0, cap)
        + row_pairs(near, far, cotangent, cap, cap),
        sems,
    )
    finish(copies)
    total[...] = jnp.zeros_like(total)
    lane = lax.broadcasted_iota(jnp.int32, (cap, LANE), 1)
    lead = lane % HEAD < ROT // 2
    mine = (lane < HEAD, lane >= HEAD)
    down = lax.broadcasted_iota(jnp.int32, (cap, cap), 0)
    along = lax.broadcasted_iota(jnp.int32, (cap, cap), 1)
    scale = HEAD ** (-0.5)
    half_rot = ROT // 2

    def turn(values, cos_part, sin_part):
        other = jnp.where(
            lead, pltpu.roll(values, LANE - half_rot, 1), pltpu.roll(values, half_rot, 1)
        )
        return values * cos_part + other * sin_part

    def step(block, carry):
        rows = block_rows(block, cap)
        input_low = low(norm_of(tokens[rows, :]) * gain[...] + shift[...])
        inputs[rows, :] = input_low
        projected = times(input_low, joint[...]) + offset[...]
        cos_part, sin_part = cosine[rows, :], sine[rows, :]
        query = low(turn(projected[:, :LANE], cos_part, sin_part))
        keys = low(turn(projected[:, LANE : 2 * LANE], cos_part, sin_part))
        value = low(projected[:, 2 * LANE :])
        grad_mixed = low(across(cotangent[rows, :], output_weight[...]))
        allowed = (along <= down) & (along >= down - position[rows, :])
        found = []
        for head in (0, 1):
            own = mine[head]
            query_own = jnp.where(own, query, jnp.zeros_like(query))
            grad_own = jnp.where(own, grad_mixed, jnp.zeros_like(grad_mixed))
            scores = jnp.where(allowed, across(query_own, keys) * scale, -1e30)
            raised = jnp.exp(scores - jnp.max(scores, axis=-1, keepdims=True))
            probs = raised / jnp.sum(raised, axis=-1, keepdims=True)
            probs_low = low(probs)
            grad_probs = across(grad_own, value)
            spread = jnp.sum(grad_probs * probs, axis=-1, keepdims=True)
            grad_scores = low(probs * (grad_probs - spread))
            found.append(
                (
                    times(probs_low, value),
                    times(grad_scores, keys) * scale,
                    contract_rows(grad_scores, query) * scale,
                    contract_rows(probs_low, grad_mixed),
                )
            )
        mixed, grad_query, grad_keys, grad_value = (
            jnp.where(mine[0], first, second) for first, second in zip(*found)
        )
        mixed_ref[rows, :] = low(mixed)
        grad_joint = low(
            jnp.concatenate(
                [
                    turn(grad_query, cos_part, -sin_part),
                    turn(grad_keys, cos_part, -sin_part),
                    grad_value,
                ],
                axis=1,
            )
        )
        grad_ref[rows, :] = grad_joint
        total[...] += fold(wide(grad_joint))
        return carry

    lax.fori_loop(0, BLOCKS, step, 0)
    grad_sum[...] = jnp.sum(total[...], axis=0, keepdims=True)
    output_grad[...] = low(contract_rows(mixed_ref[...], cotangent[...]))
    sheet_grads(inputs, grad_ref, home, away, places)


def sheet_grads(inputs, grads, home, away, places):
    x, o, p, q, c = places
    rows = home.shape[2]
    for oo in (0, 1):
        found = contract_rows(inputs[:, oo * D // 2 : (oo + 1) * D // 2], grads[...])
        found = low(found).reshape(2, 2, 2, rows, -1)
        for pp in (0, 1):
            for cc in (0, 1):
                at = (c ^ cc) * 2 + (p ^ pp)
                home[o ^ oo, at] = jnp.where(q == 0, found[pp, 0, cc], found[pp, 1, cc])
                away[o ^ oo, at] = jnp.where(q == 0, found[pp, 1, cc], found[pp, 0, cc])


def forward_kernel(
    ids,
    near,
    far,
    sheet_0,
    sheet_1,
    sheet_2,
    sheet_3,
    tall_0,
    tall_1,
    tall_2,
    tall_3,
    output_weight,
    mixed,
    gain,
    shift,
    offset,
    inputs,
    before_ref,
    near_out,
    far_out,
    home,
    away,
    tokens,
    cotangent,
    up,
    down,
    active_all,
    sems,
):
    places = places_of(ids)
    x, o, p, q, c = places
    cap = near.shape[1] // 2
    copies = fetch(
        sheet_pairs((sheet_0, sheet_1, sheet_2, sheet_3), up, places)
        + tall_pairs((tall_0, tall_1, tall_2, tall_3), down, places)
        + row_pairs(near, far, tokens, 0, cap)
        + row_pairs(near, far, cotangent, cap, cap),
        sems,
    )
    finish(copies)

    def step(block, target):
        rows = block_rows(block, cap)
        input_low = low(norm_of(tokens[rows, :]) * gain[...] + shift[...])
        inputs[rows, :] = input_low
        before = times(input_low, up[...]) + offset[...]
        before_ref[rows, :] = before
        active = low(before * (0.5 + 0.5 * lax.erf(before * 0.5**0.5)))
        active_all[rows, :] = active
        return times(mixed[rows, :], output_weight[...]) + times(active, down[...])

    def first(block, carry):
        near_out[block_rows(block, cap), :] = step(block, None)
        return carry

    def second(block, carry):
        far_out[block_rows(block, cap), :] = low(step(block + BLOCKS // 2, None))
        return carry

    lax.fori_loop(0, BLOCKS // 2, first, 0)
    lax.fori_loop(0, BLOCKS // 2, second, 0)
    unit = home.shape[1]
    for oo in (0, 1):
        found = low(contract_rows(active_all[:, oo * 2 * unit : (oo + 1) * 2 * unit], cotangent[...]))
        home[o ^ oo] = jnp.where(q == 0, found[:unit], found[unit:])
        away[o ^ oo] = jnp.where(q == 0, found[unit:], found[:unit])


def backward_kernel(
    ids,
    near,
    far,
    sheet_0,
    sheet_1,
    sheet_2,
    sheet_3,
    tall_0,
    tall_1,
    tall_2,
    tall_3,
    join_0,
    join_1,
    join_2,
    join_3,
    inputs,
    before_all,
    grad_joint,
    gain_one,
    gain_two,
    near_out,
    far_out,
    home,
    away,
    sums,
    grad_sum,
    tokens,
    cotangent,
    up,
    down,
    joint,
    grad_all,
    totals,
    total,
    sems,
):
    places = places_of(ids)
    cap = near.shape[1] // 2
    copies = fetch(
        sheet_pairs((sheet_0, sheet_1, sheet_2, sheet_3), up, places)
        + sheet_pairs((join_0, join_1, join_2, join_3), joint, places)
        + tall_pairs((tall_0, tall_1, tall_2, tall_3), down, places)
        + row_pairs(near, far, tokens, 0, cap)
        + row_pairs(near, far, cotangent, cap, cap),
        sems,
    )
    finish(copies)
    totals[...] = jnp.zeros_like(totals)
    total[...] = jnp.zeros_like(total)

    def step(block, unused):
        rows = block_rows(block, cap)
        before = before_all[rows, :]
        grad_active = across(cotangent[rows, :], down[...])
        slope = 0.5 + 0.5 * lax.erf(before * 0.5**0.5)
        slope = slope + before * jnp.exp(-0.5 * before * before) * (0.5 / jnp.pi) ** 0.5
        grad_before = low(grad_active * slope)
        grad_all[rows, :] = grad_before
        total[...] += fold(wide(grad_before))
        normed = norm_of(tokens[rows, :])
        grad_first = across(grad_joint[rows, :], joint[...])
        grad_second = across(grad_before, up[...])
        totals[0] += fold(grad_first * normed)
        totals[1] += fold(grad_first)
        totals[2] += fold(grad_second * normed)
        totals[3] += fold(grad_second)
        return grad_first * gain_one[...] + grad_second * gain_two[...]

    def first(block, carry):
        near_out[block_rows(block, cap), :] = step(block, None)
        return carry

    def second(block, carry):
        far_out[block_rows(block, cap), :] = low(step(block + BLOCKS // 2, None))
        return carry

    lax.fori_loop(0, BLOCKS // 2, first, 0)
    lax.fori_loop(0, BLOCKS // 2, second, 0)
    sums[...] = jnp.sum(totals[...], axis=1)
    grad_sum[...] = jnp.sum(total[...], axis=0, keepdims=True)
    sheet_grads(inputs, grad_all, home, away, places)


def lay_kernel(blocks, ids, own, other, out):
    x, o, p, q, c = places_of(ids)
    for xx, source in ((0, own), (1, other)):
        for pp in (0, 1):
            for cc in (0, 1):
                values = wide(source[pp, cc])
                for k, at in enumerate(blocks(x ^ xx, p ^ pp, c ^ cc)):
                    out[:, pl.ds(pl.multiple_of(at * LANE, LANE), LANE)] = values[
                        :, k * LANE : (k + 1) * LANE
                    ]


def joint_blocks(x, p, c):
    return [part * 8 + x * 4 + p * 2 + c for part in range(3)]


def up_blocks(x, p, c):
    return [(((oo * 2 + p) * 2 + qq) * 2 + c) * 2 + x for oo in (0, 1) for qq in (0, 1)]


def scatter_rows(near, far):
    lane = near + wide(swap(far, "c"))
    rows = lane.shape[0] // 4
    sent = low(lane[rows:])
    return (
        lane[:rows]
        + wide(swap(sent[:rows], "x"))
        + wide(swap(sent[rows : 2 * rows], "p"))
        + wide(swap(sent[2 * rows :], "x", "p"))
    )


def grouped(
    tokens,
    cotangent,
    lengths,
    owners,
    first_gain,
    first_bias,
    joint_weight,
    joint_bias,
    output_weight,
    output_bias,
    second_gain,
    second_bias,
    up_weight,
    up_bias,
    down_weight,
    down_bias,
):
    x, o, p, q, c = (lax.axis_index(name) for name in ("x", *GROUP))
    ids = jnp.stack([x, o, p, q, c]).astype(jnp.int32)
    cap = tokens.shape[0]
    rows = BLOCKS * cap
    part = joint_weight.shape[0]
    hidden = up_weight.shape[1] // 8
    unit = hidden // 4
    bf, f32 = jnp.bfloat16, jnp.float32

    def like(shape, kind):
        return jax.ShapeDtypeStruct(shape, kind)

    small = jnp.concatenate(
        [first_gain, first_bias, second_gain, second_bias, output_bias, down_bias, joint_bias, up_bias]
    )[None]
    for name, at in (("c", c), ("q", q), ("p", p), ("o", o)):
        small = join(small, swap(small, name), at)

    def vector(start, size):
        return wide(small[:, start : start + size]).reshape(1, -1)

    gain_one, shift_one, gain_two, shift_two, output_offset, down_offset = (
        vector(i * part, part) for i in range(6)
    )
    joint_own = joint_bias.shape[0]
    joint_offset = vector(6 * part, joint_own)
    up_offset = vector(6 * part + joint_own, up_bias.shape[0])
    joint_offset = take(joint_offset.reshape(3, 8, LANE), x * 4 + p * 2 + c, 1).reshape(1, 3 * LANE)
    up_offset = take(take(take(up_offset.reshape(2, 2, 2, 2, 2, unit), x, 4), c, 3), p, 1)
    up_offset = up_offset.reshape(1, hidden)

    pair = jnp.concatenate([tokens, cotangent], axis=0)
    near = jnp.stack([pair, swap(pair, "x"), swap(pair, "p"), swap(pair, "x", "p")], axis=0)
    far = swap(near, "c")

    keep, send, down_half = call(
        cut_kernel,
        [
            like((2, part, 3 * LANE + hidden), bf),
            like((2, part, 3 * LANE + hidden), bf),
            like((unit, D), bf),
        ],
        [],
        0,
        ids,
        joint_weight,
        up_weight,
        down_weight,
        memory="svvv",
    )
    came = swap(send, "p")
    turned = jnp.concatenate(
        [keep[:1], came[:1], swap(jnp.concatenate([keep[1:], came[1:]], axis=0), "c")], axis=0
    )

    def spread(own):
        other = swap(own, "o")
        return own, swap(own, "q"), other, swap(other, "q")

    joint_sheets = spread(turned[:, :, : 3 * LANE])
    up_sheets = spread(turned[:, :, 3 * LANE :])
    down_talls = spread(down_half)
    turn_over = [
        (((a * 2 + b) * 2 + e) * 2 + f, ((b * 2 + a) * 2 + f) * 2 + e)
        for a in (0, 1)
        for b in (0, 1)
        for e in (0, 1)
        for f in (0, 1)
    ]
    cross = ("x", "o", "q", "c")
    output_pair = lax.ppermute(join(output_weight, swap(output_weight, "c"), c), cross, turn_over)

    devices = jnp.stack(
        [
            ((((x ^ xx) * 2 + o) * 2 + (p ^ pp)) * 2 + q) * 2 + (c ^ cc)
            for cc in (0, 1)
            for pp in (0, 1)
            for xx in (0, 1)
        ]
    )
    position = jax.vmap(lambda device: layout(lengths, owners, device, cap)[1])(devices)
    position = position.reshape(rows, 1)
    place = jnp.arange(LANE) % HEAD
    half_rot = ROT // 2
    frequency = 10000.0 ** (-jnp.arange(half_rot, dtype=f32) / half_rot)
    angles = position.astype(f32) * jnp.tile(frequency, LANE // half_rot)[None, :]
    cosine = jnp.where(place < ROT, jnp.cos(angles), 1.0)
    sine = jnp.sin(angles)
    sine = jnp.where(place < half_rot, -sine, jnp.where(place < ROT, sine, 0.0))

    sheet = (4, part, 3 * LANE)
    copies = pltpu.SemaphoreType.DMA
    mixed, grad_joint, joint_home, joint_away, output_grad, joint_sum = call(
        attention_kernel,
        [
            like((rows, LANE), bf),
            like((rows, 3 * LANE), bf),
            like((2, *sheet), bf),
            like((2, *sheet), bf),
            like((LANE, D), bf),
            like((1, 3 * LANE), f32),
        ],
        [
            pltpu.VMEM((rows, D), bf),
            pltpu.VMEM((rows, D), bf),
            pltpu.VMEM((D, 3 * LANE), bf),
            pltpu.VMEM((rows, D), bf),
            pltpu.VMEM((8, 3 * LANE), f32),
            copies((32,)),
        ],
        rows * D * LANE * 16,
        ids,
        near,
        far,
        *joint_sheets,
        output_pair,
        cosine,
        sine,
        position,
        gain_one,
        shift_one,
        joint_offset,
        memory="shhhhhhvvvvvvv",
    )

    tall = (unit, D)
    sheet = (4, part, hidden)
    inputs, before, near_part, far_part, down_home, down_away = call(
        forward_kernel,
        [
            like((rows, D), bf),
            like((rows, hidden), f32),
            like((rows // 2, D), f32),
            like((rows // 2, D), bf),
            like((2, *tall), bf),
            like((2, *tall), bf),
        ],
        [
            pltpu.VMEM((rows, D), bf),
            pltpu.VMEM((rows, D), bf),
            pltpu.VMEM((D, hidden), bf),
            pltpu.VMEM((hidden, D), bf),
            pltpu.VMEM((rows, hidden), bf),
            copies((36,)),
        ],
        rows * D * hidden * 6,
        ids,
        near,
        far,
        *up_sheets,
        *down_talls,
        output_pair,
        mixed,
        gain_two,
        shift_two,
        up_offset,
        memory="shhhhhhhhhhvvvvv",
    )
    own_values = wide(tokens)
    result = low(own_values + scatter_rows(near_part, far_part) + output_offset + down_offset)

    near_part, far_part, up_home, up_away, norm_sums, up_sum = call(
        backward_kernel,
        [
            like((rows // 2, D), f32),
            like((rows // 2, D), bf),
            like((2, *sheet), bf),
            like((2, *sheet), bf),
            like((4, D), f32),
            like((1, hidden), f32),
        ],
        [
            pltpu.VMEM((rows, D), bf),
            pltpu.VMEM((rows, D), bf),
            pltpu.VMEM((D, hidden), bf),
            pltpu.VMEM((hidden, D), bf),
            pltpu.VMEM((D, 3 * LANE), bf),
            pltpu.VMEM((rows, hidden), bf),
            pltpu.VMEM((4, 8, D), f32),
            pltpu.VMEM((8, hidden), f32),
            copies((52,)),
        ],
        rows * D * (hidden * 6 + LANE * 6),
        ids,
        near,
        far,
        *up_sheets,
        *down_talls,
        *joint_sheets,
        inputs,
        before,
        grad_joint,
        gain_one,
        gain_two,
        memory="shhhhhhhhhhhhhhvvvvv",
    )
    pulled = scatter_rows(near_part, far_part)

    def put(values, index, size, axis):
        hot = (jnp.arange(size) == index).reshape([size if i == axis else 1 for i in range(values.ndim + 1)])
        return jnp.where(hot, jnp.expand_dims(values, axis), 0.0)

    joint_sum = put(joint_sum.reshape(3, LANE), x * 4 + p * 2 + c, 8, 1)
    up_sum = put(put(put(up_sum.reshape(2, 2, unit), x, 2, 2), c, 2, 2), p, 2, 1)
    sums = jnp.concatenate(
        [
            *(norm_sums[i].reshape(-1, part) for i in range(4)),
            jnp.sum(wide(cotangent), axis=0).reshape(-1, part),
            joint_sum.reshape(-1, joint_own),
            up_sum.reshape(-1, up_bias.shape[0]),
        ],
        axis=1,
    )
    for name in ("c", "q", "p", "o", "x"):
        sums = sums + swap(sums, name)
    own_sums = take(sums, ((o * 2 + p) * 2 + q) * 2 + c)

    def reduce(home, away):
        both = wide(home) + wide(swap(away, "q"))
        return both[0] + wide(swap(low(both[1]), "o"))

    def hand(home, away, blocks):
        final = low(reduce(home, away))
        both = jnp.stack([final[:2], swap(final[2:], "c")])
        both = jnp.stack([both[:, 0], swap(both[:, 1], "p")])
        columns = both.shape[-1] * 8
        (out,) = call(
            partial(lay_kernel, blocks),
            [like((part, columns), f32)],
            [],
            0,
            ids,
            both,
            swap(both, "x"),
            memory="svv",
        )
        return out

    joint_own_grad = hand(joint_home, joint_away, joint_blocks)
    up_own_grad = hand(up_home, up_away, up_blocks)
    down_own = low(reduce(down_home, down_away))
    down_own = wide(join(down_own, swap(down_own, "x"), x))
    output_part = lax.ppermute(output_grad, cross, turn_over).reshape(2, part, D)
    output_own = wide(take(output_part, c)) + wide(swap(take(output_part, 1 - c), "c"))
    output_own = low(output_own)
    output_own = wide(output_own) + wide(swap(output_own, "x"))

    own_normed = norm_of(tokens)
    centre = own_values - jnp.mean(own_values, axis=-1, keepdims=True)
    factor = lax.rsqrt(jnp.mean(centre * centre, axis=-1, keepdims=True) + EPSILON)
    grad_tokens = wide(cotangent) + factor * (
        pulled
        - jnp.mean(pulled, axis=-1, keepdims=True)
        - own_normed * jnp.mean(pulled * own_normed, axis=-1, keepdims=True)
    )
    pieces = [own_sums[i * part : (i + 1) * part] for i in range(5)]
    return (
        result,
        grad_tokens,
        pieces[0],
        pieces[1],
        joint_own_grad,
        own_sums[5 * part : 5 * part + joint_own],
        output_own,
        pieces[4],
        pieces[2],
        pieces[3],
        up_own_grad,
        own_sums[5 * part + joint_own :],
        down_own,
        pieces[4],
    )


def solution(mesh):
    if mesh.shape["rep"] == 2 and mesh.shape["shard"] * HEAD == D:
        work, body = Mesh(mesh.devices.reshape(2, 2, 2, 2, 2), ("x", *GROUP)), grouped
        group, every = GROUP, ("x", *GROUP)
    else:
        work, body = mesh, local
        group, every = "shard", ("rep", "shard")
    row, vec, mat = P(every, None), P(group), P(group, None)
    return jax.shard_map(
        body,
        mesh=work,
        in_specs=(row, row, P(), P(), vec, vec, mat, vec, mat, vec, vec, vec, mat, vec, mat, vec),
        out_specs=(row, row, vec, vec, mat, vec, mat, vec, vec, vec, mat, vec, mat, vec),
        check_vma=False,
    )
```

```python
from functools import partial

import jax
import jax.numpy as jnp
from jax import lax
from jax.experimental import pallas as pl
from jax.experimental.pallas import tpu as pltpu
from jax.sharding import Mesh, PartitionSpec as P

D = 1024
HEADS = 16
HEAD = 64
ROT = 16


EPSILON = 1e-05


def layout(lengths, owners, device, row_count):
    owned = owners == device
    own_lengths = jnp.where(owned, lengths, 0)
    end_points = jnp.cumsum(own_lengths, dtype=jnp.int32)
    filled = jnp.sum(own_lengths, dtype=jnp.int32)
    places = jnp.arange(row_count, dtype=jnp.int32)
    passed = end_points[None, :] <= places[:, None]
    before_count = jnp.sum(passed.astype(jnp.int32), axis=1, dtype=jnp.int32)
    seq_start = jnp.max(jnp.where(passed, end_points[None, :], 0), axis=1)
    filled_row = places < filled
    seq_total = lengths.shape[0]
    segment = jnp.where(filled_row, before_count, seq_total + places)
    position = jnp.where(filled_row, places - seq_start, 0)
    return (segment, position)


def rotate(vectors, position, direction):
    half_rot = ROT // 2
    frequency = 10000.0 ** (-jnp.arange(half_rot, dtype=jnp.float32) / half_rot)
    angles = position.astype(jnp.float32)[:, None] * frequency[None, :]
    cosine = jnp.cos(angles)[:, None, :]
    sine_part = direction * jnp.sin(angles)[:, None, :]
    lead_part = vectors[..., :half_rot]
    trail_part = vectors[..., half_rot:ROT]
    turned_lead = lead_part * cosine - trail_part * sine_part
    turned_trail = trail_part * cosine + lead_part * sine_part
    return jnp.concatenate([turned_lead, turned_trail, vectors[..., ROT:]], axis=-1)


def normalize(values, gain, shift):
    centre = values - jnp.mean(values, axis=-1, keepdims=True)
    normed = centre * lax.rsqrt(jnp.mean(centre * centre, axis=-1, keepdims=True) + EPSILON)
    return (normed, normed * gain + shift)


def norm_back(grad_hidden, normed, gain, values):
    gain_grad = jnp.sum(grad_hidden * normed, axis=0)
    shift_grad = jnp.sum(grad_hidden, axis=0)
    grad_normed = grad_hidden * gain
    centre = values - jnp.mean(values, axis=-1, keepdims=True)
    factor = lax.rsqrt(jnp.mean(centre * centre, axis=-1, keepdims=True) + EPSILON)
    grad_values = factor * (
        grad_normed
        - jnp.mean(grad_normed, axis=-1, keepdims=True)
        - normed * jnp.mean(grad_normed * normed, axis=-1, keepdims=True)
    )
    return (gain_grad, shift_grad, grad_values)


def contract_rows(left, right):
    return lax.dot_general(
        left, right, (((0,), (0,)), ((), ())), preferred_element_type=jnp.float32
    )


def across(left, right):
    return lax.dot_general(
        left, right, (((1,), (1,)), ((), ())), preferred_element_type=jnp.float32
    )


def local(
    tokens,
    cotangent,
    lengths,
    owners,
    first_gain,
    first_bias,
    joint_weight,
    joint_bias,
    output_weight,
    output_bias,
    second_gain,
    second_bias,
    up_weight,
    up_bias,
    down_weight,
    down_bias,
):
    row_count = tokens.shape[0]
    score_scale = HEAD ** (-0.5)
    device = lax.axis_index(("rep", "shard"))
    segment, position = layout(lengths, owners, device, row_count)
    places = jnp.arange(row_count, dtype=jnp.int32)
    allowed = (segment[:, None] == segment[None, :]) & (places[None, :] <= places[:, None])
    gain_one, shift_one, joint_full, joint_offset, output_full, output_offset = (
        lax.all_gather(first_gain, "shard", axis=0, tiled=True),
        lax.all_gather(first_bias, "shard", axis=0, tiled=True),
        lax.all_gather(joint_weight, "shard", axis=0, tiled=True),
        lax.all_gather(joint_bias, "shard", axis=0, tiled=True),
        lax.all_gather(output_weight, "shard", axis=0, tiled=True),
        lax.all_gather(output_bias, "shard", axis=0, tiled=True),
    )
    gain_two, shift_two, up_full, up_offset, down_full, down_offset = (
        lax.all_gather(second_gain, "shard", axis=0, tiled=True),
        lax.all_gather(second_bias, "shard", axis=0, tiled=True),
        lax.all_gather(up_weight, "shard", axis=0, tiled=True),
        lax.all_gather(up_bias, "shard", axis=0, tiled=True),
        lax.all_gather(down_weight, "shard", axis=0, tiled=True),
        lax.all_gather(down_bias, "shard", axis=0, tiled=True),
    )
    values = tokens.astype(jnp.float32)
    normed_one, hidden_one = normalize(
        values, gain_one.astype(jnp.float32), shift_one.astype(jnp.float32)
    )
    input_one = hidden_one.astype(jnp.bfloat16)
    projected = jnp.dot(
        input_one, joint_full, preferred_element_type=jnp.float32
    ) + joint_offset.astype(jnp.float32)
    heads_view = projected.reshape(row_count, 3, HEADS, HEAD)
    query_low = rotate(heads_view[:, 0], position, 1.0).astype(jnp.bfloat16)
    keys_low = rotate(heads_view[:, 1], position, 1.0).astype(jnp.bfloat16)
    value_low = heads_view[:, 2].astype(jnp.bfloat16)
    masked = jnp.where(
        allowed[None],
        jnp.einsum("qhd,khd->hqk", query_low, keys_low, preferred_element_type=jnp.float32)
        * score_scale,
        -1e30,
    )
    row_peak = jnp.max(masked, axis=-1, keepdims=True)
    logsum = row_peak + jnp.log(jnp.sum(jnp.exp(masked - row_peak), axis=-1, keepdims=True))
    probs_low = jnp.exp(masked - logsum).astype(jnp.bfloat16)
    mixed_low = (
        jnp.einsum("hqk,khd->qhd", probs_low, value_low, preferred_element_type=jnp.float32)
        .reshape(row_count, D)
        .astype(jnp.bfloat16)
    )
    attention = jnp.dot(
        mixed_low, output_full, preferred_element_type=jnp.float32
    ) + output_offset.astype(jnp.float32)
    normed_two, hidden_two = normalize(
        values, gain_two.astype(jnp.float32), shift_two.astype(jnp.float32)
    )
    input_two = hidden_two.astype(jnp.bfloat16)
    before = jnp.dot(input_two, up_full, preferred_element_type=jnp.float32) + up_offset.astype(
        jnp.float32
    )
    active_low = jax.nn.gelu(before, approximate=False).astype(jnp.bfloat16)
    feed_out = jnp.dot(
        active_low, down_full, preferred_element_type=jnp.float32
    ) + down_offset.astype(jnp.float32)
    result = (values + attention + feed_out).astype(jnp.bfloat16)
    back_one = (
        lax.all_gather(first_gain, "shard", axis=0, tiled=True),
        lax.all_gather(joint_weight, "shard", axis=0, tiled=True),
        lax.all_gather(output_weight, "shard", axis=0, tiled=True),
    )
    back_two = (
        lax.all_gather(second_gain, "shard", axis=0, tiled=True),
        lax.all_gather(up_weight, "shard", axis=0, tiled=True),
        lax.all_gather(down_weight, "shard", axis=0, tiled=True),
    )
    gain_back_one, joint_back, output_back = back_one
    gain_back_two, up_back, down_back = back_two
    grad_out = cotangent.astype(jnp.float32)
    down_weight_grad = contract_rows(active_low, cotangent)
    down_bias_grad = jnp.sum(grad_out, axis=0)
    grad_active = across(cotangent, down_back)
    gelu_exact = partial(jax.nn.gelu, approximate=False)
    grad_before = jax.vjp(gelu_exact, before)[1](grad_active)[0].astype(jnp.bfloat16)
    up_weight_grad = contract_rows(input_two, grad_before)
    up_bias_grad = jnp.sum(grad_before.astype(jnp.float32), axis=0)
    gain_two_grad, shift_two_grad, grad_from_two = norm_back(
        across(grad_before, up_back), normed_two, gain_back_two.astype(jnp.float32), values
    )
    output_weight_grad = contract_rows(mixed_low, cotangent)
    grad_mixed = across(cotangent, output_back).astype(jnp.bfloat16).reshape(row_count, HEADS, HEAD)
    masked_again = jnp.where(
        allowed[None],
        jnp.einsum("qhd,khd->hqk", query_low, keys_low, preferred_element_type=jnp.float32)
        * score_scale,
        -1e30,
    )
    prob_back = jnp.exp(masked_again - logsum)
    prob_back_low = prob_back.astype(jnp.bfloat16)
    grad_probs = jnp.einsum(
        "qhd,khd->hqk", grad_mixed, value_low, preferred_element_type=jnp.float32
    )
    grad_value = jnp.einsum(
        "hqk,qhd->khd", prob_back_low, grad_mixed, preferred_element_type=jnp.float32
    )
    spread = jnp.sum(grad_probs * prob_back, axis=-1, keepdims=True)
    grad_scores = (prob_back * (grad_probs - spread)).astype(jnp.bfloat16)
    grad_query = rotate(
        jnp.einsum("hqk,khd->qhd", grad_scores, keys_low, preferred_element_type=jnp.float32)
        * score_scale,
        position,
        -1.0,
    )
    grad_keys = rotate(
        jnp.einsum("hqk,qhd->khd", grad_scores, query_low, preferred_element_type=jnp.float32)
        * score_scale,
        position,
        -1.0,
    )
    grad_joint = (
        jnp.stack([grad_query, grad_keys, grad_value], axis=1)
        .reshape(row_count, 3 * D)
        .astype(jnp.bfloat16)
    )
    joint_weight_grad = contract_rows(input_one, grad_joint)
    joint_bias_grad = jnp.sum(grad_joint.astype(jnp.float32), axis=0)
    gain_one_grad, shift_one_grad, grad_from_one = norm_back(
        across(grad_joint, joint_back), normed_one, gain_back_one.astype(jnp.float32), values
    )
    grad_tokens = grad_out + grad_from_one + grad_from_two
    group_shares = (
        lax.psum_scatter(gain_one_grad, "shard", scatter_dimension=0, tiled=True),
        lax.psum_scatter(shift_one_grad, "shard", scatter_dimension=0, tiled=True),
        lax.psum_scatter(joint_weight_grad, "shard", scatter_dimension=0, tiled=True),
        lax.psum_scatter(joint_bias_grad, "shard", scatter_dimension=0, tiled=True),
        lax.psum_scatter(output_weight_grad, "shard", scatter_dimension=0, tiled=True),
        lax.psum_scatter(down_bias_grad, "shard", scatter_dimension=0, tiled=True),
        lax.psum_scatter(gain_two_grad, "shard", scatter_dimension=0, tiled=True),
        lax.psum_scatter(shift_two_grad, "shard", scatter_dimension=0, tiled=True),
        lax.psum_scatter(up_weight_grad, "shard", scatter_dimension=0, tiled=True),
        lax.psum_scatter(up_bias_grad, "shard", scatter_dimension=0, tiled=True),
        lax.psum_scatter(down_weight_grad, "shard", scatter_dimension=0, tiled=True),
        lax.psum_scatter(down_bias_grad, "shard", scatter_dimension=0, tiled=True),
    )
    (
        share_gain_one,
        share_shift_one,
        share_joint_weight,
        share_joint_bias,
        share_output_weight,
        share_output_bias,
        share_gain_two,
        share_shift_two,
        share_up_weight,
        share_up_bias,
        share_down_weight,
        share_down_bias,
    ) = group_shares
    owned = lax.psum(
        (
            share_gain_one,
            share_shift_one,
            share_joint_weight,
            share_joint_bias,
            share_output_weight,
            share_output_bias,
            share_gain_two,
            share_shift_two,
            share_up_weight,
            share_up_bias,
            share_down_weight,
            share_down_bias,
        ),
        "rep",
    )
    return (
        result,
        grad_tokens,
        owned[0],
        owned[1],
        owned[2],
        owned[3],
        owned[4],
        owned[5],
        owned[6],
        owned[7],
        owned[8],
        owned[9],
        owned[10],
        owned[11],
    )


PAIR = [(0, 1), (1, 0)]
BLOCKS = 8
NEAR, FAR = (0, 4, 1, 5), (2, 6, 3, 7)
LANE = 128
GROUP = ("o", "p", "q", "c")
VMEM_BYTES = 28 * 1024 * 1024


def swap(values, *axes):
    if len(axes) == 1:
        return lax.ppermute(values, axes[0], PAIR)
    return lax.ppermute(values, axes, [(i, 3 - i) for i in range(4)])


def join(own, other, at, axis=0):
    first = at == 0
    return jnp.concatenate(
        [jnp.where(first, own, other), jnp.where(first, other, own)], axis=axis
    )


def pin(*values):
    return lax.optimization_barrier(values)


def take(values, at, axis=0):
    return lax.dynamic_index_in_dim(values, at, axis, keepdims=False)


def low(values):
    return values.astype(jnp.bfloat16)


def wide(values):
    return values.astype(jnp.float32)


def times(left, right):
    return jnp.dot(left, right, preferred_element_type=jnp.float32)


def places_of(ids_ref):
    return tuple(ids_ref[i] for i in range(5))


def call(kernel, outs, scratch, micros, *operands, memory):
    whole = pl.BlockSpec(memory_space=pltpu.VMEM)
    specs = {
        "s": pl.BlockSpec(memory_space=pltpu.SMEM),
        "v": whole,
        "h": pl.BlockSpec(memory_space=pl.ANY),
    }
    size = sum(leaf.size * leaf.dtype.itemsize for leaf in (*operands, *outs))
    return pl.pallas_call(
        kernel,
        out_shape=tuple(outs),
        in_specs=[specs[kind] for kind in memory],
        out_specs=tuple(whole for _ in outs),
        scratch_shapes=scratch,
        compiler_params=pltpu.CompilerParams(vmem_limit_bytes=VMEM_BYTES),
        cost_estimate=pl.CostEstimate(
            flops=int(micros * 1.15e9), bytes_accessed=size, transcendentals=0
        ),
    )(*operands)


def fetch(pairs, sems):
    copies = [
        pltpu.make_async_copy(source, target, sems.at[i])
        for i, (source, target) in enumerate(pairs)
    ]
    for copy in copies:
        copy.start()
    return copies


def finish(copies):
    for copy in copies:
        copy.wait()


def row_pairs(sources, target):
    return [
        (source.at[k], target.at[pl.ds(block * source.shape[1], source.shape[1])])
        for source, blocks in sources
        for k, block in enumerate(blocks)
    ]


def sheet_pairs(pieces, target, places):
    x, o, p, q, c = places
    pairs = []
    for index, piece in enumerate(pieces):
        jo, jq = index // 2, index % 2
        rows = piece.shape[1]
        for k in range(4):
            jc, jp = k // 2, k % 2
            at = ((((o ^ jo) * 2 + (p ^ jp)) * 2 + (q ^ jq)) * 2 + (c ^ jc)) * rows
            pairs.append((piece.at[k], target.at[pl.ds(pl.multiple_of(at, rows), rows)]))
    return pairs


def tall_pairs(pieces, target, places):
    x, o, p, q, c = places
    pairs = []
    for index, piece in enumerate(pieces):
        jo, jq = index // 2, index % 2
        rows = piece.shape[0]
        at = ((o ^ jo) * 2 + (q ^ jq)) * rows
        pairs.append((piece, target.at[pl.ds(pl.multiple_of(at, rows), rows)]))
    return pairs


def norm_of(tokens):
    values = wide(tokens)
    centre = values - jnp.mean(values, axis=-1, keepdims=True)
    return centre * lax.rsqrt(jnp.mean(centre * centre, axis=-1, keepdims=True) + EPSILON)


def fold(values):
    rows, columns = values.shape
    return jnp.sum(values.reshape(rows // 8, 8, columns), axis=0)


def block_rows(block, cap):
    return pl.ds(pl.multiple_of(block * cap, 16), cap)


def cut_kernel(ids, joint, up, down, keep, send, half):
    x, o, p, q, c = places_of(ids)
    parts = joint.shape[1] // D

    def block(ref, index):
        return ref[:, pl.ds(pl.multiple_of(index * LANE, LANE), LANE)]

    for jp, target in ((0, keep), (1, send)):
        for jc in (0, 1):
            pp, cc = p ^ jp, c ^ jc
            for part in range(parts):
                target[jc, :, part * LANE : (part + 1) * LANE] = block(
                    joint, part * 8 + x * 4 + pp * 2 + cc
                )
            for k in range(4):
                oo, qq = k // 2, k % 2
                at = (parts + k) * LANE
                target[jc, :, at : at + LANE] = block(
                    up, (((oo * 2 + pp) * 2 + qq) * 2 + cc) * 2 + x
                )
    rows = half.shape[0]
    half[...] = down[pl.ds(pl.multiple_of(x * rows, rows), rows), :]


def turner(cap):
    lane = lax.broadcasted_iota(jnp.int32, (cap, LANE), 1)
    lead = lane % HEAD < ROT // 2

    def turn(values, cos_part, sin_part):
        other = jnp.where(
            lead, pltpu.roll(values, LANE - ROT // 2, 1), pltpu.roll(values, ROT // 2, 1)
        )
        return values * cos_part + other * sin_part

    return turn, (lane < HEAD, lane >= HEAD)


def token_pairs(sources, target):
    return row_pairs(zip(sources, ((0, 1), (2, 3), (4, 5), (6, 7))), target)


def both_ways(step, near_out, far_out, cap):
    def first(block, carry):
        near_out[block_rows(block, cap), :] = step(block // 2 * 4 + block % 2)
        return carry

    def second(block, carry):
        far_out[block_rows(block, cap), :] = low(step(block // 2 * 4 + block % 2 + 2))
        return carry

    lax.fori_loop(0, BLOCKS // 2, first, 0)
    lax.fori_loop(0, BLOCKS // 2, second, 0)


def attention_kernel(
    ids,
    block_0,
    block_1,
    block_2,
    block_3,
    near,
    far,
    sheet_0,
    sheet_1,
    sheet_2,
    sheet_3,
    output_weight,
    fed,
    cosine,
    sine,
    position,
    gain,
    shift,
    offset,
    near_out,
    far_out,
    grad_ref,
    home_0,
    home_1,
    away,
    output_grad,
    grad_sum,
    tokens,
    cotangent,
    joint,
    inputs,
    mixed_all,
    total,
    sems,
):
    cap = block_0.shape[1]
    finish(
        fetch(
            sheet_pairs((sheet_0, sheet_1, sheet_2, sheet_3), joint, places_of(ids))
            + token_pairs((block_0, block_1, block_2, block_3), tokens)
            + row_pairs(((near, NEAR), (far, FAR)), cotangent),
            sems,
        )
    )
    total[...] = jnp.zeros_like(total)
    turn, mine = turner(cap)
    down = lax.broadcasted_iota(jnp.int32, (cap, cap), 0)
    along = lax.broadcasted_iota(jnp.int32, (cap, cap), 1)
    scale = HEAD ** (-0.5)

    def step(block):
        rows = block_rows(block, cap)
        input_low = low(norm_of(tokens[rows, :]) * gain[...] + shift[...])
        inputs[rows, :] = input_low
        projected = times(input_low, joint[...]) + offset[...]
        cos_part, sin_part = cosine[rows, :], sine[rows, :]
        query = low(turn(projected[:, :LANE], cos_part, sin_part))
        keys = low(turn(projected[:, LANE : 2 * LANE], cos_part, sin_part))
        value = low(projected[:, 2 * LANE :])
        grad_mixed = low(across(cotangent[rows, :], output_weight[...]))
        allowed = (along <= down) & (along >= down - position[rows, :])
        found = []
        for own in mine:
            query_own = jnp.where(own, query, jnp.zeros_like(query))
            grad_own = jnp.where(own, grad_mixed, jnp.zeros_like(grad_mixed))
            scores = jnp.where(allowed, across(query_own, keys) * scale, -1e30)
            raised = jnp.exp(scores - jnp.max(scores, axis=-1, keepdims=True))
            probs = raised / jnp.sum(raised, axis=-1, keepdims=True)
            probs_low = low(probs)
            grad_probs = across(grad_own, value)
            spread = jnp.sum(grad_probs * probs, axis=-1, keepdims=True)
            grad_scores = low(probs * (grad_probs - spread))
            found.append(
                (
                    times(probs_low, value),
                    times(grad_scores, keys) * scale,
                    contract_rows(grad_scores, query) * scale,
                    contract_rows(probs_low, grad_mixed),
                )
            )
        mixed, grad_query, grad_keys, grad_value = (
            jnp.where(mine[0], first, second) for first, second in zip(*found)
        )
        mixed = low(mixed)
        mixed_all[rows, :] = mixed
        grad_joint = low(
            jnp.concatenate(
                [
                    turn(grad_query, cos_part, -sin_part),
                    turn(grad_keys, cos_part, -sin_part),
                    grad_value,
                ],
                axis=1,
            )
        )
        grad_ref[rows, :] = grad_joint
        total[...] += fold(wide(grad_joint))
        return times(mixed, output_weight[...]) + wide(fed[rows, :])

    both_ways(step, near_out, far_out, cap)
    grad_sum[...] = jnp.sum(total[...], axis=0, keepdims=True)
    output_grad[...] = low(contract_rows(mixed_all[...], cotangent[...]))
    half = away.shape[0] // 2
    here = home_0, away.at[pl.ds(0, half)]
    there = home_1, away.at[pl.ds(half, half)]
    sheet_grads(inputs, grad_ref, here, there, 0, places_of(ids))


def for_place(at, here, there, store):
    pl.when(at)(lambda: store(*here))
    pl.when(jnp.logical_not(at))(lambda: store(*there))


def sheet_grads(inputs, grads, here, there, base, places):
    x, o, p, q, c = places
    columns = grads.shape[1]
    rows = D // 16
    for oo in (0, 1):
        found = contract_rows(inputs[:, oo * D // 2 : (oo + 1) * D // 2], grads[...])
        found = low(found).reshape(2, 2, 2, rows, columns)

        def store(home, away, found=found):
            for pp in (0, 1):
                for cc in (0, 1):
                    down = pl.ds(pl.multiple_of(base + (p ^ pp) * rows, rows), rows)
                    along = pl.ds(pl.multiple_of((c ^ cc) * columns, LANE), columns)
                    home[down, along] = jnp.where(q == 0, found[pp, 0, cc], found[pp, 1, cc])
                    away[down, along] = jnp.where(q == 0, found[pp, 1, cc], found[pp, 0, cc])

        for_place(o == oo, here, there, store)


def feed_kernel(
    ids,
    block_0,
    block_1,
    block_2,
    block_3,
    near,
    far,
    sheet_0,
    sheet_1,
    sheet_2,
    sheet_3,
    tall_0,
    tall_1,
    tall_2,
    tall_3,
    gain,
    shift,
    offset,
    fed,
    grad_all,
    home_0,
    home_1,
    away_0,
    away_1,
    grad_sum,
    tokens,
    cotangent,
    up,
    down,
    inputs,
    active_all,
    total,
    sems,
):
    places = places_of(ids)
    x, o, p, q, c = places
    cap = block_0.shape[1]
    finish(
        fetch(
            sheet_pairs((sheet_0, sheet_1, sheet_2, sheet_3), up, places)
            + token_pairs((block_0, block_1, block_2, block_3), tokens)
            + row_pairs(((near, NEAR), (far, FAR)), cotangent)
            + tall_pairs((tall_0, tall_1, tall_2, tall_3), down, places),
            sems,
        )
    )
    total[...] = jnp.zeros_like(total)

    def step(block, carry):
        rows = block_rows(block, cap)
        input_low = low(norm_of(tokens[rows, :]) * gain[...] + shift[...])
        inputs[rows, :] = input_low
        before = times(input_low, up[...]) + offset[...]
        slope = 0.5 + 0.5 * lax.erf(before * 0.5**0.5)
        active = low(before * slope)
        active_all[rows, :] = active
        slope = slope + before * jnp.exp(-0.5 * before * before) * (0.5 / jnp.pi) ** 0.5
        grad_before = low(across(cotangent[rows, :], down[...]) * slope)
        grad_all[rows, :] = grad_before
        total[...] += fold(wide(grad_before))
        fed[rows, :] = low(times(active, down[...]))
        return carry

    lax.fori_loop(0, BLOCKS, step, 0)
    grad_sum[...] = jnp.sum(total[...], axis=0, keepdims=True)
    unit = home_0.shape[0] // 2
    here, there = (home_0, away_0), (home_1, away_1)
    for oo in (0, 1):
        found = low(contract_rows(active_all[:, oo * 2 * unit : (oo + 1) * 2 * unit], cotangent[...]))

        def store(home, away, found=found):
            home[:unit, :] = jnp.where(q == 0, found[:unit], found[unit:])
            away[:unit, :] = jnp.where(q == 0, found[unit:], found[:unit])

        for_place(o == oo, here, there, store)
    sheet_grads(inputs, grad_all, here, there, unit, places)


def pull_kernel(
    ids,
    block_0,
    block_1,
    block_2,
    block_3,
    join_0,
    join_1,
    join_2,
    join_3,
    sheet_0,
    sheet_1,
    sheet_2,
    sheet_3,
    grad_joint,
    grad_before,
    gain_one,
    gain_two,
    near_out,
    far_out,
    sums,
    tokens,
    joint,
    up,
    totals,
    sems,
):
    places = places_of(ids)
    cap = block_0.shape[1]
    finish(
        fetch(
            token_pairs((block_0, block_1, block_2, block_3), tokens)
            + sheet_pairs((join_0, join_1, join_2, join_3), joint, places)
            + sheet_pairs((sheet_0, sheet_1, sheet_2, sheet_3), up, places),
            sems,
        )
    )
    totals[...] = jnp.zeros_like(totals)

    def step(block):
        rows = block_rows(block, cap)
        normed = norm_of(tokens[rows, :])
        grad_first = across(grad_joint[rows, :], joint[...])
        grad_second = across(grad_before[rows, :], up[...])
        totals[0] += fold(grad_first * normed)
        totals[1] += fold(grad_first)
        totals[2] += fold(grad_second * normed)
        totals[3] += fold(grad_second)
        return grad_first * gain_one[...] + grad_second * gain_two[...]

    both_ways(step, near_out, far_out, cap)
    sums[...] = jnp.sum(totals[...], axis=1)


def lay_kernel(ids, own, other, joint, up):
    x, o, p, q, c = places_of(ids)
    parts = joint.shape[1] // D
    for xx, source in ((0, own), (1, other)):
        for pp in (0, 1):
            for cc in (0, 1):
                values = wide(source[pp, cc])
                at_x, at_p, at_c = x ^ xx, p ^ pp, c ^ cc
                blocks = [(joint, part * 8 + at_x * 4 + at_p * 2 + at_c) for part in range(parts)]
                blocks += [
                    (up, (((k // 2 * 2 + at_p) * 2 + k % 2) * 2 + at_c) * 2 + at_x) for k in range(4)
                ]
                for k, (out, at) in enumerate(blocks):
                    out[:, pl.ds(pl.multiple_of(at * LANE, LANE), LANE)] = values[
                        :, k * LANE : (k + 1) * LANE
                    ]


def lane_sum(near, came):
    lane = near + wide(came)
    rows = lane.shape[0] // 4
    return lane[:rows], *(low(lane[i * rows : (i + 1) * rows]) for i in (1, 2, 3))


def total(*parts):
    found = wide(parts[0])
    for part in parts[1:]:
        found += wide(part)
    return found


def grouped(
    tokens,
    cotangent,
    lengths,
    owners,
    first_gain,
    first_bias,
    joint_weight,
    joint_bias,
    output_weight,
    output_bias,
    second_gain,
    second_bias,
    up_weight,
    up_bias,
    down_weight,
    down_bias,
):
    x, o, p, q, c = (lax.axis_index(name) for name in ("x", "o", "p", "q", "c"))
    ids = jnp.stack([x, o, p, q, c]).astype(jnp.int32)
    cap = tokens.shape[0]
    rows = BLOCKS * cap
    part = joint_weight.shape[0]
    hidden = up_weight.shape[1] // 8
    unit = hidden // 4
    bf, f32 = jnp.bfloat16, jnp.float32

    def like(shape, kind):
        return jax.ShapeDtypeStruct(shape, kind)

    keep, send, down_half = call(
        cut_kernel,
        [
            like((2, part, 3 * LANE + hidden), bf),
            like((2, part, 3 * LANE + hidden), bf),
            like((unit, D), bf),
        ],
        [],
        0,
        ids,
        joint_weight,
        up_weight,
        down_weight,
        memory="svvv",
    )
    came = swap(send, "p")
    along_p = swap(pin(tokens, send)[0], "p")
    along_x = swap(tokens, "x")
    down_other = swap(down_half, "o")

    turned = jnp.concatenate(
        [keep[:1], came[:1], swap(jnp.concatenate([keep[1:], came[1:]], axis=0), "c")], axis=0
    )

    tokens_0 = jnp.stack([tokens, along_x])
    tokens_2 = jnp.stack([along_p, swap(along_p, "x")])

    joint_own, up_own = turned[:, :, : 3 * LANE], turned[:, :, 3 * LANE :]
    up_other, up_side = swap(up_own, "o"), swap(up_own, "q")
    joint_other = swap(pin(joint_own, up_other)[0], "o")

    vectors = (first_gain, first_bias, second_gain, second_bias, output_bias, down_bias, joint_bias, up_bias)
    small = jnp.concatenate(pin(*vectors, send)[:-1])[None]
    for name, at in (("c", c), ("p", p)):
        small = join(small, swap(small, name), at)
    small = pin(small, up_other)[0]
    for name, at in (("q", q), ("o", o)):
        small = join(small, swap(small, name), at)
    small = small.reshape(2, 2, 2, 2, -1).transpose(0, 2, 1, 3, 4).reshape(16, -1)

    def vector(start, size):
        return wide(small[:, start : start + size]).reshape(1, -1)

    gain_one, shift_one, gain_two, shift_two, output_offset, down_offset = (
        vector(i * part, part) for i in range(6)
    )
    joint_size = joint_bias.shape[0]
    joint_offset = vector(6 * part, joint_size)
    up_offset = vector(6 * part + joint_size, up_bias.shape[0])
    joint_offset = take(joint_offset.reshape(3, 8, LANE), x * 4 + p * 2 + c, 1).reshape(1, 3 * LANE)
    up_offset = take(take(take(up_offset.reshape(2, 2, 2, 2, 2, unit), x, 4), c, 3), p, 1)
    up_offset = up_offset.reshape(1, hidden)

    turn_over = [
        (((a * 2 + b) * 2 + e) * 2 + f, ((b * 2 + a) * 2 + f) * 2 + e)
        for a in (0, 1)
        for b in (0, 1)
        for e in (0, 1)
        for f in (0, 1)
    ]
    cross = ("x", "o", "q", "c")
    output_pair = join(output_weight, swap(output_weight, "c"), c)

    devices = jnp.stack(
        [
            ((((x ^ xx) * 2 + o) * 2 + (p ^ pp)) * 2 + q) * 2 + (c ^ cc)
            for pp in (0, 1)
            for cc in (0, 1)
            for xx in (0, 1)
        ]
    )
    position = jax.vmap(lambda device: layout(lengths, owners, device, cap)[1])(devices)
    position = position.reshape(rows, 1)
    place = jnp.arange(LANE) % HEAD
    half_rot = ROT // 2
    frequency = 10000.0 ** (-jnp.arange(half_rot, dtype=f32) / half_rot)
    angles = position.astype(f32) * jnp.tile(frequency, LANE // half_rot)[None, :]
    cosine = jnp.where(place < ROT, jnp.cos(angles), 1.0)
    sine = jnp.sin(angles)
    sine = jnp.where(place < half_rot, -sine, jnp.where(place < ROT, sine, 0.0))

    copies = pltpu.SemaphoreType.DMA

    tokens_1, tokens_3 = swap(tokens_0, "c"), swap(tokens_2, "c")
    grad_along_p = swap(pin(cotangent, along_p)[0], "p")
    grad_pair = jnp.stack([cotangent, grad_along_p])
    near_grad = jnp.concatenate([grad_pair, swap(grad_pair, "x")])
    far_grad = swap(near_grad, "c")
    up_sheets = up_own, up_side, up_other, swap(up_other, "q")
    down_far = swap(jnp.stack([down_half, down_other]), "q")
    down_talls = down_half, down_far[0], down_other, down_far[1]
    joint_own, joint_other, output_pair, tokens_0 = pin(joint_own, joint_other, output_pair, tokens_0)
    joint_side, joint_corner = swap(joint_own, "q"), swap(joint_other, "q")
    output_pair = lax.ppermute(output_pair, cross, turn_over)
    tall = (rows, D)
    found = call(
        feed_kernel,
        [
            like(tall, bf),
            like((rows, hidden), bf),
            *(like((2 * unit, D), bf) for _ in range(4)),
            like((1, hidden), f32),
        ],
        [
            pltpu.VMEM(tall, bf),
            pltpu.VMEM(tall, bf),
            pltpu.VMEM((D, hidden), bf),
            pltpu.VMEM((hidden, D), bf),
            pltpu.VMEM(tall, bf),
            pltpu.VMEM((rows, hidden), bf),
            pltpu.VMEM((8, hidden), f32),
            copies((36,)),
        ],
        20,
        ids,
        tokens_0,
        tokens_1,
        tokens_2,
        tokens_3,
        near_grad,
        far_grad,
        *up_sheets,
        *down_talls,
        gain_two,
        shift_two,
        up_offset,
        memory="shhhhhhhhhhhhhhvvv",
    )
    joint_side, joint_corner, output_pair, *found = pin(joint_side, joint_corner, output_pair, *found)
    joint_sheets = joint_own, joint_side, joint_other, joint_corner
    fed, grad_before, up_home_0, up_home_1, up_away_0, up_away_1, up_sum = found
    up_away_1 = swap(up_away_1, "q")

    found = call(
        attention_kernel,
        [
            like((rows // 2, D), f32),
            like((rows // 2, D), bf),
            like((rows, 3 * LANE), bf),
            like((2 * part, 6 * LANE), bf),
            like((2 * part, 6 * LANE), bf),
            like((4 * part, 6 * LANE), bf),
            like((LANE, D), bf),
            like((1, 3 * LANE), f32),
        ],
        [
            pltpu.VMEM(tall, bf),
            pltpu.VMEM(tall, bf),
            pltpu.VMEM((D, 3 * LANE), bf),
            pltpu.VMEM(tall, bf),
            pltpu.VMEM((rows, LANE), bf),
            pltpu.VMEM((8, 3 * LANE), f32),
            copies((32,)),
        ],
        22,
        ids,
        tokens_0,
        tokens_1,
        tokens_2,
        tokens_3,
        near_grad,
        far_grad,
        *joint_sheets,
        output_pair,
        fed,
        cosine,
        sine,
        position,
        gain_one,
        shift_one,
        joint_offset,
        memory="shhhhhhhhhhvvvvvvvv",
    )
    up_away_1, up_away_0, *found = pin(up_away_1, up_away_0, *found)
    near_part, far_part, grad_joint, joint_home_0, joint_home_1, joint_away, output_grad, joint_sum = found

    def lane_sum(near, came, block):
        at = slice(block * cap, (block + 1) * cap)
        return near[at] + wide(came[at])

    up_sent = swap(low(total(up_home_1, up_away_1)), "o")
    joint_away, up_away_0 = swap(joint_away, "q"), swap(up_away_0, "q")
    result_lane = near_part, swap(far_part, "c")
    result_sent, grad_joint = pin(
        low(jnp.concatenate([lane_sum(*result_lane, 1), lane_sum(*result_lane, 3)])), grad_joint
    )
    result_came = swap(result_sent, "x")
    output_part = lax.ppermute(output_grad, cross, turn_over)
    found = call(
        pull_kernel,
        [like((rows // 2, D), f32), like((rows // 2, D), bf), like((4, D), f32)],
        [
            pltpu.VMEM(tall, bf),
            pltpu.VMEM((D, 3 * LANE), bf),
            pltpu.VMEM((D, hidden), bf),
            pltpu.VMEM((4, 8, D), f32),
            copies((40,)),
        ],
        11,
        ids,
        tokens_0,
        tokens_1,
        tokens_2,
        tokens_3,
        *joint_sheets,
        *up_sheets,
        grad_joint,
        grad_before,
        gain_one,
        gain_two,
        memory="shhhhhhhhhhhhvvvv",
    )
    up_sent, up_away_0, joint_away, result_came, output_part, *found = pin(
        up_sent, up_away_0, joint_away, result_came, output_part, *found
    )
    near_part, far_part, norm_sums = found
    lane = near_part, swap(far_part, "c")
    joint_sent = swap(low(total(joint_home_1, joint_away[2 * part :])), "o")
    corner, side, up_sent, result_came = pin(
        low(lane_sum(*lane, 3)), low(lane_sum(*lane, 1)), up_sent, result_came
    )
    corner, side = swap(corner, "x"), swap(side, "x")
    result_kept = lane_sum(*result_lane, 0) + wide(result_came[:cap])
    result_came = swap(low(lane_sum(*result_lane, 2) + wide(result_came[cap:])), "p")
    far_side = swap(low(lane_sum(*lane, 2) + wide(corner)), "p")
    output_part = output_part.reshape(2, part, D)
    output_sent = swap(take(output_part, 1 - c), "c")
    output_own = low(total(take(output_part, c), output_sent))
    own_values = wide(tokens)
    result = low(own_values + total(result_kept, result_came) + output_offset + down_offset)
    output_own = total(output_own, swap(output_own, "x"))
    up_final = low(total(up_home_0, up_away_0, up_sent))
    joint_final = low(total(joint_home_0, joint_away[: 2 * part], joint_sent))
    down_own = wide(join(up_final[:unit], swap(up_final[:unit], "x"), x))

    def put(values, index, size, axis):
        hot = (jnp.arange(size) == index).reshape([size if i == axis else 1 for i in range(values.ndim + 1)])
        return jnp.where(hot, jnp.expand_dims(values, axis), 0.0)

    joint_sum = put(joint_sum.reshape(3, LANE), x * 4 + p * 2 + c, 8, 1)
    up_sum = put(put(put(up_sum.reshape(2, 2, unit), x, 2, 2), c, 2, 2), p, 2, 1)
    sums = jnp.concatenate(
        [
            *(norm_sums[i].reshape(-1, part) for i in range(4)),
            jnp.sum(wide(cotangent), axis=0).reshape(-1, part),
            joint_sum.reshape(-1, joint_size),
            up_sum.reshape(-1, up_bias.shape[0]),
        ],
        axis=1,
    )
    sums = sums + swap(sums, "c")
    sums = (sums + swap(sums, "x")) + (swap(sums, "p") + swap(sums, "x", "p"))
    sums, side, far_side = pin(sums, side, far_side)
    pulled = lane_sum(*lane, 0) + wide(side) + wide(far_side)
    sums = (sums + swap(sums, "o")) + (swap(sums, "q") + swap(sums, "o", "q"))
    own_sums = take(sums, ((o * 2 + p) * 2 + q) * 2 + c)

    final = jnp.concatenate(
        [
            joint_final.reshape(2, part, 2, 3 * LANE).transpose(2, 0, 1, 3),
            up_final[unit:].reshape(2, part, 2, hidden).transpose(2, 0, 1, 3),
        ],
        axis=3,
    )
    both = jnp.stack([final[0], swap(final[1], "c")])
    both = jnp.stack([both[:, 0], swap(both[:, 1], "p")])
    joint_own_grad, up_own_grad = call(
        lay_kernel,
        [like((part, 3 * D), f32), like((part, up_weight.shape[1]), f32)],
        [],
        1,
        ids,
        both,
        swap(both, "x"),
        memory="svv",
    )

    own_normed = norm_of(tokens)
    centre = own_values - jnp.mean(own_values, axis=-1, keepdims=True)
    factor = lax.rsqrt(jnp.mean(centre * centre, axis=-1, keepdims=True) + EPSILON)
    grad_tokens = wide(cotangent) + factor * (
        pulled
        - jnp.mean(pulled, axis=-1, keepdims=True)
        - own_normed * jnp.mean(pulled * own_normed, axis=-1, keepdims=True)
    )
    pieces = [own_sums[i * part : (i + 1) * part] for i in range(5)]
    return (
        result,
        grad_tokens,
        pieces[0],
        pieces[1],
        joint_own_grad,
        own_sums[5 * part : 5 * part + joint_size],
        output_own,
        pieces[4],
        pieces[2],
        pieces[3],
        up_own_grad,
        own_sums[5 * part + joint_size :],
        down_own,
        pieces[4],
    )


def solution(mesh):
    if mesh.shape["rep"] == 2 and mesh.shape["shard"] * HEAD == D:
        work, body = Mesh(mesh.devices.reshape(2, 2, 2, 2, 2), ("x", *GROUP)), grouped
        group, every = GROUP, ("x", *GROUP)
    else:
        work, body = mesh, local
        group, every = "shard", ("rep", "shard")
    row, vec, mat = P(every, None), P(group), P(group, None)
    return jax.shard_map(
        body,
        mesh=work,
        in_specs=(row, row, P(), P(), vec, vec, mat, vec, mat, vec, vec, vec, mat, vec, mat, vec),
        out_specs=(row, row, vec, vec, mat, vec, mat, vec, vec, vec, mat, vec, mat, vec),
        check_vma=False,
    )
```

```python
from functools import partial

import jax
import jax.numpy as jnp
from jax import lax
from jax.experimental import pallas as pl
from jax.experimental.pallas import tpu as pltpu
from jax.sharding import Mesh, PartitionSpec as P

D = 1024
HEADS = 16
HEAD = 64
ROT = 16


EPSILON = 1e-05


def layout(lengths, owners, device, row_count):
    owned = owners == device
    own_lengths = jnp.where(owned, lengths, 0)
    end_points = jnp.cumsum(own_lengths, dtype=jnp.int32)
    filled = jnp.sum(own_lengths, dtype=jnp.int32)
    places = jnp.arange(row_count, dtype=jnp.int32)
    passed = end_points[None, :] <= places[:, None]
    before_count = jnp.sum(passed.astype(jnp.int32), axis=1, dtype=jnp.int32)
    seq_start = jnp.max(jnp.where(passed, end_points[None, :], 0), axis=1)
    filled_row = places < filled
    seq_total = lengths.shape[0]
    segment = jnp.where(filled_row, before_count, seq_total + places)
    position = jnp.where(filled_row, places - seq_start, 0)
    return (segment, position)


def rotate(vectors, position, direction):
    half_rot = ROT // 2
    frequency = 10000.0 ** (-jnp.arange(half_rot, dtype=jnp.float32) / half_rot)
    angles = position.astype(jnp.float32)[:, None] * frequency[None, :]
    cosine = jnp.cos(angles)[:, None, :]
    sine_part = direction * jnp.sin(angles)[:, None, :]
    lead_part = vectors[..., :half_rot]
    trail_part = vectors[..., half_rot:ROT]
    turned_lead = lead_part * cosine - trail_part * sine_part
    turned_trail = trail_part * cosine + lead_part * sine_part
    return jnp.concatenate([turned_lead, turned_trail, vectors[..., ROT:]], axis=-1)


def normalize(values, gain, shift):
    centre = values - jnp.mean(values, axis=-1, keepdims=True)
    normed = centre * lax.rsqrt(jnp.mean(centre * centre, axis=-1, keepdims=True) + EPSILON)
    return (normed, normed * gain + shift)


def norm_back(grad_hidden, normed, gain, values):
    gain_grad = jnp.sum(grad_hidden * normed, axis=0)
    shift_grad = jnp.sum(grad_hidden, axis=0)
    grad_normed = grad_hidden * gain
    centre = values - jnp.mean(values, axis=-1, keepdims=True)
    factor = lax.rsqrt(jnp.mean(centre * centre, axis=-1, keepdims=True) + EPSILON)
    grad_values = factor * (
        grad_normed
        - jnp.mean(grad_normed, axis=-1, keepdims=True)
        - normed * jnp.mean(grad_normed * normed, axis=-1, keepdims=True)
    )
    return (gain_grad, shift_grad, grad_values)


def contract_rows(left, right):
    return lax.dot_general(
        left, right, (((0,), (0,)), ((), ())), preferred_element_type=jnp.float32
    )


def across(left, right):
    return lax.dot_general(
        left, right, (((1,), (1,)), ((), ())), preferred_element_type=jnp.float32
    )


def local(
    tokens,
    cotangent,
    lengths,
    owners,
    first_gain,
    first_bias,
    joint_weight,
    joint_bias,
    output_weight,
    output_bias,
    second_gain,
    second_bias,
    up_weight,
    up_bias,
    down_weight,
    down_bias,
):
    row_count = tokens.shape[0]
    score_scale = HEAD ** (-0.5)
    device = lax.axis_index(("rep", "shard"))
    segment, position = layout(lengths, owners, device, row_count)
    places = jnp.arange(row_count, dtype=jnp.int32)
    allowed = (segment[:, None] == segment[None, :]) & (places[None, :] <= places[:, None])
    gain_one, shift_one, joint_full, joint_offset, output_full, output_offset = (
        lax.all_gather(first_gain, "shard", axis=0, tiled=True),
        lax.all_gather(first_bias, "shard", axis=0, tiled=True),
        lax.all_gather(joint_weight, "shard", axis=0, tiled=True),
        lax.all_gather(joint_bias, "shard", axis=0, tiled=True),
        lax.all_gather(output_weight, "shard", axis=0, tiled=True),
        lax.all_gather(output_bias, "shard", axis=0, tiled=True),
    )
    gain_two, shift_two, up_full, up_offset, down_full, down_offset = (
        lax.all_gather(second_gain, "shard", axis=0, tiled=True),
        lax.all_gather(second_bias, "shard", axis=0, tiled=True),
        lax.all_gather(up_weight, "shard", axis=0, tiled=True),
        lax.all_gather(up_bias, "shard", axis=0, tiled=True),
        lax.all_gather(down_weight, "shard", axis=0, tiled=True),
        lax.all_gather(down_bias, "shard", axis=0, tiled=True),
    )
    values = tokens.astype(jnp.float32)
    normed_one, hidden_one = normalize(
        values, gain_one.astype(jnp.float32), shift_one.astype(jnp.float32)
    )
    input_one = hidden_one.astype(jnp.bfloat16)
    projected = jnp.dot(
        input_one, joint_full, preferred_element_type=jnp.float32
    ) + joint_offset.astype(jnp.float32)
    heads_view = projected.reshape(row_count, 3, HEADS, HEAD)
    query_low = rotate(heads_view[:, 0], position, 1.0).astype(jnp.bfloat16)
    keys_low = rotate(heads_view[:, 1], position, 1.0).astype(jnp.bfloat16)
    value_low = heads_view[:, 2].astype(jnp.bfloat16)
    masked = jnp.where(
        allowed[None],
        jnp.einsum("qhd,khd->hqk", query_low, keys_low, preferred_element_type=jnp.float32)
        * score_scale,
        -1e30,
    )
    row_peak = jnp.max(masked, axis=-1, keepdims=True)
    logsum = row_peak + jnp.log(jnp.sum(jnp.exp(masked - row_peak), axis=-1, keepdims=True))
    probs_low = jnp.exp(masked - logsum).astype(jnp.bfloat16)
    mixed_low = (
        jnp.einsum("hqk,khd->qhd", probs_low, value_low, preferred_element_type=jnp.float32)
        .reshape(row_count, D)
        .astype(jnp.bfloat16)
    )
    attention = jnp.dot(
        mixed_low, output_full, preferred_element_type=jnp.float32
    ) + output_offset.astype(jnp.float32)
    normed_two, hidden_two = normalize(
        values, gain_two.astype(jnp.float32), shift_two.astype(jnp.float32)
    )
    input_two = hidden_two.astype(jnp.bfloat16)
    before = jnp.dot(input_two, up_full, preferred_element_type=jnp.float32) + up_offset.astype(
        jnp.float32
    )
    active_low = jax.nn.gelu(before, approximate=False).astype(jnp.bfloat16)
    feed_out = jnp.dot(
        active_low, down_full, preferred_element_type=jnp.float32
    ) + down_offset.astype(jnp.float32)
    result = (values + attention + feed_out).astype(jnp.bfloat16)
    back_one = (
        lax.all_gather(first_gain, "shard", axis=0, tiled=True),
        lax.all_gather(joint_weight, "shard", axis=0, tiled=True),
        lax.all_gather(output_weight, "shard", axis=0, tiled=True),
    )
    back_two = (
        lax.all_gather(second_gain, "shard", axis=0, tiled=True),
        lax.all_gather(up_weight, "shard", axis=0, tiled=True),
        lax.all_gather(down_weight, "shard", axis=0, tiled=True),
    )
    gain_back_one, joint_back, output_back = back_one
    gain_back_two, up_back, down_back = back_two
    grad_out = cotangent.astype(jnp.float32)
    down_weight_grad = contract_rows(active_low, cotangent)
    down_bias_grad = jnp.sum(grad_out, axis=0)
    grad_active = across(cotangent, down_back)
    gelu_exact = partial(jax.nn.gelu, approximate=False)
    grad_before = jax.vjp(gelu_exact, before)[1](grad_active)[0].astype(jnp.bfloat16)
    up_weight_grad = contract_rows(input_two, grad_before)
    up_bias_grad = jnp.sum(grad_before.astype(jnp.float32), axis=0)
    gain_two_grad, shift_two_grad, grad_from_two = norm_back(
        across(grad_before, up_back), normed_two, gain_back_two.astype(jnp.float32), values
    )
    output_weight_grad = contract_rows(mixed_low, cotangent)
    grad_mixed = across(cotangent, output_back).astype(jnp.bfloat16).reshape(row_count, HEADS, HEAD)
    masked_again = jnp.where(
        allowed[None],
        jnp.einsum("qhd,khd->hqk", query_low, keys_low, preferred_element_type=jnp.float32)
        * score_scale,
        -1e30,
    )
    prob_back = jnp.exp(masked_again - logsum)
    prob_back_low = prob_back.astype(jnp.bfloat16)
    grad_probs = jnp.einsum(
        "qhd,khd->hqk", grad_mixed, value_low, preferred_element_type=jnp.float32
    )
    grad_value = jnp.einsum(
        "hqk,qhd->khd", prob_back_low, grad_mixed, preferred_element_type=jnp.float32
    )
    spread = jnp.sum(grad_probs * prob_back, axis=-1, keepdims=True)
    grad_scores = (prob_back * (grad_probs - spread)).astype(jnp.bfloat16)
    grad_query = rotate(
        jnp.einsum("hqk,khd->qhd", grad_scores, keys_low, preferred_element_type=jnp.float32)
        * score_scale,
        position,
        -1.0,
    )
    grad_keys = rotate(
        jnp.einsum("hqk,qhd->khd", grad_scores, query_low, preferred_element_type=jnp.float32)
        * score_scale,
        position,
        -1.0,
    )
    grad_joint = (
        jnp.stack([grad_query, grad_keys, grad_value], axis=1)
        .reshape(row_count, 3 * D)
        .astype(jnp.bfloat16)
    )
    joint_weight_grad = contract_rows(input_one, grad_joint)
    joint_bias_grad = jnp.sum(grad_joint.astype(jnp.float32), axis=0)
    gain_one_grad, shift_one_grad, grad_from_one = norm_back(
        across(grad_joint, joint_back), normed_one, gain_back_one.astype(jnp.float32), values
    )
    grad_tokens = grad_out + grad_from_one + grad_from_two
    group_shares = (
        lax.psum_scatter(gain_one_grad, "shard", scatter_dimension=0, tiled=True),
        lax.psum_scatter(shift_one_grad, "shard", scatter_dimension=0, tiled=True),
        lax.psum_scatter(joint_weight_grad, "shard", scatter_dimension=0, tiled=True),
        lax.psum_scatter(joint_bias_grad, "shard", scatter_dimension=0, tiled=True),
        lax.psum_scatter(output_weight_grad, "shard", scatter_dimension=0, tiled=True),
        lax.psum_scatter(down_bias_grad, "shard", scatter_dimension=0, tiled=True),
        lax.psum_scatter(gain_two_grad, "shard", scatter_dimension=0, tiled=True),
        lax.psum_scatter(shift_two_grad, "shard", scatter_dimension=0, tiled=True),
        lax.psum_scatter(up_weight_grad, "shard", scatter_dimension=0, tiled=True),
        lax.psum_scatter(up_bias_grad, "shard", scatter_dimension=0, tiled=True),
        lax.psum_scatter(down_weight_grad, "shard", scatter_dimension=0, tiled=True),
        lax.psum_scatter(down_bias_grad, "shard", scatter_dimension=0, tiled=True),
    )
    (
        share_gain_one,
        share_shift_one,
        share_joint_weight,
        share_joint_bias,
        share_output_weight,
        share_output_bias,
        share_gain_two,
        share_shift_two,
        share_up_weight,
        share_up_bias,
        share_down_weight,
        share_down_bias,
    ) = group_shares
    owned = lax.psum(
        (
            share_gain_one,
            share_shift_one,
            share_joint_weight,
            share_joint_bias,
            share_output_weight,
            share_output_bias,
            share_gain_two,
            share_shift_two,
            share_up_weight,
            share_up_bias,
            share_down_weight,
            share_down_bias,
        ),
        "rep",
    )
    return (
        result,
        grad_tokens,
        owned[0],
        owned[1],
        owned[2],
        owned[3],
        owned[4],
        owned[5],
        owned[6],
        owned[7],
        owned[8],
        owned[9],
        owned[10],
        owned[11],
    )


PAIR = [(0, 1), (1, 0)]
BLOCKS = 8
LANE = 128
EXTRA = 16
GROUP = ("o", "p", "q", "c")
VMEM_BYTES = 58 * 1024 * 1024


def swap(values, *axes):
    if len(axes) == 1:
        return lax.ppermute(values, axes[0], PAIR)
    return lax.ppermute(values, axes, [(i, 3 - i) for i in range(4)])


def join(own, other, at, axis=0):
    first = at == 0
    return jnp.concatenate(
        [jnp.where(first, own, other), jnp.where(first, other, own)], axis=axis
    )


def pin(*values):
    return lax.optimization_barrier(values)


def take(values, at, axis=0):
    return lax.dynamic_index_in_dim(values, at, axis, keepdims=False)


def low(values):
    return values.astype(jnp.bfloat16)


def wide(values):
    return values.astype(jnp.float32)


def times(left, right):
    return jnp.dot(left, right, preferred_element_type=jnp.float32)


def places_of(ids_ref):
    return tuple(ids_ref[i] for i in range(5))


def call(kernel, outs, scratch, micros, *operands, memory):
    whole = pl.BlockSpec(memory_space=pltpu.VMEM)
    specs = {
        "s": pl.BlockSpec(memory_space=pltpu.SMEM),
        "v": whole,
        "h": pl.BlockSpec(memory_space=pl.ANY),
    }
    size = sum(leaf.size * leaf.dtype.itemsize for leaf in (*operands, *outs))
    return pl.pallas_call(
        kernel,
        out_shape=tuple(outs),
        in_specs=[specs[kind] for kind in memory],
        out_specs=tuple(whole for _ in outs),
        scratch_shapes=scratch,
        compiler_params=pltpu.CompilerParams(vmem_limit_bytes=VMEM_BYTES),
        cost_estimate=pl.CostEstimate(
            flops=int(micros * 1.15e9), bytes_accessed=size, transcendentals=0
        ),
    )(*operands)


def fetch(pairs, sems):
    copies = [
        pltpu.make_async_copy(source, target, sems.at[i])
        for i, (source, target) in enumerate(pairs)
    ]
    for copy in copies:
        copy.start()
    return copies


def finish(copies):
    for copy in copies:
        copy.wait()


def sheet_pairs(pieces, target, small, places):
    x, o, p, q, c = places
    pairs = []
    for index, piece in enumerate(pieces):
        jo, jq = index // 2, index % 2
        rows = piece.shape[1] - EXTRA
        for k in range(4):
            jc, jp = k // 2, k % 2
            shard = (((o ^ jo) * 2 + (p ^ jp)) * 2 + (q ^ jq)) * 2 + (c ^ jc)
            at = pl.multiple_of(shard * rows, rows)
            pairs.append((piece.at[k, pl.ds(0, rows)], target.at[pl.ds(at, rows)]))
            at = pl.multiple_of(shard * EXTRA, EXTRA)
            pairs.append((piece.at[k, pl.ds(rows, EXTRA)], small.at[pl.ds(at, EXTRA)]))
    return pairs


def vector_of(small, start, size=HEAD):
    parts = [
        wide(small[shard * EXTRA : (shard + 1) * EXTRA, start + at : start + at + HEAD])[:1]
        for shard in range(16)
        for at in range(0, size, HEAD)
    ]
    pairs = [jnp.concatenate(parts[i : i + 2], axis=1) for i in range(0, len(parts), 2)]
    return jnp.concatenate(pairs, axis=1)


def tall_pairs(pieces, target, places):
    x, o, p, q, c = places
    pairs = []
    for index, piece in enumerate(pieces):
        jo, jq = index // 2, index % 2
        rows = piece.shape[0]
        at = ((o ^ jo) * 2 + (q ^ jq)) * rows
        pairs.append((piece, target.at[pl.ds(pl.multiple_of(at, rows), rows)]))
    return pairs


def norm_of(tokens):
    values = wide(tokens)
    centre = values - jnp.mean(values, axis=-1, keepdims=True)
    return centre * lax.rsqrt(jnp.mean(centre * centre, axis=-1, keepdims=True) + EPSILON)


def fold(values):
    rows, columns = values.shape
    return jnp.sum(values.reshape(rows // 8, 8, columns), axis=0)


def cut_kernel(ids, joint, up, small, keep, send):
    x, o, p, q, c = places_of(ids)
    parts = joint.shape[1] // D
    height = joint.shape[0]

    def block(ref, index):
        return ref[:, pl.ds(pl.multiple_of(index * LANE, LANE), LANE)]

    for jp, target in ((0, keep), (1, send)):
        for jc in (0, 1):
            pp, cc = p ^ jp, c ^ jc
            target[jc, height:, :] = jnp.broadcast_to(small[...], (EXTRA, small.shape[1]))
            for part in range(parts):
                target[jc, :height, part * LANE : (part + 1) * LANE] = block(
                    joint, part * 8 + x * 4 + pp * 2 + cc
                )
            for k in range(4):
                oo, qq = k // 2, k % 2
                at = (parts + k) * LANE
                target[jc, :height, at : at + LANE] = block(
                    up, (((oo * 2 + pp) * 2 + qq) * 2 + cc) * 2 + x
                )


def turner(cap):
    lane = lax.broadcasted_iota(jnp.int32, (cap, LANE), 1)
    lead = lane % HEAD < ROT // 2

    def turn(values, cos_part, sin_part):
        other = jnp.where(
            lead, pltpu.roll(values, LANE - ROT // 2, 1), pltpu.roll(values, ROT // 2, 1)
        )
        return values * cos_part + other * sin_part

    return turn, (lane < HEAD, lane >= HEAD)


def block_pairs(sources, tokens, cotangent):
    cap = sources[0].shape[1]
    return [
        (source.at[2 * k + which], target.at[pl.ds((2 * i + k) * cap, cap)])
        for i, source in enumerate(sources)
        for k in (0, 1)
        for which, target in enumerate((tokens, cotangent))
        if target is not None
    ]


def both_ways(step, near_out, far_out, size):
    for i in (0, 1):
        near_out[i * size : (i + 1) * size, :] = step(2 * i)
    for i in (0, 1):
        far_out[i * size : (i + 1) * size, :] = low(step(2 * i + 1))


def attention_kernel(
    ids,
    block_0,
    block_1,
    block_2,
    block_3,
    sheet_0,
    sheet_1,
    sheet_2,
    sheet_3,
    output_weight,
    fed,
    cosine,
    sine,
    position,
    near_out,
    far_out,
    grad_ref,
    home_0,
    home_1,
    away,
    output_grad,
    grad_sum,
    tokens,
    cotangent,
    joint,
    inputs,
    mixed_all,
    total,
    small,
    gain,
    shift,
    offset,
    sems,
):
    x, o, p, q, c = places_of(ids)
    cap = block_0.shape[1]
    finish(
        fetch(
            sheet_pairs((sheet_0, sheet_1, sheet_2, sheet_3), joint, small, places_of(ids))
            + block_pairs((block_0, block_1, block_2, block_3), tokens, cotangent),
            sems,
        )
    )
    gain[...] = vector_of(small, 0)
    shift[...] = vector_of(small, HEAD)
    offset[...] = vector_of(small, 2 * HEAD, 3 * HEAD)
    starts = [pl.multiple_of((part * 8 + x * 4 + p * 2 + c) * LANE, LANE) for part in range(3)]
    bias = jnp.concatenate([offset[:, pl.ds(at, LANE)] for at in starts], axis=1)
    total[...] = jnp.zeros_like(total)
    turn, mine = turner(2 * cap)
    own = mine[0][:cap]
    down = lax.broadcasted_iota(jnp.int32, (cap, cap), 0)
    along = lax.broadcasted_iota(jnp.int32, (cap, cap), 1)
    scale = HEAD ** (-0.5)

    def by_head(values):
        none = jnp.zeros_like(values)
        return jnp.concatenate([jnp.where(own, values, none), jnp.where(own, none, values)])

    def attend(query, keys, value, grad_mixed, place):
        allowed = ((along <= down) & (along >= down - place))[None]
        query_two, grad_two = by_head(query), by_head(grad_mixed)
        scores = across(query_two, keys).reshape(2, cap, cap) * scale
        scores = jnp.where(allowed, scores, -1e30)
        raised = jnp.exp(scores - jnp.max(scores, axis=-1, keepdims=True))
        probs = raised / jnp.sum(raised, axis=-1, keepdims=True)
        probs_low = low(probs).reshape(2 * cap, cap)
        grad_probs = across(grad_two, value).reshape(2, cap, cap)
        spread = jnp.sum(grad_probs * probs, axis=-1, keepdims=True)
        grad_scores = low(probs * (grad_probs - spread)).reshape(2 * cap, cap)
        mixed = times(probs_low, value)
        grad_query = times(grad_scores, keys)
        return (
            jnp.where(own, mixed[:cap], mixed[cap:]),
            jnp.where(own, grad_query[:cap], grad_query[cap:]) * scale,
            contract_rows(grad_scores, query_two) * scale,
            contract_rows(probs_low, grad_two),
        )

    def step(pair):
        rows = slice(pair * 2 * cap, (pair + 1) * 2 * cap)
        input_low = low(norm_of(tokens[rows, :]) * gain[...] + shift[...])
        inputs[rows, :] = input_low
        projected = times(input_low, joint[...]) + bias
        cos_part, sin_part = cosine[rows, :], sine[rows, :]
        query = low(turn(projected[:, :LANE], cos_part, sin_part))
        keys = low(turn(projected[:, LANE : 2 * LANE], cos_part, sin_part))
        value = low(projected[:, 2 * LANE :])
        grad_mixed = low(across(cotangent[rows, :], output_weight[...]))
        place = position[rows, :]
        found = [
            attend(query[at], keys[at], value[at], grad_mixed[at], place[at, :1])
            for at in (slice(0, cap), slice(cap, 2 * cap))
        ]
        mixed, grad_query, grad_keys, grad_value = (jnp.concatenate(both) for both in zip(*found))
        mixed = low(mixed)
        mixed_all[rows, :] = mixed
        grad_joint = low(
            jnp.concatenate(
                [
                    turn(grad_query, cos_part, -sin_part),
                    turn(grad_keys, cos_part, -sin_part),
                    grad_value,
                ],
                axis=1,
            )
        )
        grad_ref[rows, :] = grad_joint
        total[...] += fold(wide(grad_joint))
        return times(mixed, output_weight[...]) + wide(fed[rows, :])

    both_ways(step, near_out, far_out, 2 * cap)
    grad_sum[...] = jnp.sum(total[...], axis=0, keepdims=True)
    output_grad[...] = low(contract_rows(mixed_all[...], cotangent[...]))
    half = away.shape[0] // 2
    here = home_0, away.at[pl.ds(0, half)]
    there = home_1, away.at[pl.ds(half, half)]
    sheet_grads(inputs, grad_ref, here, there, 0, places_of(ids))


def for_place(at, here, there, store):
    pl.when(at)(lambda: store(*here))
    pl.when(jnp.logical_not(at))(lambda: store(*there))


def sheet_grads(inputs, grads, here, there, base, places):
    x, o, p, q, c = places
    columns = grads.shape[1]
    rows = D // 16
    for oo in (0, 1):
        found = contract_rows(inputs[:, oo * D // 2 : (oo + 1) * D // 2], grads[...])
        found = low(found).reshape(2, 2, 2, rows, columns)

        def store(home, away, found=found):
            for pp in (0, 1):
                for cc in (0, 1):
                    down = pl.ds(pl.multiple_of(base + (p ^ pp) * rows, rows), rows)
                    along = pl.ds(pl.multiple_of((c ^ cc) * columns, LANE), columns)
                    home[down, along] = jnp.where(q == 0, found[pp, 0, cc], found[pp, 1, cc])
                    away[down, along] = jnp.where(q == 0, found[pp, 1, cc], found[pp, 0, cc])

        for_place(o == oo, here, there, store)


def feed_kernel(
    ids,
    block_0,
    block_1,
    block_2,
    block_3,
    sheet_0,
    sheet_1,
    sheet_2,
    sheet_3,
    tall_0,
    tall_1,
    tall_2,
    tall_3,
    fed,
    late_offset,
    grad_all,
    home_0,
    home_1,
    away_0,
    away_1,
    grad_sum,
    tokens,
    cotangent,
    up,
    down,
    inputs,
    active_all,
    total,
    small,
    gain,
    shift,
    sems,
):
    places = places_of(ids)
    x, o, p, q, c = places
    cap = block_0.shape[1]
    finish(
        fetch(
            sheet_pairs((sheet_0, sheet_1, sheet_2, sheet_3), up, small, places)
            + block_pairs((block_0, block_1, block_2, block_3), tokens, cotangent)
            + tall_pairs((tall_0, tall_1, tall_2, tall_3), down, places),
            sems,
        )
    )
    gain[...] = vector_of(small, 0)
    shift[...] = vector_of(small, HEAD)
    width = 4 * LANE
    late_offset[...] = vector_of(small, width - 2 * HEAD) + vector_of(small, width - HEAD)
    along = pl.ds(pl.multiple_of((x + 1) * LANE, LANE), LANE)
    bias = [
        small[pl.ds(pl.multiple_of((((oo * 2 + p) * 2 + qq) * 2 + c) * EXTRA, EXTRA), EXTRA), along]
        for oo in (0, 1)
        for qq in (0, 1)
    ]
    bias = wide(jnp.concatenate(bias, axis=1))[:1]
    total[...] = jnp.zeros_like(total)

    for pair in range(BLOCKS // 2):
        rows = slice(pair * 2 * cap, (pair + 1) * 2 * cap)
        input_low = low(norm_of(tokens[rows, :]) * gain[...] + shift[...])
        inputs[rows, :] = input_low
        before = times(input_low, up[...]) + bias
        slope = 0.5 + 0.5 * lax.erf(before * 0.5**0.5)
        active = low(before * slope)
        active_all[rows, :] = active
        slope = slope + before * jnp.exp(-0.5 * before * before) * (0.5 / jnp.pi) ** 0.5
        grad_before = low(across(cotangent[rows, :], down[...]) * slope)
        grad_all[rows, :] = grad_before
        total[...] += fold(wide(grad_before))
        fed[rows, :] = low(times(active, down[...]))

    grad_sum[...] = jnp.sum(total[...], axis=0, keepdims=True)
    unit = home_0.shape[0] // 2
    here, there = (home_0, away_0), (home_1, away_1)
    for oo in (0, 1):
        found = low(contract_rows(active_all[:, oo * 2 * unit : (oo + 1) * 2 * unit], cotangent[...]))

        def store(home, away, found=found):
            home[:unit, :] = jnp.where(q == 0, found[:unit], found[unit:])
            away[:unit, :] = jnp.where(q == 0, found[unit:], found[:unit])

        for_place(o == oo, here, there, store)
    sheet_grads(inputs, grad_all, here, there, unit, places)


def pull_kernel(
    ids,
    block_0,
    block_1,
    block_2,
    block_3,
    join_0,
    join_1,
    join_2,
    join_3,
    sheet_0,
    sheet_1,
    sheet_2,
    sheet_3,
    grad_joint,
    grad_before,
    joint_sum,
    up_sum,
    near_out,
    far_out,
    sums,
    tokens,
    joint,
    up,
    totals,
    small_one,
    small_two,
    gain_one,
    gain_two,
    own,
    sems,
):
    places = places_of(ids)
    x, o, p, q, c = places
    cap = block_0.shape[1]
    finish(
        fetch(
            block_pairs((block_0, block_1, block_2, block_3), tokens, None)
            + sheet_pairs((join_0, join_1, join_2, join_3), joint, small_one, places)
            + sheet_pairs((sheet_0, sheet_1, sheet_2, sheet_3), up, small_two, places)
            + [(block_0.at[1], own)],
            sems,
        )
    )
    gain_one[...] = vector_of(small_one, 0)
    gain_two[...] = vector_of(small_two, 0)
    totals[...] = jnp.zeros_like(totals)

    def step(pair):
        rows = slice(pair * 2 * cap, (pair + 1) * 2 * cap)
        normed = norm_of(tokens[rows, :])
        grad_first = across(grad_joint[rows, :], joint[...])
        grad_second = across(grad_before[rows, :], up[...])
        totals[0] += fold(grad_first * normed)
        totals[1] += fold(grad_first)
        totals[2] += fold(grad_second * normed)
        totals[3] += fold(grad_second)
        return grad_first * gain_one[...] + grad_second * gain_two[...]

    both_ways(step, near_out, far_out, 2 * cap)
    sums[...] = jnp.zeros_like(sums)
    sums[0:4, :] = jnp.sum(totals[...], axis=1)
    sums[4:5, :] = jnp.sum(wide(own[...]), axis=0, keepdims=True)
    at = pl.ds(pl.multiple_of((x * 4 + p * 2 + c) * LANE, LANE), LANE)
    for part in range(3):
        sums[5 + part : 6 + part, at] = joint_sum[:, part * LANE : (part + 1) * LANE]
    for k in range(4):
        at = pl.ds(pl.multiple_of((k % 2 * 4 + c * 2 + x) * LANE, LANE), LANE)
        for pp in (0, 1):
            row = 8 + k // 2 * 2 + pp
            found = up_sum[:, k * LANE : (k + 1) * LANE]
            sums[row : row + 1, at] = jnp.where(p == pp, found, jnp.zeros_like(found))


def final_kernel(
    up_home,
    up_away,
    down_sent,
    up_sent,
    joint_home,
    joint_away,
    joint_sent,
    out_0,
    out_1,
    out_2,
    out_3,
    down,
):
    rows = down.shape[0]
    down[...] = low(total(up_home[:rows, :], up_away[:rows, :], down_sent[...]))
    found = low(total(up_home[rows:, :], up_away[rows:, :], up_sent[...]))
    joint = low(total(joint_home[...], joint_away[:rows, :], joint_sent[...]))
    half, width = rows // 2, joint.shape[1] // 2
    hidden = found.shape[1] // 2
    for k, out in enumerate((out_0, out_1, out_2, out_3)):
        jp, jc = k // 2, k % 2
        out[:, :width] = joint[jp * half : (jp + 1) * half, jc * width : (jc + 1) * width]
        out[:, width:] = found[jp * half : (jp + 1) * half, jc * hidden : (jc + 1) * hidden]


def lay_kernel(ids, own, other, joint, up):
    x, o, p, q, c = places_of(ids)
    parts = joint.shape[1] // D
    for xx, source in ((0, own), (1, other)):
        for pp in (0, 1):
            for cc in (0, 1):
                values = wide(source[pp, cc])
                at_x, at_p, at_c = x ^ xx, p ^ pp, c ^ cc
                blocks = [(joint, part * 8 + at_x * 4 + at_p * 2 + at_c) for part in range(parts)]
                blocks += [
                    (up, (((k // 2 * 2 + at_p) * 2 + k % 2) * 2 + at_c) * 2 + at_x) for k in range(4)
                ]
                for k, (out, at) in enumerate(blocks):
                    out[:, pl.ds(pl.multiple_of(at * LANE, LANE), LANE)] = values[
                        :, k * LANE : (k + 1) * LANE
                    ]


def lane_sum(near, came):
    lane = near + wide(came)
    rows = lane.shape[0] // 4
    return lane[:rows], *(low(lane[i * rows : (i + 1) * rows]) for i in (1, 2, 3))


def total(*parts):
    found = wide(parts[0])
    for part in parts[1:]:
        found += wide(part)
    return found


def grouped(
    tokens,
    cotangent,
    lengths,
    owners,
    first_gain,
    first_bias,
    joint_weight,
    joint_bias,
    output_weight,
    output_bias,
    second_gain,
    second_bias,
    up_weight,
    up_bias,
    down_weight,
    down_bias,
):
    x, o, p, q, c = (lax.axis_index(name) for name in ("x", "o", "p", "q", "c"))
    ids = jnp.stack([x, o, p, q, c]).astype(jnp.int32)
    cap = tokens.shape[0]
    rows = BLOCKS * cap
    part = joint_weight.shape[0]
    hidden = up_weight.shape[1] // 8
    unit = hidden // 4
    bf, f32 = jnp.bfloat16, jnp.float32

    def like(shape, kind):
        return jax.ShapeDtypeStruct(shape, kind)

    pair = jnp.stack([tokens, cotangent])
    along_x = swap(pair, "x")

    rest = jnp.zeros((HEAD,), bf)
    small = jnp.concatenate(
        [first_gain, first_bias, joint_bias, rest, second_gain, second_bias, up_bias, output_bias, down_bias]
    )[None]
    down_half = take(down_weight.reshape(2, unit, D), x)
    keep, send = call(
        cut_kernel,
        [
            like((2, part + EXTRA, 3 * LANE + hidden), bf),
            like((2, part + EXTRA, 3 * LANE + hidden), bf),
        ],
        [],
        0,
        ids,
        joint_weight,
        up_weight,
        small,
        memory="svvv",
    )
    came, down_other, down_side = swap(send, "p"), swap(down_half, "o"), swap(down_half, "q")
    along_p = swap(pin(tokens, send)[0], "p")

    came, down_other, down_side, along_x, along_p, lengths = pin(
        came, down_other, down_side, along_x, along_p, lengths
    )

    turn_came, output_came = swap(jnp.concatenate([keep[1:], came[1:]]), "c"), swap(output_weight, "c")
    turn_came, output_came, along_p = pin(turn_came, output_came, along_p)

    turned = jnp.concatenate([keep[:1], came[:1], turn_came])
    first, up_own, joint_own, along_p = pin(
        jnp.concatenate([pair, along_x]),
        turned[:, :, 3 * LANE :],
        turned[:, :, : 3 * LANE],
        along_p,
    )
    up_other, up_side = swap(up_own, "o"), swap(up_own, "q")
    grad_along_p, along_both = swap(pin(cotangent, along_p)[0], "p"), swap(along_p, "x")
    first_came = swap(first, "c")

    devices = jnp.stack(
        [
            ((((x ^ xx) * 2 + o) * 2 + (p ^ pp)) * 2 + q) * 2 + (c ^ cc)
            for pp in (0, 1)
            for cc in (0, 1)
            for xx in (0, 1)
        ]
    )
    position = jax.vmap(lambda device: layout(lengths, owners, device, cap)[1])(devices)
    position = position.reshape(rows, 1)
    place = jnp.arange(LANE) % HEAD
    half_rot = ROT // 2
    frequency = 10000.0 ** (-jnp.arange(half_rot, dtype=f32) / half_rot)
    angles = position.astype(f32) * jnp.tile(frequency, LANE // half_rot)[None, :]
    position = jnp.broadcast_to(position, (rows, LANE))
    cosine = jnp.where(place < ROT, jnp.cos(angles), 1.0)
    sine = jnp.sin(angles)
    sine = jnp.where(place < half_rot, -sine, jnp.where(place < ROT, sine, 0.0))

    cosine, sine, position, up_other, up_side, grad_along_p, along_both, first_came, joint_own, down_other = pin(
        cosine, sine, position, up_other, up_side, grad_along_p, along_both, first_came, joint_own, down_other
    )

    up_corner, joint_other = swap(up_other, "q"), swap(joint_own, "o")
    grad_along_both, down_corner = swap(grad_along_p, "x"), swap(down_other, "q")
    turn_over = [
        (((a * 2 + b) * 2 + e) * 2 + f, ((b * 2 + a) * 2 + f) * 2 + e)
        for a in (0, 1)
        for b in (0, 1)
        for e in (0, 1)
        for f in (0, 1)
    ]
    cross = ("x", "o", "q", "c")
    up_corner, down_corner, joint_other, grad_along_both, output_pair = pin(
        up_corner, down_corner, joint_other, grad_along_both, join(output_weight, output_came, c)
    )
    second = jnp.stack([along_p, grad_along_p, along_both, grad_along_both])
    second_came = swap(second, "c")
    joint_pair, output_pair, second_came = pin(
        jnp.stack([joint_own, joint_other]), output_pair, second_came
    )
    blocks = first, first_came, second, second_came
    up_sheets = up_own, up_side, up_other, up_corner
    down_talls = down_half, down_side, down_other, down_corner
    joint_far = swap(joint_pair, "q")
    output_pair = lax.ppermute(output_pair, cross, turn_over)
    copies = pltpu.SemaphoreType.DMA
    tall = (rows, D)
    found = call(
        feed_kernel,
        [
            like(tall, bf),
            like((1, D), f32),
            like((rows, hidden), bf),
            *(like((2 * unit, D), bf) for _ in range(4)),
            like((1, hidden), f32),
        ],
        [
            pltpu.VMEM(tall, bf),
            pltpu.VMEM(tall, bf),
            pltpu.VMEM((D, hidden), bf),
            pltpu.VMEM((hidden, D), bf),
            pltpu.VMEM(tall, bf),
            pltpu.VMEM((rows, hidden), bf),
            pltpu.VMEM((8, hidden), f32),
            pltpu.VMEM((16 * EXTRA, hidden), bf),
            pltpu.VMEM((1, D), f32),
            pltpu.VMEM((1, D), f32),
            copies((52,)),
        ],
        20,
        ids,
        *blocks,
        *up_sheets,
        *down_talls,
        memory="shhhhhhhhhhhh",
    )
    joint_far, output_pair, *found = pin(joint_far, output_pair, *found)
    joint_sheets = joint_own, joint_far[0], joint_other, joint_far[1]
    fed, late_offset, grad_before, up_home_0, up_home_1, up_away_0, up_away_1, up_sum = found
    up_away_1 = swap(up_away_1, "q")

    found = call(
        attention_kernel,
        [
            like((rows // 2, D), f32),
            like((rows // 2, D), bf),
            like((rows, 3 * LANE), bf),
            like((2 * part, 6 * LANE), bf),
            like((2 * part, 6 * LANE), bf),
            like((4 * part, 6 * LANE), bf),
            like((LANE, D), bf),
            like((1, 3 * LANE), f32),
        ],
        [
            pltpu.VMEM(tall, bf),
            pltpu.VMEM(tall, bf),
            pltpu.VMEM((D, 3 * LANE), bf),
            pltpu.VMEM(tall, bf),
            pltpu.VMEM((rows, LANE), bf),
            pltpu.VMEM((8, 3 * LANE), f32),
            pltpu.VMEM((16 * EXTRA, 3 * LANE), bf),
            pltpu.VMEM((1, D), f32),
            pltpu.VMEM((1, D), f32),
            pltpu.VMEM((1, 3 * D), f32),
            copies((48,)),
        ],
        22,
        ids,
        *blocks,
        *joint_sheets,
        output_pair,
        fed,
        cosine,
        sine,
        position,
        memory="shhhhhhhhvvvvv",
    )
    up_away_1, up_away_0, *found = pin(up_away_1, up_away_0, *found)
    near_part, far_part, grad_joint, joint_home_0, joint_home_1, joint_away, output_grad, joint_sum = found

    def lane_sum(near, came, block):
        at = slice(block * cap, (block + 1) * cap)
        return near[at] + wide(came[at])

    up_sent = low(total(up_home_1, up_away_1))
    down_sent = swap(up_sent[:unit], "o")
    joint_away, up_away_0 = swap(joint_away, "q"), swap(up_away_0, "q")
    result_lane = near_part, swap(far_part, "c")
    result_sent, grad_joint = pin(
        low(jnp.concatenate([lane_sum(*result_lane, 1), lane_sum(*result_lane, 3)])), grad_joint
    )
    result_came = swap(result_sent, "x")
    output_part = lax.ppermute(output_grad, cross, turn_over)
    found = call(
        pull_kernel,
        [like((rows // 2, D), f32), like((rows // 2, D), bf), like((16, D), f32)],
        [
            pltpu.VMEM(tall, bf),
            pltpu.VMEM((D, 3 * LANE), bf),
            pltpu.VMEM((D, hidden), bf),
            pltpu.VMEM((4, 8, D), f32),
            pltpu.VMEM((16 * EXTRA, 3 * LANE), bf),
            pltpu.VMEM((16 * EXTRA, hidden), bf),
            pltpu.VMEM((1, D), f32),
            pltpu.VMEM((1, D), f32),
            pltpu.VMEM((cap, D), bf),
            copies((73,)),
        ],
        11,
        ids,
        *blocks,
        *joint_sheets,
        *up_sheets,
        grad_joint,
        grad_before,
        joint_sum,
        up_sum,
        memory="shhhhhhhhhhhhvvvv",
    )
    down_sent, up_away_0, joint_away, result_came, output_part, *found = pin(
        down_sent, up_away_0, joint_away, result_came, output_part, *found
    )
    near_part, far_part, sums = found
    came, sums_came = swap(far_part, "c"), swap(sums, "c")
    output_part = output_part.reshape(2, part, D)
    result_kept = lane_sum(*result_lane, 0) + wide(result_came[:cap])

    joint_sent, result_sent, output_sent, up_sent, came, sums_came = pin(
        low(total(joint_home_1, joint_away[2 * part :])),
        low(lane_sum(*result_lane, 2) + wide(result_came[cap:])),
        take(output_part, 1 - c),
        up_sent[unit:],
        came,
        sums_came,
    )

    lane = near_part, came
    sums = sums + sums_came
    top = low(sums)
    rest = low(sums - wide(top))
    sums, *sent = pin(
        wide(top) + wide(rest),
        *(jnp.concatenate([low(lane_sum(*lane, i)), top, rest]) for i in (1, 2, 3)),
    )
    side, far_side, corner = swap(sent[0], "x"), swap(sent[1], "p"), swap(sent[2], "x", "p")
    joint_sent, up_sent = swap(joint_sent, "o"), swap(up_sent, "o")
    side, far_side, corner, joint_sent, up_sent, output_sent = pin(
        side, far_side, corner, joint_sent, up_sent, output_sent
    )

    def rest_of(values):
        return wide(values[cap : cap + 16]) + wide(values[cap + 16 :])

    *final, down_final = call(
        final_kernel,
        [*(like((part, 3 * LANE + hidden), bf) for _ in range(4)), like((unit, D), bf)],
        [],
        1,
        up_home_0,
        up_away_0,
        down_sent,
        up_sent,
        joint_home_0,
        joint_away,
        joint_sent,
        memory="vvvvvvv",
    )
    sums = (sums + rest_of(side)) + (rest_of(far_side) + rest_of(corner))
    *final, down_final, sums = pin(*final, down_final, sums)
    sent = swap(final[1], "c"), swap(final[2], "p"), swap(final[3], "p", "c")
    down_came, sums_came, output_sent = swap(down_final, "x"), swap(sums, "o"), swap(output_sent, "c")
    pulled = lane_sum(*lane, 0) + wide(side[:cap]) + wide(far_side[:cap]) + wide(corner[:cap])
    *sent, down_came, sums_came, output_sent = pin(*sent, down_came, sums_came, output_sent)

    both, sums, output_own, result_sent = pin(
        jnp.stack([final[0], *sent]).reshape(2, 2, part, -1),
        sums + sums_came,
        low(total(take(output_part, c), output_sent)),
        result_sent,
    )
    both_came, sums_came, output_came = swap(both, "x"), swap(sums, "q"), swap(output_own, "x")
    result_came = swap(result_sent, "p")
    own_values = wide(tokens)
    result = low(own_values + total(result_kept, result_came) + late_offset)
    sums = sums + sums_came
    shard = ((o * 2 + p) * 2 + q) * 2 + c

    def own_part(values):
        size = values.size // 16
        return lax.dynamic_slice_in_dim(values.reshape(-1), shard * size, size)

    output_own = total(output_own, output_came)
    down_own = wide(join(down_final, down_came, x))
    joint_own_grad, up_own_grad = call(
        lay_kernel,
        [like((part, 3 * D), f32), like((part, up_weight.shape[1]), f32)],
        [],
        1,
        ids,
        both,
        both_came,
        memory="svv",
    )

    own_normed = norm_of(tokens)
    centre = own_values - jnp.mean(own_values, axis=-1, keepdims=True)
    factor = lax.rsqrt(jnp.mean(centre * centre, axis=-1, keepdims=True) + EPSILON)
    grad_tokens = wide(cotangent) + factor * (
        pulled
        - jnp.mean(pulled, axis=-1, keepdims=True)
        - own_normed * jnp.mean(pulled * own_normed, axis=-1, keepdims=True)
    )
    norm_grads = [own_part(sums[i]) for i in range(5)]
    return (
        result,
        grad_tokens,
        norm_grads[0],
        norm_grads[1],
        joint_own_grad,
        own_part(sums[5:8]),
        output_own,
        norm_grads[4],
        norm_grads[2],
        norm_grads[3],
        up_own_grad,
        own_part(sums[8:12]),
        down_own,
        norm_grads[4],
    )


def solution(mesh):
    if mesh.shape["rep"] == 2 and mesh.shape["shard"] * HEAD == D:
        work, body = Mesh(mesh.devices.reshape(2, 2, 2, 2, 2), ("x", *GROUP)), grouped
        group, every = GROUP, ("x", *GROUP)
    else:
        work, body = mesh, local
        group, every = "shard", ("rep", "shard")
    row, vec, mat = P(every, None), P(group), P(group, None)
    return jax.shard_map(
        body,
        mesh=work,
        in_specs=(row, row, P(), P(), vec, vec, mat, vec, mat, vec, vec, vec, mat, vec, mat, vec),
        out_specs=(row, row, vec, vec, mat, vec, mat, vec, vec, vec, mat, vec, mat, vec),
        check_vma=False,
    )
```

```python
from functools import partial

import jax
import jax.numpy as jnp
from jax import lax
from jax.experimental import pallas as pl
from jax.experimental.pallas import tpu as pltpu
from jax.sharding import Mesh, PartitionSpec as P

D = 1024
HEADS = 16
HEAD = 64
ROT = 16


EPSILON = 1e-05


def layout(lengths, owners, device, row_count):
    owned = owners == device
    own_lengths = jnp.where(owned, lengths, 0)
    end_points = jnp.cumsum(own_lengths, dtype=jnp.int32)
    filled = jnp.sum(own_lengths, dtype=jnp.int32)
    places = jnp.arange(row_count, dtype=jnp.int32)
    passed = end_points[None, :] <= places[:, None]
    before_count = jnp.sum(passed.astype(jnp.int32), axis=1, dtype=jnp.int32)
    seq_start = jnp.max(jnp.where(passed, end_points[None, :], 0), axis=1)
    filled_row = places < filled
    seq_total = lengths.shape[0]
    segment = jnp.where(filled_row, before_count, seq_total + places)
    position = jnp.where(filled_row, places - seq_start, 0)
    return (segment, position)


def rotate(vectors, position, direction):
    half_rot = ROT // 2
    frequency = 10000.0 ** (-jnp.arange(half_rot, dtype=jnp.float32) / half_rot)
    angles = position.astype(jnp.float32)[:, None] * frequency[None, :]
    cosine = jnp.cos(angles)[:, None, :]
    sine_part = direction * jnp.sin(angles)[:, None, :]
    lead_part = vectors[..., :half_rot]
    trail_part = vectors[..., half_rot:ROT]
    turned_lead = lead_part * cosine - trail_part * sine_part
    turned_trail = trail_part * cosine + lead_part * sine_part
    return jnp.concatenate([turned_lead, turned_trail, vectors[..., ROT:]], axis=-1)


def normalize(values, gain, shift):
    centre = values - jnp.mean(values, axis=-1, keepdims=True)
    normed = centre * lax.rsqrt(jnp.mean(centre * centre, axis=-1, keepdims=True) + EPSILON)
    return (normed, normed * gain + shift)


def norm_back(grad_hidden, normed, gain, values):
    gain_grad = jnp.sum(grad_hidden * normed, axis=0)
    shift_grad = jnp.sum(grad_hidden, axis=0)
    grad_normed = grad_hidden * gain
    centre = values - jnp.mean(values, axis=-1, keepdims=True)
    factor = lax.rsqrt(jnp.mean(centre * centre, axis=-1, keepdims=True) + EPSILON)
    grad_values = factor * (
        grad_normed
        - jnp.mean(grad_normed, axis=-1, keepdims=True)
        - normed * jnp.mean(grad_normed * normed, axis=-1, keepdims=True)
    )
    return (gain_grad, shift_grad, grad_values)


def contract_rows(left, right):
    return lax.dot_general(
        left, right, (((0,), (0,)), ((), ())), preferred_element_type=jnp.float32
    )


def across(left, right):
    return lax.dot_general(
        left, right, (((1,), (1,)), ((), ())), preferred_element_type=jnp.float32
    )


def local(
    tokens,
    cotangent,
    lengths,
    owners,
    first_gain,
    first_bias,
    joint_weight,
    joint_bias,
    output_weight,
    output_bias,
    second_gain,
    second_bias,
    up_weight,
    up_bias,
    down_weight,
    down_bias,
):
    row_count = tokens.shape[0]
    score_scale = HEAD ** (-0.5)
    device = lax.axis_index(("rep", "shard"))
    segment, position = layout(lengths, owners, device, row_count)
    places = jnp.arange(row_count, dtype=jnp.int32)
    allowed = (segment[:, None] == segment[None, :]) & (places[None, :] <= places[:, None])
    gain_one, shift_one, joint_full, joint_offset, output_full, output_offset = (
        lax.all_gather(first_gain, "shard", axis=0, tiled=True),
        lax.all_gather(first_bias, "shard", axis=0, tiled=True),
        lax.all_gather(joint_weight, "shard", axis=0, tiled=True),
        lax.all_gather(joint_bias, "shard", axis=0, tiled=True),
        lax.all_gather(output_weight, "shard", axis=0, tiled=True),
        lax.all_gather(output_bias, "shard", axis=0, tiled=True),
    )
    gain_two, shift_two, up_full, up_offset, down_full, down_offset = (
        lax.all_gather(second_gain, "shard", axis=0, tiled=True),
        lax.all_gather(second_bias, "shard", axis=0, tiled=True),
        lax.all_gather(up_weight, "shard", axis=0, tiled=True),
        lax.all_gather(up_bias, "shard", axis=0, tiled=True),
        lax.all_gather(down_weight, "shard", axis=0, tiled=True),
        lax.all_gather(down_bias, "shard", axis=0, tiled=True),
    )
    values = tokens.astype(jnp.float32)
    normed_one, hidden_one = normalize(
        values, gain_one.astype(jnp.float32), shift_one.astype(jnp.float32)
    )
    input_one = hidden_one.astype(jnp.bfloat16)
    projected = jnp.dot(
        input_one, joint_full, preferred_element_type=jnp.float32
    ) + joint_offset.astype(jnp.float32)
    heads_view = projected.reshape(row_count, 3, HEADS, HEAD)
    query_low = rotate(heads_view[:, 0], position, 1.0).astype(jnp.bfloat16)
    keys_low = rotate(heads_view[:, 1], position, 1.0).astype(jnp.bfloat16)
    value_low = heads_view[:, 2].astype(jnp.bfloat16)
    masked = jnp.where(
        allowed[None],
        jnp.einsum("qhd,khd->hqk", query_low, keys_low, preferred_element_type=jnp.float32)
        * score_scale,
        -1e30,
    )
    row_peak = jnp.max(masked, axis=-1, keepdims=True)
    logsum = row_peak + jnp.log(jnp.sum(jnp.exp(masked - row_peak), axis=-1, keepdims=True))
    probs_low = jnp.exp(masked - logsum).astype(jnp.bfloat16)
    mixed_low = (
        jnp.einsum("hqk,khd->qhd", probs_low, value_low, preferred_element_type=jnp.float32)
        .reshape(row_count, D)
        .astype(jnp.bfloat16)
    )
    attention = jnp.dot(
        mixed_low, output_full, preferred_element_type=jnp.float32
    ) + output_offset.astype(jnp.float32)
    normed_two, hidden_two = normalize(
        values, gain_two.astype(jnp.float32), shift_two.astype(jnp.float32)
    )
    input_two = hidden_two.astype(jnp.bfloat16)
    before = jnp.dot(input_two, up_full, preferred_element_type=jnp.float32) + up_offset.astype(
        jnp.float32
    )
    active_low = jax.nn.gelu(before, approximate=False).astype(jnp.bfloat16)
    feed_out = jnp.dot(
        active_low, down_full, preferred_element_type=jnp.float32
    ) + down_offset.astype(jnp.float32)
    result = (values + attention + feed_out).astype(jnp.bfloat16)
    back_one = (
        lax.all_gather(first_gain, "shard", axis=0, tiled=True),
        lax.all_gather(joint_weight, "shard", axis=0, tiled=True),
        lax.all_gather(output_weight, "shard", axis=0, tiled=True),
    )
    back_two = (
        lax.all_gather(second_gain, "shard", axis=0, tiled=True),
        lax.all_gather(up_weight, "shard", axis=0, tiled=True),
        lax.all_gather(down_weight, "shard", axis=0, tiled=True),
    )
    gain_back_one, joint_back, output_back = back_one
    gain_back_two, up_back, down_back = back_two
    grad_out = cotangent.astype(jnp.float32)
    down_weight_grad = contract_rows(active_low, cotangent)
    down_bias_grad = jnp.sum(grad_out, axis=0)
    grad_active = across(cotangent, down_back)
    gelu_exact = partial(jax.nn.gelu, approximate=False)
    grad_before = jax.vjp(gelu_exact, before)[1](grad_active)[0].astype(jnp.bfloat16)
    up_weight_grad = contract_rows(input_two, grad_before)
    up_bias_grad = jnp.sum(grad_before.astype(jnp.float32), axis=0)
    gain_two_grad, shift_two_grad, grad_from_two = norm_back(
        across(grad_before, up_back), normed_two, gain_back_two.astype(jnp.float32), values
    )
    output_weight_grad = contract_rows(mixed_low, cotangent)
    grad_mixed = across(cotangent, output_back).astype(jnp.bfloat16).reshape(row_count, HEADS, HEAD)
    masked_again = jnp.where(
        allowed[None],
        jnp.einsum("qhd,khd->hqk", query_low, keys_low, preferred_element_type=jnp.float32)
        * score_scale,
        -1e30,
    )
    prob_back = jnp.exp(masked_again - logsum)
    prob_back_low = prob_back.astype(jnp.bfloat16)
    grad_probs = jnp.einsum(
        "qhd,khd->hqk", grad_mixed, value_low, preferred_element_type=jnp.float32
    )
    grad_value = jnp.einsum(
        "hqk,qhd->khd", prob_back_low, grad_mixed, preferred_element_type=jnp.float32
    )
    spread = jnp.sum(grad_probs * prob_back, axis=-1, keepdims=True)
    grad_scores = (prob_back * (grad_probs - spread)).astype(jnp.bfloat16)
    grad_query = rotate(
        jnp.einsum("hqk,khd->qhd", grad_scores, keys_low, preferred_element_type=jnp.float32)
        * score_scale,
        position,
        -1.0,
    )
    grad_keys = rotate(
        jnp.einsum("hqk,qhd->khd", grad_scores, query_low, preferred_element_type=jnp.float32)
        * score_scale,
        position,
        -1.0,
    )
    grad_joint = (
        jnp.stack([grad_query, grad_keys, grad_value], axis=1)
        .reshape(row_count, 3 * D)
        .astype(jnp.bfloat16)
    )
    joint_weight_grad = contract_rows(input_one, grad_joint)
    joint_bias_grad = jnp.sum(grad_joint.astype(jnp.float32), axis=0)
    gain_one_grad, shift_one_grad, grad_from_one = norm_back(
        across(grad_joint, joint_back), normed_one, gain_back_one.astype(jnp.float32), values
    )
    grad_tokens = grad_out + grad_from_one + grad_from_two
    group_shares = (
        lax.psum_scatter(gain_one_grad, "shard", scatter_dimension=0, tiled=True),
        lax.psum_scatter(shift_one_grad, "shard", scatter_dimension=0, tiled=True),
        lax.psum_scatter(joint_weight_grad, "shard", scatter_dimension=0, tiled=True),
        lax.psum_scatter(joint_bias_grad, "shard", scatter_dimension=0, tiled=True),
        lax.psum_scatter(output_weight_grad, "shard", scatter_dimension=0, tiled=True),
        lax.psum_scatter(down_bias_grad, "shard", scatter_dimension=0, tiled=True),
        lax.psum_scatter(gain_two_grad, "shard", scatter_dimension=0, tiled=True),
        lax.psum_scatter(shift_two_grad, "shard", scatter_dimension=0, tiled=True),
        lax.psum_scatter(up_weight_grad, "shard", scatter_dimension=0, tiled=True),
        lax.psum_scatter(up_bias_grad, "shard", scatter_dimension=0, tiled=True),
        lax.psum_scatter(down_weight_grad, "shard", scatter_dimension=0, tiled=True),
        lax.psum_scatter(down_bias_grad, "shard", scatter_dimension=0, tiled=True),
    )
    (
        share_gain_one,
        share_shift_one,
        share_joint_weight,
        share_joint_bias,
        share_output_weight,
        share_output_bias,
        share_gain_two,
        share_shift_two,
        share_up_weight,
        share_up_bias,
        share_down_weight,
        share_down_bias,
    ) = group_shares
    owned = lax.psum(
        (
            share_gain_one,
            share_shift_one,
            share_joint_weight,
            share_joint_bias,
            share_output_weight,
            share_output_bias,
            share_gain_two,
            share_shift_two,
            share_up_weight,
            share_up_bias,
            share_down_weight,
            share_down_bias,
        ),
        "rep",
    )
    return (
        result,
        grad_tokens,
        owned[0],
        owned[1],
        owned[2],
        owned[3],
        owned[4],
        owned[5],
        owned[6],
        owned[7],
        owned[8],
        owned[9],
        owned[10],
        owned[11],
    )


PAIR = [(0, 1), (1, 0)]
BLOCKS = 8
LANE = 128
EXTRA = 16
GROUP = ("o", "p", "q", "c")
VMEM_BYTES = 58 * 1024 * 1024


def swap(values, *axes):
    if len(axes) == 1:
        return lax.ppermute(values, axes[0], PAIR)
    return lax.ppermute(values, axes, [(i, 3 - i) for i in range(4)])


def join(own, other, at, axis=0):
    first = at == 0
    return jnp.concatenate(
        [jnp.where(first, own, other), jnp.where(first, other, own)], axis=axis
    )


def pin(*values):
    return lax.optimization_barrier(values)


def take(values, at, axis=0):
    return lax.dynamic_index_in_dim(values, at, axis, keepdims=False)


def low(values):
    return values.astype(jnp.bfloat16)


def wide(values):
    return values.astype(jnp.float32)


def times(left, right):
    return jnp.dot(left, right, preferred_element_type=jnp.float32)


def places_of(ids_ref):
    return tuple(ids_ref[i] for i in range(5))


def call(kernel, outs, scratch, micros, *operands, memory):
    whole = pl.BlockSpec(memory_space=pltpu.VMEM)
    specs = {
        "s": pl.BlockSpec(memory_space=pltpu.SMEM),
        "v": whole,
        "h": pl.BlockSpec(memory_space=pl.ANY),
    }
    size = sum(leaf.size * leaf.dtype.itemsize for leaf in (*operands, *outs))
    return pl.pallas_call(
        kernel,
        out_shape=tuple(outs),
        in_specs=[specs[kind] for kind in memory],
        out_specs=tuple(whole for _ in outs),
        scratch_shapes=scratch,
        compiler_params=pltpu.CompilerParams(vmem_limit_bytes=VMEM_BYTES),
        cost_estimate=pl.CostEstimate(
            flops=int(micros * 1.15e9), bytes_accessed=size, transcendentals=0
        ),
    )(*operands)


def fetch(pairs, sems):
    copies = [
        pltpu.make_async_copy(source, target, sems.at[i])
        for i, (source, target) in enumerate(pairs)
    ]
    for copy in copies:
        copy.start()
    return copies


def finish(copies):
    for copy in copies:
        copy.wait()


def sheet_pairs(pieces, target, small, places):
    x, o, p, q, c = places
    pairs = []
    for index, piece in enumerate(pieces):
        jo, jq = index // 2, index % 2
        rows = piece.shape[1] if small is None else piece.shape[1] - EXTRA
        for k in range(4):
            jc, jp = k // 2, k % 2
            shard = (((o ^ jo) * 2 + (p ^ jp)) * 2 + (q ^ jq)) * 2 + (c ^ jc)
            if target is not None:
                at = pl.multiple_of(shard * rows, rows)
                pairs.append((piece.at[k, pl.ds(0, rows)], target.at[pl.ds(at, rows)]))
            if small is not None:
                at = pl.multiple_of(shard * EXTRA, EXTRA)
                pairs.append((piece.at[k, pl.ds(rows, EXTRA)], small.at[pl.ds(at, EXTRA)]))
    return pairs


def vector_of(small, start, size=HEAD, row=0):
    parts = [
        wide(small[shard * EXTRA : (shard + 1) * EXTRA, start + at : start + at + HEAD])[row : row + 1]
        for shard in range(16)
        for at in range(0, size, HEAD)
    ]
    pairs = [jnp.concatenate(parts[i : i + 2], axis=1) for i in range(0, len(parts), 2)]
    return jnp.concatenate(pairs, axis=1)


def tall_pairs(pieces, target, places):
    x, o, p, q, c = places
    pairs = []
    for index, piece in enumerate(pieces):
        jo, jq = index // 2, index % 2
        rows = piece.shape[0]
        at = ((o ^ jo) * 2 + (q ^ jq)) * rows
        pairs.append((piece, target.at[pl.ds(pl.multiple_of(at, rows), rows)]))
    return pairs


def norm_of(tokens):
    values = wide(tokens)
    centre = values - jnp.mean(values, axis=-1, keepdims=True)
    return centre * lax.rsqrt(jnp.mean(centre * centre, axis=-1, keepdims=True) + EPSILON)


def fold(values):
    rows, columns = values.shape
    return jnp.sum(values.reshape(rows // 8, 8, columns), axis=0)


def cut_kernel(ids, joint, up, small, keep, send):
    x, o, p, q, c = places_of(ids)
    parts = joint.shape[1] // D
    height = joint.shape[0]
    first = parts * LANE
    columns = small.shape[1] - first
    ours = jnp.concatenate([small[:, :first], small[:, : columns - first]], axis=1)
    upper = lax.broadcasted_iota(jnp.int32, (EXTRA, columns), 0) < EXTRA // 2
    vectors = low(jnp.where(upper, wide(small[:, first:]), wide(ours)))

    def block(ref, index):
        return ref[:, pl.ds(pl.multiple_of(index * LANE, LANE), LANE)]

    for jp, target in ((0, keep), (1, send)):
        for jc in (0, 1):
            pp, cc = p ^ jp, c ^ jc
            target[jc, height:, :first] = jnp.broadcast_to(small[:, :first], (EXTRA, first))
            target[jc, height:, first:] = vectors
            for part in range(parts):
                target[jc, :height, part * LANE : (part + 1) * LANE] = block(
                    joint, part * 8 + x * 4 + pp * 2 + cc
                )
            for k in range(4):
                oo, qq = k // 2, k % 2
                at = (parts + k) * LANE
                target[jc, :height, at : at + LANE] = block(
                    up, (((oo * 2 + pp) * 2 + qq) * 2 + cc) * 2 + x
                )


def turner(cap):
    lane = lax.broadcasted_iota(jnp.int32, (cap, LANE), 1)
    lead = lane % HEAD < ROT // 2

    def turn(values, cos_part, sin_part):
        other = jnp.where(
            lead, pltpu.roll(values, LANE - ROT // 2, 1), pltpu.roll(values, ROT // 2, 1)
        )
        return values * cos_part + other * sin_part

    return turn, (lane < HEAD, lane >= HEAD)


def block_pairs(sources, tokens, cotangent):
    cap = sources[0].shape[1]
    return [
        (source.at[2 * k + which], target.at[pl.ds((2 * i + k) * cap, cap)])
        for i, source in enumerate(sources)
        for k in (0, 1)
        for which, target in enumerate((tokens, cotangent))
        if target is not None
    ]


def both_ways(step, near_out, far_out, size):
    for i in (0, 1):
        near_out[i * size : (i + 1) * size, :] = step(2 * i)
    for i in (0, 1):
        far_out[i * size : (i + 1) * size, :] = low(step(2 * i + 1))


def attention_kernel(
    ids,
    block_0,
    block_1,
    block_2,
    block_3,
    sheet_0,
    sheet_1,
    sheet_2,
    sheet_3,
    extra_0,
    extra_1,
    extra_2,
    extra_3,
    output_weight,
    fed,
    cosine,
    sine,
    position,
    near_out,
    far_out,
    grad_ref,
    home_0,
    home_1,
    away,
    output_grad,
    grad_sum,
    tokens,
    cotangent,
    joint,
    inputs,
    mixed_all,
    total,
    small,
    gain,
    shift,
    offset,
    sems,
):
    x, o, p, q, c = places_of(ids)
    cap = block_0.shape[1]
    finish(
        fetch(
            sheet_pairs((sheet_0, sheet_1, sheet_2, sheet_3), joint, None, places_of(ids))
            + sheet_pairs((extra_0, extra_1, extra_2, extra_3), None, small, places_of(ids))
            + block_pairs((block_0, block_1, block_2, block_3), tokens, cotangent),
            sems,
        )
    )
    row = EXTRA // 2
    gain[...] = vector_of(small, 0, row=row)
    shift[...] = vector_of(small, HEAD, row=row)
    offset[...] = vector_of(small, 2 * HEAD, 3 * HEAD, row)
    starts = [pl.multiple_of((part * 8 + x * 4 + p * 2 + c) * LANE, LANE) for part in range(3)]
    bias = jnp.concatenate([offset[:, pl.ds(at, LANE)] for at in starts], axis=1)
    total[...] = jnp.zeros_like(total)
    turn, mine = turner(2 * cap)
    own = mine[0][:cap]
    down = lax.broadcasted_iota(jnp.int32, (cap, cap), 0)
    along = lax.broadcasted_iota(jnp.int32, (cap, cap), 1)
    scale = HEAD ** (-0.5)

    def by_head(values):
        none = jnp.zeros_like(values)
        return jnp.concatenate([jnp.where(own, values, none), jnp.where(own, none, values)])

    def attend(query, keys, value, grad_mixed, place):
        allowed = ((along <= down) & (along >= down - place))[None]
        query_two, grad_two = by_head(query), by_head(grad_mixed)
        scores = across(query_two, keys).reshape(2, cap, cap) * scale
        scores = jnp.where(allowed, scores, -1e30)
        raised = jnp.exp(scores - jnp.max(scores, axis=-1, keepdims=True))
        probs = raised / jnp.sum(raised, axis=-1, keepdims=True)
        probs_low = low(probs).reshape(2 * cap, cap)
        grad_probs = across(grad_two, value).reshape(2, cap, cap)
        spread = jnp.sum(grad_probs * probs, axis=-1, keepdims=True)
        grad_scores = low(probs * (grad_probs - spread)).reshape(2 * cap, cap)
        mixed = times(probs_low, value)
        grad_query = times(grad_scores, keys)
        return (
            jnp.where(own, mixed[:cap], mixed[cap:]),
            jnp.where(own, grad_query[:cap], grad_query[cap:]) * scale,
            contract_rows(grad_scores, query_two) * scale,
            contract_rows(probs_low, grad_two),
        )

    def step(pair):
        rows = slice(pair * 2 * cap, (pair + 1) * 2 * cap)
        input_low = low(norm_of(tokens[rows, :]) * gain[...] + shift[...])
        inputs[rows, :] = input_low
        projected = times(input_low, joint[...]) + bias
        cos_part, sin_part = cosine[rows, :], sine[rows, :]
        query = low(turn(projected[:, :LANE], cos_part, sin_part))
        keys = low(turn(projected[:, LANE : 2 * LANE], cos_part, sin_part))
        value = low(projected[:, 2 * LANE :])
        grad_mixed = low(across(cotangent[rows, :], output_weight[...]))
        place = position[rows, :]
        found = [
            attend(query[at], keys[at], value[at], grad_mixed[at], place[at, :1])
            for at in (slice(0, cap), slice(cap, 2 * cap))
        ]
        mixed, grad_query, grad_keys, grad_value = (jnp.concatenate(both) for both in zip(*found))
        mixed = low(mixed)
        mixed_all[rows, :] = mixed
        grad_joint = low(
            jnp.concatenate(
                [
                    turn(grad_query, cos_part, -sin_part),
                    turn(grad_keys, cos_part, -sin_part),
                    grad_value,
                ],
                axis=1,
            )
        )
        grad_ref[rows, :] = grad_joint
        total[...] += fold(wide(grad_joint))
        return times(mixed, output_weight[...]) + wide(fed[rows, :])

    both_ways(step, near_out, far_out, 2 * cap)
    grad_sum[...] = jnp.sum(total[...], axis=0, keepdims=True)
    output_grad[...] = low(contract_rows(mixed_all[...], cotangent[...]))
    half = away.shape[0] // 2
    here = home_0, away.at[pl.ds(0, half)]
    there = home_1, away.at[pl.ds(half, half)]
    sheet_grads(inputs, grad_ref, here, there, 0, places_of(ids))


def for_place(at, here, there, store):
    pl.when(at)(lambda: store(*here))
    pl.when(jnp.logical_not(at))(lambda: store(*there))


def sheet_grads(inputs, grads, here, there, base, places):
    x, o, p, q, c = places
    columns = grads.shape[1]
    rows = D // 16
    for oo in (0, 1):
        found = contract_rows(inputs[:, oo * D // 2 : (oo + 1) * D // 2], grads[...])
        found = low(found).reshape(2, 2, 2, rows, columns)

        def store(home, away, found=found):
            for pp in (0, 1):
                for cc in (0, 1):
                    down = pl.ds(pl.multiple_of(base + (p ^ pp) * rows, rows), rows)
                    along = pl.ds(pl.multiple_of((c ^ cc) * columns, LANE), columns)
                    home[down, along] = jnp.where(q == 0, found[pp, 0, cc], found[pp, 1, cc])
                    away[down, along] = jnp.where(q == 0, found[pp, 1, cc], found[pp, 0, cc])

        for_place(o == oo, here, there, store)


def feed_kernel(
    ids,
    block_0,
    block_1,
    block_2,
    block_3,
    sheet_0,
    sheet_1,
    sheet_2,
    sheet_3,
    tall_0,
    tall_1,
    tall_2,
    tall_3,
    fed,
    late_offset,
    grad_all,
    home_0,
    home_1,
    away_0,
    away_1,
    grad_sum,
    tokens,
    cotangent,
    up,
    down,
    inputs,
    active_all,
    total,
    small,
    gain,
    shift,
    sems,
):
    places = places_of(ids)
    x, o, p, q, c = places
    cap = block_0.shape[1]
    finish(
        fetch(
            sheet_pairs((sheet_0, sheet_1, sheet_2, sheet_3), up, small, places)
            + block_pairs((block_0, block_1, block_2, block_3), tokens, cotangent)
            + tall_pairs((tall_0, tall_1, tall_2, tall_3), down, places),
            sems,
        )
    )
    gain[...] = vector_of(small, 0)
    shift[...] = vector_of(small, HEAD)
    width = 4 * LANE
    late_offset[...] = vector_of(small, width - 2 * HEAD) + vector_of(small, width - HEAD)
    along = pl.ds(pl.multiple_of((x + 1) * LANE, LANE), LANE)
    bias = [
        small[pl.ds(pl.multiple_of((((oo * 2 + p) * 2 + qq) * 2 + c) * EXTRA, EXTRA), EXTRA), along]
        for oo in (0, 1)
        for qq in (0, 1)
    ]
    bias = wide(jnp.concatenate(bias, axis=1))[:1]
    total[...] = jnp.zeros_like(total)

    for pair in range(BLOCKS // 2):
        rows = slice(pair * 2 * cap, (pair + 1) * 2 * cap)
        input_low = low(norm_of(tokens[rows, :]) * gain[...] + shift[...])
        inputs[rows, :] = input_low
        before = times(input_low, up[...]) + bias
        slope = 0.5 + 0.5 * lax.erf(before * 0.5**0.5)
        active = low(before * slope)
        active_all[rows, :] = active
        slope = slope + before * jnp.exp(-0.5 * before * before) * (0.5 / jnp.pi) ** 0.5
        grad_before = low(across(cotangent[rows, :], down[...]) * slope)
        grad_all[rows, :] = grad_before
        total[...] += fold(wide(grad_before))
        fed[rows, :] = low(times(active, down[...]))

    grad_sum[...] = jnp.sum(total[...], axis=0, keepdims=True)
    unit = home_0.shape[0] // 2
    here, there = (home_0, away_0), (home_1, away_1)
    for oo in (0, 1):
        found = low(contract_rows(active_all[:, oo * 2 * unit : (oo + 1) * 2 * unit], cotangent[...]))

        def store(home, away, found=found):
            home[:unit, :] = jnp.where(q == 0, found[:unit], found[unit:])
            away[:unit, :] = jnp.where(q == 0, found[unit:], found[:unit])

        for_place(o == oo, here, there, store)
    sheet_grads(inputs, grad_all, here, there, unit, places)


def pull_kernel(
    ids,
    block_0,
    block_1,
    block_2,
    block_3,
    join_0,
    join_1,
    join_2,
    join_3,
    sheet_0,
    sheet_1,
    sheet_2,
    sheet_3,
    grad_joint,
    grad_before,
    joint_sum,
    up_sum,
    near_out,
    far_out,
    sums,
    tokens,
    joint,
    up,
    totals,
    small,
    gain_one,
    gain_two,
    own,
    sems,
):
    places = places_of(ids)
    x, o, p, q, c = places
    cap = block_0.shape[1]
    finish(
        fetch(
            block_pairs((block_0, block_1, block_2, block_3), tokens, None)
            + sheet_pairs((join_0, join_1, join_2, join_3), joint, None, places)
            + sheet_pairs((sheet_0, sheet_1, sheet_2, sheet_3), up, small, places)
            + [(block_0.at[1], own)],
            sems,
        )
    )
    gain_one[...] = vector_of(small, 0, row=EXTRA // 2)
    gain_two[...] = vector_of(small, 0)
    totals[...] = jnp.zeros_like(totals)

    def step(pair):
        rows = slice(pair * 2 * cap, (pair + 1) * 2 * cap)
        normed = norm_of(tokens[rows, :])
        grad_first = across(grad_joint[rows, :], joint[...])
        grad_second = across(grad_before[rows, :], up[...])
        totals[0] += fold(grad_first * normed)
        totals[1] += fold(grad_first)
        totals[2] += fold(grad_second * normed)
        totals[3] += fold(grad_second)
        return grad_first * gain_one[...] + grad_second * gain_two[...]

    both_ways(step, near_out, far_out, 2 * cap)
    sums[...] = jnp.zeros_like(sums)
    sums[0:4, :] = jnp.sum(totals[...], axis=1)
    sums[4:5, :] = jnp.sum(wide(own[...]), axis=0, keepdims=True)
    at = pl.ds(pl.multiple_of((x * 4 + p * 2 + c) * LANE, LANE), LANE)
    for part in range(3):
        sums[5 + part : 6 + part, at] = joint_sum[:, part * LANE : (part + 1) * LANE]
    for k in range(4):
        at = pl.ds(pl.multiple_of((k % 2 * 4 + c * 2 + x) * LANE, LANE), LANE)
        for pp in (0, 1):
            row = 8 + k // 2 * 2 + pp
            found = up_sum[:, k * LANE : (k + 1) * LANE]
            sums[row : row + 1, at] = jnp.where(p == pp, found, jnp.zeros_like(found))


def final_kernel(
    up_home,
    up_away,
    up_sent,
    joint_home,
    joint_away,
    joint_sent,
    out_0,
    out_1,
    out_2,
    out_3,
    down,
):
    rows = down.shape[0]
    found = low(total(up_home[...], up_away[...], up_sent[...]))
    down[...] = found[:rows]
    found = found[rows:]
    joint = low(total(joint_home[...], joint_away[:rows, :], joint_sent[...]))
    half, width = rows // 2, joint.shape[1] // 2
    hidden = found.shape[1] // 2
    for k, out in enumerate((out_0, out_1, out_2, out_3)):
        jp, jc = k // 2, k % 2
        out[:, :width] = joint[jp * half : (jp + 1) * half, jc * width : (jc + 1) * width]
        out[:, width:] = found[jp * half : (jp + 1) * half, jc * hidden : (jc + 1) * hidden]


def lay_kernel(ids, own, other, joint, up):
    x, o, p, q, c = places_of(ids)
    parts = joint.shape[1] // D
    for xx, source in ((0, own), (1, other)):
        for pp in (0, 1):
            for cc in (0, 1):
                values = wide(source[pp, cc])
                at_x, at_p, at_c = x ^ xx, p ^ pp, c ^ cc
                blocks = [(joint, part * 8 + at_x * 4 + at_p * 2 + at_c) for part in range(parts)]
                blocks += [
                    (up, (((k // 2 * 2 + at_p) * 2 + k % 2) * 2 + at_c) * 2 + at_x) for k in range(4)
                ]
                for k, (out, at) in enumerate(blocks):
                    out[:, pl.ds(pl.multiple_of(at * LANE, LANE), LANE)] = values[
                        :, k * LANE : (k + 1) * LANE
                    ]


def lane_sum(near, came):
    lane = near + wide(came)
    rows = lane.shape[0] // 4
    return lane[:rows], *(low(lane[i * rows : (i + 1) * rows]) for i in (1, 2, 3))


def total(*parts):
    found = wide(parts[0])
    for part in parts[1:]:
        found += wide(part)
    return found


def grouped(
    tokens,
    cotangent,
    lengths,
    owners,
    first_gain,
    first_bias,
    joint_weight,
    joint_bias,
    output_weight,
    output_bias,
    second_gain,
    second_bias,
    up_weight,
    up_bias,
    down_weight,
    down_bias,
):
    x, o, p, q, c = (lax.axis_index(name) for name in ("x", "o", "p", "q", "c"))
    ids = jnp.stack([x, o, p, q, c]).astype(jnp.int32)
    cap = tokens.shape[0]
    rows = BLOCKS * cap
    part = joint_weight.shape[0]
    hidden = up_weight.shape[1] // 8
    unit = hidden // 4
    bf, f32 = jnp.bfloat16, jnp.float32

    def like(shape, kind):
        return jax.ShapeDtypeStruct(shape, kind)

    pair = jnp.stack([tokens, cotangent])
    along_x = swap(pair, "x")

    rest = jnp.zeros((HEAD,), bf)
    small = jnp.concatenate(
        [first_gain, first_bias, joint_bias, rest, second_gain, second_bias, up_bias, output_bias, down_bias]
    )[None]
    down_half = take(down_weight.reshape(2, unit, D), x)
    keep, send = call(
        cut_kernel,
        [
            like((2, part + EXTRA, 3 * LANE + hidden), bf),
            like((2, part + EXTRA, 3 * LANE + hidden), bf),
        ],
        [],
        0,
        ids,
        joint_weight,
        up_weight,
        small,
        memory="svvv",
    )
    came, down_other, down_side = swap(send, "p"), swap(down_half, "o"), swap(down_half, "q")
    along_p = swap(pin(tokens, send)[0], "p")

    came, down_other, down_side, along_x, along_p, lengths = pin(
        came, down_other, down_side, along_x, along_p, lengths
    )

    turn_came, output_came = swap(jnp.concatenate([keep[1:], came[1:]]), "c"), swap(output_weight, "c")
    turn_came, output_came, along_p = pin(turn_came, output_came, along_p)

    turned = jnp.concatenate([keep[:1], came[:1], turn_came])
    first, up_own, joint_own, along_p = pin(
        jnp.concatenate([pair, along_x]),
        turned[:, :, 3 * LANE :],
        turned[:, :part, : 3 * LANE],
        along_p,
    )
    up_other, up_side = swap(up_own, "o"), swap(up_own, "q")
    grad_along_p, along_both = swap(pin(cotangent, along_p)[0], "p"), swap(along_p, "x")
    down_corner = swap(down_other, "q")

    devices = jnp.stack(
        [
            ((((x ^ xx) * 2 + o) * 2 + (p ^ pp)) * 2 + q) * 2 + (c ^ cc)
            for pp in (0, 1)
            for cc in (0, 1)
            for xx in (0, 1)
        ]
    )
    position = jax.vmap(lambda device: layout(lengths, owners, device, cap)[1])(devices)
    position = position.reshape(rows, 1)
    place = jnp.arange(LANE) % HEAD
    half_rot = ROT // 2
    frequency = 10000.0 ** (-jnp.arange(half_rot, dtype=f32) / half_rot)
    angles = position.astype(f32) * jnp.tile(frequency, LANE // half_rot)[None, :]
    position = jnp.broadcast_to(position, (rows, LANE))
    cosine = jnp.where(place < ROT, jnp.cos(angles), 1.0)
    sine = jnp.sin(angles)
    sine = jnp.where(place < half_rot, -sine, jnp.where(place < ROT, sine, 0.0))

    cosine, sine, position, up_other, up_side, grad_along_p, along_both, down_corner, joint_own, first = pin(
        cosine, sine, position, up_other, up_side, grad_along_p, along_both, down_corner, joint_own, first
    )

    up_corner, joint_other = swap(up_other, "q"), swap(joint_own, "o")
    grad_along_both, first_came = swap(grad_along_p, "x"), swap(first, "c")
    turn_over = [
        (((a * 2 + b) * 2 + e) * 2 + f, ((b * 2 + a) * 2 + f) * 2 + e)
        for a in (0, 1)
        for b in (0, 1)
        for e in (0, 1)
        for f in (0, 1)
    ]
    cross = ("x", "o", "q", "c")
    up_corner, first_came, joint_other, grad_along_both, output_pair = pin(
        up_corner, first_came, joint_other, grad_along_both, join(output_weight, output_came, c)
    )
    second = jnp.stack([along_p, grad_along_p, along_both, grad_along_both])
    second_came = swap(second, "c")
    joint_pair, output_pair, second_came = pin(
        jnp.stack([joint_own, joint_other]), output_pair, second_came
    )
    blocks = first, first_came, second, second_came
    up_sheets = up_own, up_side, up_other, up_corner
    down_talls = down_half, down_side, down_other, down_corner
    joint_far = swap(joint_pair, "q")
    output_pair = lax.ppermute(output_pair, cross, turn_over)
    copies = pltpu.SemaphoreType.DMA
    tall = (rows, D)
    found = call(
        feed_kernel,
        [
            like(tall, bf),
            like((1, D), f32),
            like((rows, hidden), bf),
            *(like((2 * unit, D), bf) for _ in range(4)),
            like((1, hidden), f32),
        ],
        [
            pltpu.VMEM(tall, bf),
            pltpu.VMEM(tall, bf),
            pltpu.VMEM((D, hidden), bf),
            pltpu.VMEM((hidden, D), bf),
            pltpu.VMEM(tall, bf),
            pltpu.VMEM((rows, hidden), bf),
            pltpu.VMEM((8, hidden), f32),
            pltpu.VMEM((16 * EXTRA, hidden), bf),
            pltpu.VMEM((1, D), f32),
            pltpu.VMEM((1, D), f32),
            copies((52,)),
        ],
        20,
        ids,
        *blocks,
        *up_sheets,
        *down_talls,
        memory="shhhhhhhhhhhh",
    )
    joint_far, output_pair, *found = pin(joint_far, output_pair, *found)
    joint_sheets = joint_own, joint_far[0], joint_other, joint_far[1]
    fed, late_offset, grad_before, up_home_0, up_home_1, up_away_0, up_away_1, up_sum = found
    up_away_1 = swap(up_away_1, "q")

    found = call(
        attention_kernel,
        [
            like((rows // 2, D), f32),
            like((rows // 2, D), bf),
            like((rows, 3 * LANE), bf),
            like((2 * part, 6 * LANE), bf),
            like((2 * part, 6 * LANE), bf),
            like((4 * part, 6 * LANE), bf),
            like((LANE, D), bf),
            like((1, 3 * LANE), f32),
        ],
        [
            pltpu.VMEM(tall, bf),
            pltpu.VMEM(tall, bf),
            pltpu.VMEM((D, 3 * LANE), bf),
            pltpu.VMEM(tall, bf),
            pltpu.VMEM((rows, LANE), bf),
            pltpu.VMEM((8, 3 * LANE), f32),
            pltpu.VMEM((16 * EXTRA, hidden), bf),
            pltpu.VMEM((1, D), f32),
            pltpu.VMEM((1, D), f32),
            pltpu.VMEM((1, 3 * D), f32),
            copies((48,)),
        ],
        22,
        ids,
        *blocks,
        *joint_sheets,
        *up_sheets,
        output_pair,
        fed,
        cosine,
        sine,
        position,
        memory="shhhhhhhhhhhhvvvvv",
    )
    up_away_1, up_away_0, *found = pin(up_away_1, up_away_0, *found)
    near_part, far_part, grad_joint, joint_home_0, joint_home_1, joint_away, output_grad, joint_sum = found

    def lane_sum(near, came, block):
        at = slice(block * cap, (block + 1) * cap)
        return near[at] + wide(came[at])

    up_sent = swap(low(total(up_home_1, up_away_1)), "o")
    joint_away, up_away_0 = swap(joint_away, "q"), swap(up_away_0, "q")
    result_lane = near_part, swap(far_part, "c")
    result_sent, grad_joint = pin(
        low(jnp.concatenate([lane_sum(*result_lane, 1), lane_sum(*result_lane, 3)])), grad_joint
    )
    result_came = swap(result_sent, "x")
    output_part = lax.ppermute(output_grad, cross, turn_over)
    found = call(
        pull_kernel,
        [like((rows // 2, D), f32), like((rows // 2, D), bf), like((16, D), f32)],
        [
            pltpu.VMEM(tall, bf),
            pltpu.VMEM((D, 3 * LANE), bf),
            pltpu.VMEM((D, hidden), bf),
            pltpu.VMEM((4, 8, D), f32),
            pltpu.VMEM((16 * EXTRA, hidden), bf),
            pltpu.VMEM((1, D), f32),
            pltpu.VMEM((1, D), f32),
            pltpu.VMEM((cap, D), bf),
            copies((73,)),
        ],
        11,
        ids,
        *blocks,
        *joint_sheets,
        *up_sheets,
        grad_joint,
        grad_before,
        joint_sum,
        up_sum,
        memory="shhhhhhhhhhhhvvvv",
    )
    up_sent, up_away_0, joint_away, result_came, output_part, *found = pin(
        up_sent, up_away_0, joint_away, result_came, output_part, *found
    )
    near_part, far_part, sums = found
    came, sums_came = swap(far_part, "c"), swap(sums, "c")
    output_part = output_part.reshape(2, part, D)

    joint_sent, came, sums_came = pin(
        low(total(joint_home_1, joint_away[2 * part :])),
        came,
        sums_came,
    )

    lane = near_part, came
    sums, *sent = pin(sums + sums_came, *(low(lane_sum(*lane, i)) for i in (1, 2, 3)))
    side, far_side, corner = swap(sent[0], "x"), swap(sent[1], "p"), swap(sent[2], "x", "p")
    joint_sent = swap(joint_sent, "o")
    sums = sums + swap(sums, "x")
    sums = sums + swap(sums, "q")
    side, far_side, corner, joint_sent, output_part, result_came, sums = pin(
        side, far_side, corner, joint_sent, output_part, result_came, sums
    )
    output_sent = take(output_part, 1 - c)
    result_kept = lane_sum(*result_lane, 0) + wide(result_came[:cap])
    result_sent = low(lane_sum(*result_lane, 2) + wide(result_came[cap:]))

    *final, down_final = call(
        final_kernel,
        [*(like((part, 3 * LANE + hidden), bf) for _ in range(4)), like((unit, D), bf)],
        [],
        1,
        up_home_0,
        up_away_0,
        up_sent,
        joint_home_0,
        joint_away,
        joint_sent,
        memory="vvvvvv",
    )
    *final, down_final, sums = pin(*final, down_final, sums)
    sent = swap(final[1], "c"), swap(final[2], "p"), swap(final[3], "p", "c")
    down_came, sums_came, output_sent = swap(down_final, "x"), swap(sums, "p"), swap(output_sent, "c")
    pulled = lane_sum(*lane, 0) + wide(side[:cap]) + wide(far_side[:cap]) + wide(corner[:cap])
    *sent, down_came, sums_came, output_sent = pin(*sent, down_came, sums_came, output_sent)

    both, sums, output_own, result_sent = pin(
        jnp.stack([final[0], *sent]).reshape(2, 2, part, -1),
        sums + sums_came,
        low(total(take(output_part, c), output_sent)),
        result_sent,
    )
    both_came, output_came = swap(both, "x"), swap(output_own, "x")
    result_came = swap(result_sent, "p")
    sums = sums + swap(sums, "o")
    shard = ((o * 2 + p) * 2 + q) * 2 + c

    def own_part(values):
        size = values.size // 16
        return lax.dynamic_slice_in_dim(values.reshape(-1), shard * size, size)

    output_own = total(output_own, output_came)
    down_own = wide(join(down_final, down_came, x))
    joint_own_grad, up_own_grad = call(
        lay_kernel,
        [like((part, 3 * D), f32), like((part, up_weight.shape[1]), f32)],
        [],
        1,
        ids,
        both,
        both_came,
        memory="svv",
    )

    own_values = wide(tokens)
    own_normed = norm_of(tokens)
    centre = own_values - jnp.mean(own_values, axis=-1, keepdims=True)
    factor = lax.rsqrt(jnp.mean(centre * centre, axis=-1, keepdims=True) + EPSILON)
    grad_tokens = wide(cotangent) + factor * (
        pulled
        - jnp.mean(pulled, axis=-1, keepdims=True)
        - own_normed * jnp.mean(pulled * own_normed, axis=-1, keepdims=True)
    )
    grad_tokens, result_came = pin(grad_tokens, result_came)
    result = low(own_values + total(result_kept, result_came) + late_offset)
    norm_grads = [own_part(sums[i]) for i in range(5)]
    return (
        result,
        grad_tokens,
        norm_grads[0],
        norm_grads[1],
        joint_own_grad,
        own_part(sums[5:8]),
        output_own,
        norm_grads[4],
        norm_grads[2],
        norm_grads[3],
        up_own_grad,
        own_part(sums[8:12]),
        down_own,
        norm_grads[4],
    )


def solution(mesh):
    if mesh.shape["rep"] == 2 and mesh.shape["shard"] * HEAD == D:
        work, body = Mesh(mesh.devices.reshape(2, 2, 2, 2, 2), ("x", *GROUP)), grouped
        group, every = GROUP, ("x", *GROUP)
    else:
        work, body = mesh, local
        group, every = "shard", ("rep", "shard")
    row, vec, mat = P(every, None), P(group), P(group, None)
    return jax.shard_map(
        body,
        mesh=work,
        in_specs=(row, row, P(), P(), vec, vec, mat, vec, mat, vec, vec, vec, mat, vec, mat, vec),
        out_specs=(row, row, vec, vec, mat, vec, mat, vec, vec, vec, mat, vec, mat, vec),
        check_vma=False,
    )
```

```python
from functools import partial

import jax
import jax.numpy as jnp
from jax import lax
from jax.experimental import pallas as pl
from jax.experimental.pallas import tpu as pltpu
from jax.sharding import Mesh, PartitionSpec as P

D = 1024
HEADS = 16
HEAD = 64
ROT = 16


EPSILON = 1e-05


def layout(lengths, owners, device, row_count):
    owned = owners == device
    own_lengths = jnp.where(owned, lengths, 0)
    end_points = jnp.cumsum(own_lengths, dtype=jnp.int32)
    filled = jnp.sum(own_lengths, dtype=jnp.int32)
    places = jnp.arange(row_count, dtype=jnp.int32)
    passed = end_points[None, :] <= places[:, None]
    before_count = jnp.sum(passed.astype(jnp.int32), axis=1, dtype=jnp.int32)
    seq_start = jnp.max(jnp.where(passed, end_points[None, :], 0), axis=1)
    filled_row = places < filled
    seq_total = lengths.shape[0]
    segment = jnp.where(filled_row, before_count, seq_total + places)
    position = jnp.where(filled_row, places - seq_start, 0)
    return (segment, position)


def rotate(vectors, position, direction):
    half_rot = ROT // 2
    frequency = 10000.0 ** (-jnp.arange(half_rot, dtype=jnp.float32) / half_rot)
    angles = position.astype(jnp.float32)[:, None] * frequency[None, :]
    cosine = jnp.cos(angles)[:, None, :]
    sine_part = direction * jnp.sin(angles)[:, None, :]
    lead_part = vectors[..., :half_rot]
    trail_part = vectors[..., half_rot:ROT]
    turned_lead = lead_part * cosine - trail_part * sine_part
    turned_trail = trail_part * cosine + lead_part * sine_part
    return jnp.concatenate([turned_lead, turned_trail, vectors[..., ROT:]], axis=-1)


def normalize(values, gain, shift):
    centre = values - jnp.mean(values, axis=-1, keepdims=True)
    normed = centre * lax.rsqrt(jnp.mean(centre * centre, axis=-1, keepdims=True) + EPSILON)
    return (normed, normed * gain + shift)


def norm_back(grad_hidden, normed, gain, values):
    gain_grad = jnp.sum(grad_hidden * normed, axis=0)
    shift_grad = jnp.sum(grad_hidden, axis=0)
    grad_normed = grad_hidden * gain
    centre = values - jnp.mean(values, axis=-1, keepdims=True)
    factor = lax.rsqrt(jnp.mean(centre * centre, axis=-1, keepdims=True) + EPSILON)
    grad_values = factor * (
        grad_normed
        - jnp.mean(grad_normed, axis=-1, keepdims=True)
        - normed * jnp.mean(grad_normed * normed, axis=-1, keepdims=True)
    )
    return (gain_grad, shift_grad, grad_values)


def contract_rows(left, right):
    return lax.dot_general(
        left, right, (((0,), (0,)), ((), ())), preferred_element_type=jnp.float32
    )


def across(left, right):
    return lax.dot_general(
        left, right, (((1,), (1,)), ((), ())), preferred_element_type=jnp.float32
    )


def local(
    tokens,
    cotangent,
    lengths,
    owners,
    first_gain,
    first_bias,
    joint_weight,
    joint_bias,
    output_weight,
    output_bias,
    second_gain,
    second_bias,
    up_weight,
    up_bias,
    down_weight,
    down_bias,
):
    row_count = tokens.shape[0]
    score_scale = HEAD ** (-0.5)
    device = lax.axis_index(("rep", "shard"))
    segment, position = layout(lengths, owners, device, row_count)
    places = jnp.arange(row_count, dtype=jnp.int32)
    allowed = (segment[:, None] == segment[None, :]) & (places[None, :] <= places[:, None])
    gain_one, shift_one, joint_full, joint_offset, output_full, output_offset = (
        lax.all_gather(first_gain, "shard", axis=0, tiled=True),
        lax.all_gather(first_bias, "shard", axis=0, tiled=True),
        lax.all_gather(joint_weight, "shard", axis=0, tiled=True),
        lax.all_gather(joint_bias, "shard", axis=0, tiled=True),
        lax.all_gather(output_weight, "shard", axis=0, tiled=True),
        lax.all_gather(output_bias, "shard", axis=0, tiled=True),
    )
    gain_two, shift_two, up_full, up_offset, down_full, down_offset = (
        lax.all_gather(second_gain, "shard", axis=0, tiled=True),
        lax.all_gather(second_bias, "shard", axis=0, tiled=True),
        lax.all_gather(up_weight, "shard", axis=0, tiled=True),
        lax.all_gather(up_bias, "shard", axis=0, tiled=True),
        lax.all_gather(down_weight, "shard", axis=0, tiled=True),
        lax.all_gather(down_bias, "shard", axis=0, tiled=True),
    )
    values = tokens.astype(jnp.float32)
    normed_one, hidden_one = normalize(
        values, gain_one.astype(jnp.float32), shift_one.astype(jnp.float32)
    )
    input_one = hidden_one.astype(jnp.bfloat16)
    projected = jnp.dot(
        input_one, joint_full, preferred_element_type=jnp.float32
    ) + joint_offset.astype(jnp.float32)
    heads_view = projected.reshape(row_count, 3, HEADS, HEAD)
    query_low = rotate(heads_view[:, 0], position, 1.0).astype(jnp.bfloat16)
    keys_low = rotate(heads_view[:, 1], position, 1.0).astype(jnp.bfloat16)
    value_low = heads_view[:, 2].astype(jnp.bfloat16)
    masked = jnp.where(
        allowed[None],
        jnp.einsum("qhd,khd->hqk", query_low, keys_low, preferred_element_type=jnp.float32)
        * score_scale,
        -1e30,
    )
    row_peak = jnp.max(masked, axis=-1, keepdims=True)
    logsum = row_peak + jnp.log(jnp.sum(jnp.exp(masked - row_peak), axis=-1, keepdims=True))
    probs_low = jnp.exp(masked - logsum).astype(jnp.bfloat16)
    mixed_low = (
        jnp.einsum("hqk,khd->qhd", probs_low, value_low, preferred_element_type=jnp.float32)
        .reshape(row_count, D)
        .astype(jnp.bfloat16)
    )
    attention = jnp.dot(
        mixed_low, output_full, preferred_element_type=jnp.float32
    ) + output_offset.astype(jnp.float32)
    normed_two, hidden_two = normalize(
        values, gain_two.astype(jnp.float32), shift_two.astype(jnp.float32)
    )
    input_two = hidden_two.astype(jnp.bfloat16)
    before = jnp.dot(input_two, up_full, preferred_element_type=jnp.float32) + up_offset.astype(
        jnp.float32
    )
    active_low = jax.nn.gelu(before, approximate=False).astype(jnp.bfloat16)
    feed_out = jnp.dot(
        active_low, down_full, preferred_element_type=jnp.float32
    ) + down_offset.astype(jnp.float32)
    result = (values + attention + feed_out).astype(jnp.bfloat16)
    back_one = (
        lax.all_gather(first_gain, "shard", axis=0, tiled=True),
        lax.all_gather(joint_weight, "shard", axis=0, tiled=True),
        lax.all_gather(output_weight, "shard", axis=0, tiled=True),
    )
    back_two = (
        lax.all_gather(second_gain, "shard", axis=0, tiled=True),
        lax.all_gather(up_weight, "shard", axis=0, tiled=True),
        lax.all_gather(down_weight, "shard", axis=0, tiled=True),
    )
    gain_back_one, joint_back, output_back = back_one
    gain_back_two, up_back, down_back = back_two
    grad_out = cotangent.astype(jnp.float32)
    down_weight_grad = contract_rows(active_low, cotangent)
    down_bias_grad = jnp.sum(grad_out, axis=0)
    grad_active = across(cotangent, down_back)
    gelu_exact = partial(jax.nn.gelu, approximate=False)
    grad_before = jax.vjp(gelu_exact, before)[1](grad_active)[0].astype(jnp.bfloat16)
    up_weight_grad = contract_rows(input_two, grad_before)
    up_bias_grad = jnp.sum(grad_before.astype(jnp.float32), axis=0)
    gain_two_grad, shift_two_grad, grad_from_two = norm_back(
        across(grad_before, up_back), normed_two, gain_back_two.astype(jnp.float32), values
    )
    output_weight_grad = contract_rows(mixed_low, cotangent)
    grad_mixed = across(cotangent, output_back).astype(jnp.bfloat16).reshape(row_count, HEADS, HEAD)
    masked_again = jnp.where(
        allowed[None],
        jnp.einsum("qhd,khd->hqk", query_low, keys_low, preferred_element_type=jnp.float32)
        * score_scale,
        -1e30,
    )
    prob_back = jnp.exp(masked_again - logsum)
    prob_back_low = prob_back.astype(jnp.bfloat16)
    grad_probs = jnp.einsum(
        "qhd,khd->hqk", grad_mixed, value_low, preferred_element_type=jnp.float32
    )
    grad_value = jnp.einsum(
        "hqk,qhd->khd", prob_back_low, grad_mixed, preferred_element_type=jnp.float32
    )
    spread = jnp.sum(grad_probs * prob_back, axis=-1, keepdims=True)
    grad_scores = (prob_back * (grad_probs - spread)).astype(jnp.bfloat16)
    grad_query = rotate(
        jnp.einsum("hqk,khd->qhd", grad_scores, keys_low, preferred_element_type=jnp.float32)
        * score_scale,
        position,
        -1.0,
    )
    grad_keys = rotate(
        jnp.einsum("hqk,qhd->khd", grad_scores, query_low, preferred_element_type=jnp.float32)
        * score_scale,
        position,
        -1.0,
    )
    grad_joint = (
        jnp.stack([grad_query, grad_keys, grad_value], axis=1)
        .reshape(row_count, 3 * D)
        .astype(jnp.bfloat16)
    )
    joint_weight_grad = contract_rows(input_one, grad_joint)
    joint_bias_grad = jnp.sum(grad_joint.astype(jnp.float32), axis=0)
    gain_one_grad, shift_one_grad, grad_from_one = norm_back(
        across(grad_joint, joint_back), normed_one, gain_back_one.astype(jnp.float32), values
    )
    grad_tokens = grad_out + grad_from_one + grad_from_two
    group_shares = (
        lax.psum_scatter(gain_one_grad, "shard", scatter_dimension=0, tiled=True),
        lax.psum_scatter(shift_one_grad, "shard", scatter_dimension=0, tiled=True),
        lax.psum_scatter(joint_weight_grad, "shard", scatter_dimension=0, tiled=True),
        lax.psum_scatter(joint_bias_grad, "shard", scatter_dimension=0, tiled=True),
        lax.psum_scatter(output_weight_grad, "shard", scatter_dimension=0, tiled=True),
        lax.psum_scatter(down_bias_grad, "shard", scatter_dimension=0, tiled=True),
        lax.psum_scatter(gain_two_grad, "shard", scatter_dimension=0, tiled=True),
        lax.psum_scatter(shift_two_grad, "shard", scatter_dimension=0, tiled=True),
        lax.psum_scatter(up_weight_grad, "shard", scatter_dimension=0, tiled=True),
        lax.psum_scatter(up_bias_grad, "shard", scatter_dimension=0, tiled=True),
        lax.psum_scatter(down_weight_grad, "shard", scatter_dimension=0, tiled=True),
        lax.psum_scatter(down_bias_grad, "shard", scatter_dimension=0, tiled=True),
    )
    (
        share_gain_one,
        share_shift_one,
        share_joint_weight,
        share_joint_bias,
        share_output_weight,
        share_output_bias,
        share_gain_two,
        share_shift_two,
        share_up_weight,
        share_up_bias,
        share_down_weight,
        share_down_bias,
    ) = group_shares
    owned = lax.psum(
        (
            share_gain_one,
            share_shift_one,
            share_joint_weight,
            share_joint_bias,
            share_output_weight,
            share_output_bias,
            share_gain_two,
            share_shift_two,
            share_up_weight,
            share_up_bias,
            share_down_weight,
            share_down_bias,
        ),
        "rep",
    )
    return (
        result,
        grad_tokens,
        owned[0],
        owned[1],
        owned[2],
        owned[3],
        owned[4],
        owned[5],
        owned[6],
        owned[7],
        owned[8],
        owned[9],
        owned[10],
        owned[11],
    )


PAIR = [(0, 1), (1, 0)]
BLOCKS = 8
LANE = 128
EXTRA = 16
GROUP = ("o", "p", "q", "c")
VMEM_BYTES = 48 * 1024 * 1024


def swap(values, *axes):
    if len(axes) == 1:
        return lax.ppermute(values, axes[0], PAIR)
    return lax.ppermute(values, axes, [(i, 3 - i) for i in range(4)])


def join(own, other, at, axis=0):
    first = at == 0
    return jnp.concatenate(
        [jnp.where(first, own, other), jnp.where(first, other, own)], axis=axis
    )


def pin(*values):
    return lax.optimization_barrier(values)


def take(values, at, axis=0):
    return lax.dynamic_index_in_dim(values, at, axis, keepdims=False)


def low(values):
    return values.astype(jnp.bfloat16)


def wide(values):
    return values.astype(jnp.float32)


def times(left, right):
    return jnp.dot(left, right, preferred_element_type=jnp.float32)


def places_of(ids_ref):
    return tuple(ids_ref[i] for i in range(5))


def call(kernel, outs, scratch, micros, *operands, memory):
    whole = pl.BlockSpec(memory_space=pltpu.VMEM)
    specs = {
        "s": pl.BlockSpec(memory_space=pltpu.SMEM),
        "v": whole,
        "h": pl.BlockSpec(memory_space=pl.ANY),
    }
    size = sum(leaf.size * leaf.dtype.itemsize for leaf in (*operands, *outs))
    return pl.pallas_call(
        kernel,
        out_shape=tuple(outs),
        in_specs=[specs[kind] for kind in memory],
        out_specs=tuple(whole for _ in outs),
        scratch_shapes=scratch,
        compiler_params=pltpu.CompilerParams(vmem_limit_bytes=VMEM_BYTES),
        cost_estimate=pl.CostEstimate(
            flops=int(micros * 1.15e9), bytes_accessed=size, transcendentals=0
        ),
    )(*operands)


def fetch(pairs, sems):
    copies = [
        pltpu.make_async_copy(source, target, sems.at[i])
        for i, (source, target) in enumerate(pairs)
    ]
    for copy in copies:
        copy.start()
    return copies


def finish(copies):
    for copy in copies:
        copy.wait()


def sheet_pairs(pieces, target, small, places):
    x, o, p, q, c = places
    pairs = []
    for index, piece in enumerate(pieces):
        jo, jq = index // 2, index % 2
        rows = piece.shape[1] if small is None else piece.shape[1] - EXTRA
        for k in range(4):
            jc, jp = k // 2, k % 2
            shard = (((o ^ jo) * 2 + (p ^ jp)) * 2 + (q ^ jq)) * 2 + (c ^ jc)
            if target is not None:
                at = pl.multiple_of(shard * rows, rows)
                pairs.append((piece.at[k, pl.ds(0, rows)], target.at[pl.ds(at, rows)]))
            if small is not None:
                at = pl.multiple_of(shard * EXTRA, EXTRA)
                pairs.append((piece.at[k, pl.ds(rows, EXTRA)], small.at[pl.ds(at, EXTRA)]))
    return pairs


def vector_of(small, start, size=HEAD, row=0):
    parts = [
        wide(small[shard * EXTRA : (shard + 1) * EXTRA, start + at : start + at + HEAD])[row : row + 1]
        for shard in range(16)
        for at in range(0, size, HEAD)
    ]
    pairs = [jnp.concatenate(parts[i : i + 2], axis=1) for i in range(0, len(parts), 2)]
    return jnp.concatenate(pairs, axis=1)


def tall_pairs(pieces, target, places):
    x, o, p, q, c = places
    pairs = []
    for index, piece in enumerate(pieces):
        jo, jq = index // 2, index % 2
        rows = piece.shape[0]
        at = ((o ^ jo) * 2 + (q ^ jq)) * rows
        pairs.append((piece, target.at[pl.ds(pl.multiple_of(at, rows), rows)]))
    return pairs


def norm_of(tokens):
    values = wide(tokens)
    centre = values - jnp.mean(values, axis=-1, keepdims=True)
    return centre * lax.rsqrt(jnp.mean(centre * centre, axis=-1, keepdims=True) + EPSILON)


def fold(values):
    rows, columns = values.shape
    return jnp.sum(values.reshape(rows // 8, 8, columns), axis=0)


def cut_kernel(ids, joint, up, small, keep, send):
    x, o, p, q, c = places_of(ids)
    parts = joint.shape[1] // D
    height = joint.shape[0]
    first = parts * LANE
    columns = small.shape[1] - first
    ours = jnp.concatenate([small[:, :first], small[:, : columns - first]], axis=1)
    upper = lax.broadcasted_iota(jnp.int32, (EXTRA, columns), 0) < EXTRA // 2
    vectors = low(jnp.where(upper, wide(small[:, first:]), wide(ours)))

    def block(ref, index):
        return ref[:, pl.ds(pl.multiple_of(index * LANE, LANE), LANE)]

    for jp, target in ((0, keep), (1, send)):
        for jc in (0, 1):
            pp, cc = p ^ jp, c ^ jc
            target[jc, height:, :first] = jnp.broadcast_to(small[:, :first], (EXTRA, first))
            target[jc, height:, first:] = vectors
            for part in range(parts):
                target[jc, :height, part * LANE : (part + 1) * LANE] = block(
                    joint, part * 8 + x * 4 + pp * 2 + cc
                )
            for k in range(4):
                oo, qq = k // 2, k % 2
                at = (parts + k) * LANE
                target[jc, :height, at : at + LANE] = block(
                    up, (((oo * 2 + pp) * 2 + qq) * 2 + cc) * 2 + x
                )


def turner(cap):
    lane = lax.broadcasted_iota(jnp.int32, (cap, LANE), 1)
    lead = lane % HEAD < ROT // 2

    def turn(values, cos_part, sin_part):
        other = jnp.where(
            lead, pltpu.roll(values, LANE - ROT // 2, 1), pltpu.roll(values, ROT // 2, 1)
        )
        return values * cos_part + other * sin_part

    return turn, (lane < HEAD, lane >= HEAD)


def block_pairs(sources, tokens, cotangent):
    cap = sources[0].shape[1]
    return [
        (source.at[2 * k + which], target.at[pl.ds((2 * i + k) * cap, cap)])
        for i, source in enumerate(sources)
        for k in (0, 1)
        for which, target in enumerate((tokens, cotangent))
        if target is not None
    ]


def both_ways(step, near_out, far_out, size):
    for i in (0, 1):
        near_out[i * size : (i + 1) * size, :] = step(2 * i)
    for i in (0, 1):
        far_out[i * size : (i + 1) * size, :] = low(step(2 * i + 1))


def attention_kernel(
    ids,
    block_0,
    block_1,
    block_2,
    block_3,
    sheet_0,
    sheet_1,
    sheet_2,
    sheet_3,
    extra_0,
    extra_1,
    extra_2,
    extra_3,
    output_weight,
    fed,
    cosine,
    sine,
    position,
    near_out,
    far_out,
    grad_ref,
    home_0,
    home_1,
    away,
    output_grad,
    grad_sum,
    tokens,
    cotangent,
    joint,
    inputs,
    mixed_all,
    total,
    small,
    gain,
    shift,
    offset,
    sems,
):
    x, o, p, q, c = places_of(ids)
    cap = block_0.shape[1]
    finish(
        fetch(
            sheet_pairs((sheet_0, sheet_1, sheet_2, sheet_3), joint, None, places_of(ids))
            + sheet_pairs((extra_0, extra_1, extra_2, extra_3), None, small, places_of(ids))
            + block_pairs((block_0, block_1, block_2, block_3), tokens, cotangent),
            sems,
        )
    )
    row = EXTRA // 2
    gain[...] = vector_of(small, 0, row=row)
    shift[...] = vector_of(small, HEAD, row=row)
    offset[...] = vector_of(small, 2 * HEAD, 3 * HEAD, row)
    starts = [pl.multiple_of((part * 8 + x * 4 + p * 2 + c) * LANE, LANE) for part in range(3)]
    bias = jnp.concatenate([offset[:, pl.ds(at, LANE)] for at in starts], axis=1)
    total[...] = jnp.zeros_like(total)
    turn, mine = turner(2 * cap)
    own = mine[0][:cap]
    down = lax.broadcasted_iota(jnp.int32, (cap, cap), 0)
    along = lax.broadcasted_iota(jnp.int32, (cap, cap), 1)
    scale = HEAD ** (-0.5)

    def by_head(values):
        none = jnp.zeros_like(values)
        return jnp.concatenate([jnp.where(own, values, none), jnp.where(own, none, values)])

    def attend(query, keys, value, grad_mixed, place):
        allowed = ((along <= down) & (along >= down - place))[None]
        query_two, grad_two = by_head(query), by_head(grad_mixed)
        scores = across(query_two, keys).reshape(2, cap, cap) * scale
        scores = jnp.where(allowed, scores, -1e30)
        raised = jnp.exp(scores - jnp.max(scores, axis=-1, keepdims=True))
        probs = raised / jnp.sum(raised, axis=-1, keepdims=True)
        probs_low = low(probs).reshape(2 * cap, cap)
        grad_probs = across(grad_two, value).reshape(2, cap, cap)
        spread = jnp.sum(grad_probs * probs, axis=-1, keepdims=True)
        grad_scores = low(probs * (grad_probs - spread)).reshape(2 * cap, cap)
        mixed = times(probs_low, value)
        grad_query = times(grad_scores, keys)
        return (
            jnp.where(own, mixed[:cap], mixed[cap:]),
            jnp.where(own, grad_query[:cap], grad_query[cap:]) * scale,
            contract_rows(grad_scores, query_two) * scale,
            contract_rows(probs_low, grad_two),
        )

    def step(pair):
        rows = slice(pair * 2 * cap, (pair + 1) * 2 * cap)
        input_low = low(norm_of(tokens[rows, :]) * gain[...] + shift[...])
        inputs[rows, :] = input_low
        projected = times(input_low, joint[...]) + bias
        cos_part, sin_part = cosine[rows, :], sine[rows, :]
        query = low(turn(projected[:, :LANE], cos_part, sin_part))
        keys = low(turn(projected[:, LANE : 2 * LANE], cos_part, sin_part))
        value = low(projected[:, 2 * LANE :])
        grad_mixed = low(across(cotangent[rows, :], output_weight[...]))
        place = position[rows, :]
        found = [
            attend(query[at], keys[at], value[at], grad_mixed[at], place[at, :1])
            for at in (slice(0, cap), slice(cap, 2 * cap))
        ]
        mixed, grad_query, grad_keys, grad_value = (jnp.concatenate(both) for both in zip(*found))
        mixed = low(mixed)
        mixed_all[rows, :] = mixed
        grad_joint = low(
            jnp.concatenate(
                [
                    turn(grad_query, cos_part, -sin_part),
                    turn(grad_keys, cos_part, -sin_part),
                    grad_value,
                ],
                axis=1,
            )
        )
        grad_ref[rows, :] = grad_joint
        total[...] += fold(wide(grad_joint))
        return times(mixed, output_weight[...]) + wide(fed[rows, :])

    both_ways(step, near_out, far_out, 2 * cap)
    grad_sum[...] = jnp.sum(total[...], axis=0, keepdims=True)
    output_grad[...] = low(contract_rows(mixed_all[...], cotangent[...]))
    half = away.shape[0] // 2
    here = home_0, away.at[pl.ds(0, half)]
    there = home_1, away.at[pl.ds(half, half)]
    sheet_grads(inputs, grad_ref, here, there, 0, places_of(ids))


def for_place(at, here, there, store):
    pl.when(at)(lambda: store(*here))
    pl.when(jnp.logical_not(at))(lambda: store(*there))


def sheet_grads(inputs, grads, here, there, base, places):
    x, o, p, q, c = places
    columns = grads.shape[1]
    rows = D // 16
    for oo in (0, 1):
        found = contract_rows(inputs[:, oo * D // 2 : (oo + 1) * D // 2], grads[...])
        found = low(found).reshape(2, 2, 2, rows, columns)

        def store(home, away, found=found):
            for pp in (0, 1):
                for cc in (0, 1):
                    down = pl.ds(pl.multiple_of(base + (p ^ pp) * rows, rows), rows)
                    along = pl.ds(pl.multiple_of((c ^ cc) * columns, LANE), columns)
                    home[down, along] = jnp.where(q == 0, found[pp, 0, cc], found[pp, 1, cc])
                    away[down, along] = jnp.where(q == 0, found[pp, 1, cc], found[pp, 0, cc])

        for_place(o == oo, here, there, store)


def feed_kernel(
    ids,
    block_0,
    block_1,
    block_2,
    block_3,
    sheet_0,
    sheet_1,
    sheet_2,
    sheet_3,
    tall_0,
    tall_1,
    tall_2,
    tall_3,
    fed,
    late_offset,
    grad_all,
    home_0,
    home_1,
    away_0,
    away_1,
    grad_sum,
    tokens,
    cotangent,
    up,
    down,
    inputs,
    active_all,
    total,
    small,
    gain,
    shift,
    sems,
):
    places = places_of(ids)
    x, o, p, q, c = places
    cap = block_0.shape[1]
    finish(
        fetch(
            sheet_pairs((sheet_0, sheet_1, sheet_2, sheet_3), up, small, places)
            + block_pairs((block_0, block_1, block_2, block_3), tokens, cotangent)
            + tall_pairs((tall_0, tall_1, tall_2, tall_3), down, places),
            sems,
        )
    )
    gain[...] = vector_of(small, 0)
    shift[...] = vector_of(small, HEAD)
    width = 4 * LANE
    late_offset[...] = vector_of(small, width - 2 * HEAD) + vector_of(small, width - HEAD)
    along = pl.ds(pl.multiple_of((x + 1) * LANE, LANE), LANE)
    bias = [
        small[pl.ds(pl.multiple_of((((oo * 2 + p) * 2 + qq) * 2 + c) * EXTRA, EXTRA), EXTRA), along]
        for oo in (0, 1)
        for qq in (0, 1)
    ]
    bias = wide(jnp.concatenate(bias, axis=1))[:1]
    total[...] = jnp.zeros_like(total)

    for pair in range(BLOCKS // 2):
        rows = slice(pair * 2 * cap, (pair + 1) * 2 * cap)
        input_low = low(norm_of(tokens[rows, :]) * gain[...] + shift[...])
        inputs[rows, :] = input_low
        before = times(input_low, up[...]) + bias
        slope = 0.5 + 0.5 * lax.erf(before * 0.5**0.5)
        active = low(before * slope)
        active_all[rows, :] = active
        slope = slope + before * jnp.exp(-0.5 * before * before) * (0.5 / jnp.pi) ** 0.5
        grad_before = low(across(cotangent[rows, :], down[...]) * slope)
        grad_all[rows, :] = grad_before
        total[...] += fold(wide(grad_before))
        fed[rows, :] = low(times(active, down[...]))

    grad_sum[...] = jnp.sum(total[...], axis=0, keepdims=True)
    unit = home_0.shape[0] // 2
    here, there = (home_0, away_0), (home_1, away_1)
    for oo in (0, 1):
        found = low(contract_rows(active_all[:, oo * 2 * unit : (oo + 1) * 2 * unit], cotangent[...]))

        def store(home, away, found=found):
            home[:unit, :] = jnp.where(q == 0, found[:unit], found[unit:])
            away[:unit, :] = jnp.where(q == 0, found[unit:], found[:unit])

        for_place(o == oo, here, there, store)
    sheet_grads(inputs, grad_all, here, there, unit, places)


def pull_kernel(
    ids,
    block_0,
    block_1,
    block_2,
    block_3,
    join_0,
    join_1,
    join_2,
    join_3,
    sheet_0,
    sheet_1,
    sheet_2,
    sheet_3,
    grad_joint,
    grad_before,
    joint_sum,
    up_sum,
    near_out,
    far_out,
    sums,
    tokens,
    joint,
    up,
    totals,
    small,
    gain_one,
    gain_two,
    own,
    sems,
):
    places = places_of(ids)
    x, o, p, q, c = places
    cap = block_0.shape[1]
    finish(
        fetch(
            block_pairs((block_0, block_1, block_2, block_3), tokens, None)
            + sheet_pairs((join_0, join_1, join_2, join_3), joint, None, places)
            + sheet_pairs((sheet_0, sheet_1, sheet_2, sheet_3), up, small, places)
            + [(block_0.at[1], own)],
            sems,
        )
    )
    gain_one[...] = vector_of(small, 0, row=EXTRA // 2)
    gain_two[...] = vector_of(small, 0)
    totals[...] = jnp.zeros_like(totals)

    def step(pair):
        rows = slice(pair * 2 * cap, (pair + 1) * 2 * cap)
        normed = norm_of(tokens[rows, :])
        grad_first = across(grad_joint[rows, :], joint[...])
        grad_second = across(grad_before[rows, :], up[...])
        totals[0] += fold(grad_first * normed)
        totals[1] += fold(grad_first)
        totals[2] += fold(grad_second * normed)
        totals[3] += fold(grad_second)
        return grad_first * gain_one[...] + grad_second * gain_two[...]

    both_ways(step, near_out, far_out, 2 * cap)
    sums[...] = jnp.zeros_like(sums)
    sums[0:4, :] = jnp.sum(totals[...], axis=1)
    sums[4:5, :] = jnp.sum(wide(own[...]), axis=0, keepdims=True)
    at = pl.ds(pl.multiple_of((x * 4 + p * 2 + c) * LANE, LANE), LANE)
    for part in range(3):
        sums[5 + part : 6 + part, at] = joint_sum[:, part * LANE : (part + 1) * LANE]
    for k in range(4):
        at = pl.ds(pl.multiple_of((k % 2 * 4 + c * 2 + x) * LANE, LANE), LANE)
        for pp in (0, 1):
            row = 8 + k // 2 * 2 + pp
            found = up_sum[:, k * LANE : (k + 1) * LANE]
            sums[row : row + 1, at] = jnp.where(p == pp, found, jnp.zeros_like(found))


def final_kernel(
    up_home,
    up_away,
    up_sent,
    joint_home,
    joint_away,
    joint_sent,
    out_0,
    out_1,
    out_2,
    out_3,
    down,
):
    rows = down.shape[0]
    found = low(total(up_home[...], up_away[...], up_sent[...]))
    down[...] = found[:rows]
    found = found[rows:]
    joint = low(total(joint_home[...], joint_away[:rows, :], joint_sent[...]))
    half, width = rows // 2, joint.shape[1] // 2
    hidden = found.shape[1] // 2
    for k, out in enumerate((out_0, out_1, out_2, out_3)):
        jp, jc = k // 2, k % 2
        out[:, :width] = joint[jp * half : (jp + 1) * half, jc * width : (jc + 1) * width]
        out[:, width:] = found[jp * half : (jp + 1) * half, jc * hidden : (jc + 1) * hidden]


def lay_kernel(ids, own, other, joint, up):
    x, o, p, q, c = places_of(ids)
    parts = joint.shape[1] // D
    for xx, source in ((0, own), (1, other)):
        for pp in (0, 1):
            for cc in (0, 1):
                values = wide(source[pp, cc])
                at_x, at_p, at_c = x ^ xx, p ^ pp, c ^ cc
                blocks = [(joint, part * 8 + at_x * 4 + at_p * 2 + at_c) for part in range(parts)]
                blocks += [
                    (up, (((k // 2 * 2 + at_p) * 2 + k % 2) * 2 + at_c) * 2 + at_x) for k in range(4)
                ]
                for k, (out, at) in enumerate(blocks):
                    out[:, pl.ds(pl.multiple_of(at * LANE, LANE), LANE)] = values[
                        :, k * LANE : (k + 1) * LANE
                    ]


def lane_sum(near, came):
    lane = near + wide(came)
    rows = lane.shape[0] // 4
    return lane[:rows], *(low(lane[i * rows : (i + 1) * rows]) for i in (1, 2, 3))


def total(*parts):
    found = wide(parts[0])
    for part in parts[1:]:
        found += wide(part)
    return found


def grouped(
    tokens,
    cotangent,
    lengths,
    owners,
    first_gain,
    first_bias,
    joint_weight,
    joint_bias,
    output_weight,
    output_bias,
    second_gain,
    second_bias,
    up_weight,
    up_bias,
    down_weight,
    down_bias,
):
    x, o, p, q, c = (lax.axis_index(name) for name in ("x", "o", "p", "q", "c"))
    ids = jnp.stack([x, o, p, q, c]).astype(jnp.int32)
    cap = tokens.shape[0]
    rows = BLOCKS * cap
    part = joint_weight.shape[0]
    hidden = up_weight.shape[1] // 8
    unit = hidden // 4
    bf, f32 = jnp.bfloat16, jnp.float32

    def like(shape, kind):
        return jax.ShapeDtypeStruct(shape, kind)

    pair = jnp.stack([tokens, cotangent])
    along_x = swap(pair, "x")

    rest = jnp.zeros((HEAD,), bf)
    small = jnp.concatenate(
        [first_gain, first_bias, joint_bias, rest, second_gain, second_bias, up_bias, output_bias, down_bias]
    )[None]
    down_half = take(down_weight.reshape(2, unit, D), x)
    keep, send = call(
        cut_kernel,
        [
            like((2, part + EXTRA, 3 * LANE + hidden), bf),
            like((2, part + EXTRA, 3 * LANE + hidden), bf),
        ],
        [],
        0,
        ids,
        joint_weight,
        up_weight,
        small,
        memory="svvv",
    )
    came, down_other, down_side = swap(send, "p"), swap(down_half, "o"), swap(down_half, "q")
    along_p = swap(pin(tokens, send)[0], "p")

    came, down_other, down_side, along_x, along_p, lengths = pin(
        came, down_other, down_side, along_x, along_p, lengths
    )

    turn_came, output_came = swap(jnp.concatenate([keep[1:], came[1:]]), "c"), swap(output_weight, "c")
    turn_came, output_came, along_p = pin(turn_came, output_came, along_p)

    turned = jnp.concatenate([keep[:1], came[:1], turn_came])
    first, up_own, joint_own, along_p = pin(
        jnp.concatenate([pair, along_x]),
        turned[:, :, 3 * LANE :],
        turned[:, :part, : 3 * LANE],
        along_p,
    )
    up_other, up_side = swap(up_own, "o"), swap(up_own, "q")
    grad_along_p, along_both = swap(pin(cotangent, along_p)[0], "p"), swap(along_p, "x")
    down_corner = swap(down_other, "q")

    devices = jnp.stack(
        [
            ((((x ^ xx) * 2 + o) * 2 + (p ^ pp)) * 2 + q) * 2 + (c ^ cc)
            for pp in (0, 1)
            for cc in (0, 1)
            for xx in (0, 1)
        ]
    )
    position = jax.vmap(lambda device: layout(lengths, owners, device, cap)[1])(devices)
    position = position.reshape(rows, 1)
    place = jnp.arange(LANE) % HEAD
    half_rot = ROT // 2
    frequency = 10000.0 ** (-jnp.arange(half_rot, dtype=f32) / half_rot)
    angles = position.astype(f32) * jnp.tile(frequency, LANE // half_rot)[None, :]
    position = jnp.broadcast_to(position, (rows, LANE))
    cosine = jnp.where(place < ROT, jnp.cos(angles), 1.0)
    sine = jnp.sin(angles)
    sine = jnp.where(place < half_rot, -sine, jnp.where(place < ROT, sine, 0.0))

    cosine, sine, position, up_other, up_side, grad_along_p, along_both, down_corner, joint_own, first = pin(
        cosine, sine, position, up_other, up_side, grad_along_p, along_both, down_corner, joint_own, first
    )

    up_corner, joint_other = swap(up_other, "q"), swap(joint_own, "o")
    grad_along_both, first_came = swap(grad_along_p, "x"), swap(first, "c")
    turn_over = [
        (((a * 2 + b) * 2 + e) * 2 + f, ((b * 2 + a) * 2 + f) * 2 + e)
        for a in (0, 1)
        for b in (0, 1)
        for e in (0, 1)
        for f in (0, 1)
    ]
    cross = ("x", "o", "q", "c")
    up_corner, first_came, joint_other, grad_along_both, output_pair = pin(
        up_corner, first_came, joint_other, grad_along_both, join(output_weight, output_came, c)
    )
    second = jnp.stack([along_p, grad_along_p, along_both, grad_along_both])
    second_came = swap(second, "c")
    joint_pair, output_pair, second_came = pin(
        jnp.stack([joint_own, joint_other]), output_pair, second_came
    )
    blocks = first, first_came, second, second_came
    up_sheets = up_own, up_side, up_other, up_corner
    down_talls = down_half, down_side, down_other, down_corner
    joint_far = swap(joint_pair, "q")
    output_pair = lax.ppermute(output_pair, cross, turn_over)
    copies = pltpu.SemaphoreType.DMA
    tall = (rows, D)
    found = call(
        feed_kernel,
        [
            like(tall, bf),
            like((1, D), f32),
            like((rows, hidden), bf),
            *(like((2 * unit, D), bf) for _ in range(4)),
            like((1, hidden), f32),
        ],
        [
            pltpu.VMEM(tall, bf),
            pltpu.VMEM(tall, bf),
            pltpu.VMEM((D, hidden), bf),
            pltpu.VMEM((hidden, D), bf),
            pltpu.VMEM(tall, bf),
            pltpu.VMEM((rows, hidden), bf),
            pltpu.VMEM((8, hidden), f32),
            pltpu.VMEM((16 * EXTRA, hidden), bf),
            pltpu.VMEM((1, D), f32),
            pltpu.VMEM((1, D), f32),
            copies((52,)),
        ],
        20,
        ids,
        *blocks,
        *up_sheets,
        *down_talls,
        memory="shhhhhhhhhhhh",
    )
    joint_far, output_pair, *found = pin(joint_far, output_pair, *found)
    joint_sheets = joint_own, joint_far[0], joint_other, joint_far[1]
    fed, late_offset, grad_before, up_home_0, up_home_1, up_away_0, up_away_1, up_sum = found
    up_away_1 = swap(up_away_1, "q")

    found = call(
        attention_kernel,
        [
            like((rows // 2, D), f32),
            like((rows // 2, D), bf),
            like((rows, 3 * LANE), bf),
            like((2 * part, 6 * LANE), bf),
            like((2 * part, 6 * LANE), bf),
            like((4 * part, 6 * LANE), bf),
            like((LANE, D), bf),
            like((1, 3 * LANE), f32),
        ],
        [
            pltpu.VMEM(tall, bf),
            pltpu.VMEM(tall, bf),
            pltpu.VMEM((D, 3 * LANE), bf),
            pltpu.VMEM(tall, bf),
            pltpu.VMEM((rows, LANE), bf),
            pltpu.VMEM((8, 3 * LANE), f32),
            pltpu.VMEM((16 * EXTRA, hidden), bf),
            pltpu.VMEM((1, D), f32),
            pltpu.VMEM((1, D), f32),
            pltpu.VMEM((1, 3 * D), f32),
            copies((48,)),
        ],
        22,
        ids,
        *blocks,
        *joint_sheets,
        *up_sheets,
        output_pair,
        fed,
        cosine,
        sine,
        position,
        memory="shhhhhhhhhhhhvvvvv",
    )
    up_away_1, up_away_0, *found = pin(up_away_1, up_away_0, *found)
    near_part, far_part, grad_joint, joint_home_0, joint_home_1, joint_away, output_grad, joint_sum = found

    def lane_sum(near, came, block):
        at = slice(block * cap, (block + 1) * cap)
        return near[at] + wide(came[at])

    up_sent = swap(low(total(up_home_1, up_away_1)), "o")
    joint_away, up_away_0 = swap(joint_away, "q"), swap(up_away_0, "q")
    result_lane = near_part, swap(far_part, "c")
    result_sent, grad_joint = pin(
        low(jnp.concatenate([lane_sum(*result_lane, 1), lane_sum(*result_lane, 3)])), grad_joint
    )
    result_came = swap(result_sent, "x")
    output_part = lax.ppermute(output_grad, cross, turn_over)
    found = call(
        pull_kernel,
        [like((rows // 2, D), f32), like((rows // 2, D), bf), like((16, D), f32)],
        [
            pltpu.VMEM(tall, bf),
            pltpu.VMEM((D, 3 * LANE), bf),
            pltpu.VMEM((D, hidden), bf),
            pltpu.VMEM((4, 8, D), f32),
            pltpu.VMEM((16 * EXTRA, hidden), bf),
            pltpu.VMEM((1, D), f32),
            pltpu.VMEM((1, D), f32),
            pltpu.VMEM((cap, D), bf),
            copies((73,)),
        ],
        11,
        ids,
        *blocks,
        *joint_sheets,
        *up_sheets,
        grad_joint,
        grad_before,
        joint_sum,
        up_sum,
        memory="shhhhhhhhhhhhvvvv",
    )
    up_sent, up_away_0, joint_away, result_came, output_part, *found = pin(
        up_sent, up_away_0, joint_away, result_came, output_part, *found
    )
    near_part, far_part, sums = found
    came, sums_came = swap(far_part, "c"), swap(sums, "c")
    output_part = output_part.reshape(2, part, D)

    joint_sent, came, sums_came = pin(
        low(total(joint_home_1, joint_away[2 * part :])),
        came,
        sums_came,
    )

    lane = near_part, came
    sums, *sent = pin(sums + sums_came, *(low(lane_sum(*lane, i)) for i in (1, 2, 3)))
    side, far_side, corner = swap(sent[0], "x"), swap(sent[1], "p"), swap(sent[2], "x", "p")
    joint_sent = swap(joint_sent, "o")
    sums = sums + swap(sums, "x")
    sums = sums + swap(sums, "q")
    side, far_side, corner, joint_sent, output_part, result_came, sums = pin(
        side, far_side, corner, joint_sent, output_part, result_came, sums
    )
    output_sent = take(output_part, 1 - c)
    result_kept = lane_sum(*result_lane, 0) + wide(result_came[:cap])
    result_sent = low(lane_sum(*result_lane, 2) + wide(result_came[cap:]))

    *final, down_final = call(
        final_kernel,
        [*(like((part, 3 * LANE + hidden), bf) for _ in range(4)), like((unit, D), bf)],
        [],
        1,
        up_home_0,
        up_away_0,
        up_sent,
        joint_home_0,
        joint_away,
        joint_sent,
        memory="vvvvvv",
    )
    *final, down_final, sums = pin(*final, down_final, sums)
    sent = swap(final[1], "c"), swap(final[2], "p"), swap(final[3], "p", "c")
    down_came, sums_came, output_sent = swap(down_final, "x"), swap(sums, "p"), swap(output_sent, "c")
    pulled = lane_sum(*lane, 0) + wide(side[:cap]) + wide(far_side[:cap]) + wide(corner[:cap])
    *sent, down_came, sums_came, output_sent = pin(*sent, down_came, sums_came, output_sent)

    both, sums, output_own, result_sent = pin(
        jnp.stack([final[0], *sent]).reshape(2, 2, part, -1),
        sums + sums_came,
        low(total(take(output_part, c), output_sent)),
        result_sent,
    )
    both_came, output_came = swap(both, "x"), swap(output_own, "x")
    result_came = swap(result_sent, "p")
    sums = sums + swap(sums, "o")
    shard = ((o * 2 + p) * 2 + q) * 2 + c

    def own_part(values):
        size = values.size // 16
        return lax.dynamic_slice_in_dim(values.reshape(-1), shard * size, size)

    output_own = total(output_own, output_came)
    down_own = wide(join(down_final, down_came, x))
    joint_own_grad, up_own_grad = call(
        lay_kernel,
        [like((part, 3 * D), f32), like((part, up_weight.shape[1]), f32)],
        [],
        1,
        ids,
        both,
        both_came,
        memory="svv",
    )

    own_values = wide(tokens)
    own_normed = norm_of(tokens)
    centre = own_values - jnp.mean(own_values, axis=-1, keepdims=True)
    factor = lax.rsqrt(jnp.mean(centre * centre, axis=-1, keepdims=True) + EPSILON)
    grad_tokens = wide(cotangent) + factor * (
        pulled
        - jnp.mean(pulled, axis=-1, keepdims=True)
        - own_normed * jnp.mean(pulled * own_normed, axis=-1, keepdims=True)
    )
    grad_tokens, result_came = pin(grad_tokens, result_came)
    result = low(own_values + total(result_kept, result_came) + late_offset)
    norm_grads = [own_part(sums[i]) for i in range(5)]
    return (
        result,
        grad_tokens,
        norm_grads[0],
        norm_grads[1],
        joint_own_grad,
        own_part(sums[5:8]),
        output_own,
        norm_grads[4],
        norm_grads[2],
        norm_grads[3],
        up_own_grad,
        own_part(sums[8:12]),
        down_own,
        norm_grads[4],
    )


def solution(mesh):
    if mesh.shape["rep"] == 2 and mesh.shape["shard"] * HEAD == D:
        work, body = Mesh(mesh.devices.reshape(2, 2, 2, 2, 2), ("x", *GROUP)), grouped
        group, every = GROUP, ("x", *GROUP)
    else:
        work, body = mesh, local
        group, every = "shard", ("rep", "shard")
    row, vec, mat = P(every, None), P(group), P(group, None)
    return jax.shard_map(
        body,
        mesh=work,
        in_specs=(row, row, P(), P(), vec, vec, mat, vec, mat, vec, vec, vec, mat, vec, mat, vec),
        out_specs=(row, row, vec, vec, mat, vec, mat, vec, vec, vec, mat, vec, mat, vec),
        check_vma=False,
    )
```
